128 devices in a mesh: dp: 16 (over x_lo, z, core), tensor: 8 (over y, x_hi).
Axes of the slice: x: 4 (x_hi: 2, x_lo: 2; x = x_hi * 2 + x_lo), y: 4, z: 4, core: 2. Of those that a mesh axis runs over, the one named last changes fastest.
Arguments:
- tokens: bfloat16 [16384, 2048], P(('dp', 'tensor')), may hold values from -6 to 6
- cotangent: bfloat16 [16384, 2048], P(('dp', 'tensor')), may hold values from -6 to 6
- attn_gain: float32 [2048], replicated, may hold values from 0.1 to 1.9
- mlp_gain: float32 [2048], replicated, may hold values from 0.1 to 1.9
- query_gain: float32 [128], replicated, may hold values from 0.1 to 1.9
- key_gain: float32 [128], replicated, may hold values from 0.1 to 1.9
- w_query: bfloat16 [2048, 2048], P('dp', 'tensor'), may hold values from -0.125 to 0.125
- key_weight: bfloat16 [2048, 1024], P('dp', 'tensor'), may hold values from -0.125 to 0.125
- value_weight: bfloat16 [2048, 1024], P('dp', 'tensor'), may hold values from -0.125 to 0.125
- w_out: bfloat16 [2048, 2048], P('dp', 'tensor'), may hold values from -1.5 to 1.5
- w_gate: bfloat16 [2048, 6144], P('dp', 'tensor'), may hold values from -0.125 to 0.125
- w_up: bfloat16 [2048, 6144], P('dp', 'tensor'), may hold values from -0.125 to 0.125
- w_down: bfloat16 [2048, 6144], P('dp', 'tensor'), may hold values from -0.078125 to 0.078125
Outputs:
- result: bfloat16 [16384, 2048], P(('dp', 'tensor'))
- tokens_grad: float32 [16384, 2048], P(('dp', 'tensor'))
- attn_gain_grad: float32 [2048], replicated
- mlp_gain_grad: float32 [2048], replicated
- query_gain_grad: float32 [128], replicated
- key_gain_grad: float32 [128], replicated
- w_query_grad: float32 [2048, 2048], P('dp', 'tensor')
- key_weight_gradient: float32 [2048, 1024], P('dp', 'tensor')
- w_value_grad: float32 [2048, 1024], P('dp', 'tensor')
- w_out_grad: float32 [2048, 2048], P('dp', 'tensor')
- w_gate_grad: float32 [2048, 6144], P('dp', 'tensor')
- w_up_grad: float32 [2048, 6144], P('dp', 'tensor')
- w_down_grad: float32 [2048, 6144], P('dp', 'tensor')
The draws below stay inside these ranges and needn't reach their ends.
All inputs are finite; a program needn't handle non-finite values.
Results may differ from the reference program's by a relative error of at most 0.023.
Values may be sent and summed in bfloat16 or wider, within the bound.
A program may use at most 128 MiB of HBM per device.

```python
import jax
import jax.numpy as jnp
from jax import lax

MODEL_WIDTH = 2048
HQ = 16
KEY_VALUE_HEADS = 8
HEAD_WIDTH = 128
FF = 6144
SEQ_LEN = 1024
QBLOCK = 512
TOKENS = 16384
N_DP = 16


def block_levels(key, dims, cuts, smallest, top_value):
    def one(position, shards_of):
        heights = jax.random.uniform(jax.random.fold_in(jax.random.fold_in(key, 6), position), (shards_of,), jnp.float32, smallest / len(cuts), top_value / len(cuts))
        return jnp.repeat(jnp.exp(heights), dims[position] // shards_of).reshape((-1,) + (1,) * (len(dims) - position - 1))

    loudness = one(*cuts[0])
    for cut in cuts[1:]:
        loudness = loudness * one(*cut)
    return loudness


def gaussian(key, dims, width, reach, cuts=(), kind=jnp.bfloat16):
    level = block_levels(key, dims, cuts, -0.22, 0.18) if cuts else 1.0
    values = jax.random.normal(key, dims, jnp.float32) * width * level
    return jnp.minimum(jnp.maximum(values, -reach), reach).astype(kind)


def setup_inputs(seed: int = 0) -> dict:
    splits = jax.random.split(jax.random.key(seed), 14)
    tokens = gaussian(splits[0], (TOKENS, MODEL_WIDTH), 1.0, 6.0, ((0, 128),))
    cotangent = gaussian(splits[1], (TOKENS, MODEL_WIDTH), 1.0, 6.0, ((0, 128),))
    attn_gain = jnp.clip(1.0 + 0.18 * jax.random.normal(splits[2], (MODEL_WIDTH,), jnp.float32), 0.1, 1.9)
    mlp_gain = jnp.clip(1.0 + 0.18 * jax.random.normal(splits[3], (MODEL_WIDTH,), jnp.float32), 0.1, 1.9)
    query_gain = jnp.clip(1.0 + 0.18 * jax.random.normal(splits[4], (HEAD_WIDTH,), jnp.float32), 0.1, 1.9)
    key_gain = jnp.clip(1.0 + 0.18 * jax.random.normal(splits[5], (HEAD_WIDTH,), jnp.float32), 0.1, 1.9)
    w_query = gaussian(splits[6], (MODEL_WIDTH, HQ * HEAD_WIDTH), MODEL_WIDTH ** -0.5, 0.125, ((0, 16), (1, 8)))
    key_weight = gaussian(splits[7], (MODEL_WIDTH, KEY_VALUE_HEADS * HEAD_WIDTH), MODEL_WIDTH ** -0.5, 0.125, ((0, 16), (1, 8)))
    value_weight = gaussian(splits[8], (MODEL_WIDTH, KEY_VALUE_HEADS * HEAD_WIDTH), MODEL_WIDTH ** -0.5, 0.125, ((0, 16), (1, 8)))
    w_out = gaussian(splits[9], (MODEL_WIDTH, HQ * HEAD_WIDTH), (max(HQ * HEAD_WIDTH // 128, 8)) ** -0.5, 1.5, ((0, 16), (1, 8)))
    w_gate = gaussian(splits[10], (MODEL_WIDTH, FF), MODEL_WIDTH ** -0.5, 0.125, ((0, 16), (1, 8)))
    w_up = gaussian(splits[11], (MODEL_WIDTH, FF), MODEL_WIDTH ** -0.5, 0.125, ((0, 16), (1, 8)))
    w_down = gaussian(splits[12], (MODEL_WIDTH, FF), FF ** -0.5, 0.078125, ((0, 16), (1, 8)))
    return dict(tokens=tokens, cotangent=cotangent, attn_gain=attn_gain, mlp_gain=mlp_gain, query_gain=query_gain, key_gain=key_gain, w_query=w_query, key_weight=key_weight, value_weight=value_weight, w_out=w_out, w_gate=w_gate, w_up=w_up, w_down=w_down)


EPS = 1e-06
ROPE_BASE = 1000000.0
MASKED = -1e+30
PRECISE = lax.Precision.HIGHEST

@jax.custom_vjp
def low(v):
    return lax.optimization_barrier(v.astype(jnp.bfloat16)).astype(jnp.float32)

@jax.custom_vjp
def low_back(v):
    return v

def low_keep(v):
    return (low(v), None)

def low_pass(kept, grad):
    return (grad,)

def backward_mask(v):
    return (v, None)

def back_low(kept, grad):
    return (low(grad),)
low.defvjp(low_keep, low_pass)
low_back.defvjp(backward_mask, back_low)

def norm_rows(values, gain):
    inverse = lax.rsqrt(lax.optimization_barrier(jnp.mean(values * values, axis=-1, keepdims=True)) + EPS)
    return values * inverse * gain

def rope_tables(length, head_size):
    half_size = head_size // 2
    positions = jnp.arange(length, dtype=jnp.float32)[:, None]
    frequency = ROPE_BASE ** (-2.0 * jnp.arange(half_size, dtype=jnp.float32) / head_size)
    rotary_angles = positions * frequency[None, :]
    return (jnp.cos(rotary_angles), jnp.sin(rotary_angles))

def rotate(values, cosine, sine):
    half_size = values.shape[-1] // 2
    first_half = values[..., :half_size]
    second_half = values[..., half_size:]
    cos_wide = cosine[:, None, :]
    sin_wide = sine[:, None, :]
    return jnp.concatenate([first_half * cos_wide - second_half * sin_wide, second_half * cos_wide + first_half * sin_wide], axis=-1)

def attend_block(query_block, first_row, key_rot, value_low):
    block_rows = query_block.shape[0]
    length = key_rot.shape[0]
    score_scale = query_block.shape[-1] ** (-0.5)
    scores = jnp.einsum('bkgd,lkd->kgbl', query_block, key_rot, precision=PRECISE) * score_scale
    scores = low_back(scores)
    row_pos = first_row + jnp.arange(block_rows, dtype=jnp.int32)
    col_pos = jnp.arange(length, dtype=jnp.int32)
    causal_keep = col_pos[None, :] <= row_pos[:, None]
    scores = jnp.where(causal_keep, scores, MASKED)
    row_peak = lax.optimization_barrier(jnp.max(scores, axis=-1, keepdims=True))
    raised = jnp.exp(scores - row_peak)
    weights_low = low(raised / lax.optimization_barrier(jnp.sum(raised, axis=-1, keepdims=True)))
    return jnp.einsum('kgbl,lkd->bkgd', weights_low, value_low, precision=PRECISE)

def layer(tokens, attn_gain, mlp_gain, query_gain, key_gain, w_query, key_weight, value_weight, w_out, w_gate, w_up, w_down):
    length = tokens.shape[0]
    head_size = query_gain.shape[0]
    heads_q = w_query.shape[1] // head_size
    heads_kv = key_weight.shape[1] // head_size
    group_size = heads_q // heads_kv
    normed = low(norm_rows(tokens, attn_gain))
    q_lin = low_back(jnp.dot(normed, w_query, precision=PRECISE)).reshape(length, heads_q, head_size)
    k_lin = low_back(jnp.dot(normed, key_weight, precision=PRECISE)).reshape(length, heads_kv, head_size)
    v_low = low(low_back(jnp.dot(normed, value_weight, precision=PRECISE))).reshape(length, heads_kv, head_size)
    cosine, sine = rope_tables(length, head_size)
    q_rot = low(rotate(norm_rows(q_lin, query_gain), cosine, sine))
    k_rot = low(rotate(norm_rows(k_lin, key_gain), cosine, sine))
    block_rows = min(QBLOCK, length)
    block_count = length // block_rows
    q_blocks = q_rot.reshape(block_count, block_rows, heads_kv, group_size, head_size)
    block_starts = jnp.arange(block_count, dtype=jnp.int32) * block_rows
    attend = jax.checkpoint(lambda block_pair: attend_block(block_pair[0], block_pair[1], k_rot, v_low))
    attended = lax.map(attend, (q_blocks, block_starts))
    attended = low_back(low(attended.reshape(length, heads_q * head_size)))
    branch_attn = low_back(jnp.dot(attended, w_out.T, precision=PRECISE))
    middle = tokens + branch_attn
    normed_mlp = low(norm_rows(middle, mlp_gain))
    gate_lin = low_back(jnp.dot(normed_mlp, w_gate, precision=PRECISE))
    up_lin = low_back(jnp.dot(normed_mlp, w_up, precision=PRECISE))
    hidden = low(jax.nn.silu(gate_lin) * up_lin)
    branch_mlp = low_back(jnp.dot(hidden, w_down.T, precision=PRECISE))
    return middle + branch_mlp

def reference(tokens, cotangent, attn_gain, mlp_gain, query_gain, key_gain, w_query, key_weight, value_weight, w_out, w_gate, w_up, w_down):
    params = tuple((item.astype(jnp.float32) for item in (attn_gain, mlp_gain, query_gain, key_gain, w_query, key_weight, value_weight, w_out, w_gate, w_up, w_down)))
    sequences = tokens.astype(jnp.float32).reshape(N_DP, SEQ_LEN, MODEL_WIDTH)
    cot_seqs = cotangent.astype(jnp.float32).reshape(N_DP, SEQ_LEN, MODEL_WIDTH)

    def one_sequence(grad_sums, item_pair):
        seq_rows, seq_cot = item_pair
        outcome, pullback = jax.vjp(layer, seq_rows, *params)
        grads = pullback(seq_cot)
        new_sums = tuple((acc + part for acc, part in zip(grad_sums, grads[1:])))
        return (new_sums, (outcome, grads[0]))
    start_sums = tuple((jnp.zeros_like(item) for item in params))
    grad_sums, (outcomes, input_grads) = lax.scan(one_sequence, start_sums, (sequences, cot_seqs))
    result = outcomes.reshape(TOKENS, MODEL_WIDTH).astype(jnp.bfloat16)
    tokens_grad = input_grads.reshape(TOKENS, MODEL_WIDTH)
    return (result, tokens_grad, grad_sums[0], grad_sums[1], grad_sums[2], grad_sums[3], grad_sums[4], grad_sums[5], grad_sums[6], grad_sums[7], grad_sums[8], grad_sums[9], grad_sums[10])
```

```python
import functools

import numpy as np
import jax
import jax.numpy as jnp
from jax import lax
from jax.experimental import pallas as pl
from jax.experimental.pallas import tpu as pltpu
from jax.sharding import PartitionSpec as P

EPS = 1e-06
ROPE_BASE = 1000000.0
MESH = pl.DeviceIdType.MESH
BF = jnp.bfloat16
F32 = jnp.float32
HEAD = 128
WIDTH = 2048
BLOCK = 128
ROWS = 1024
A_COLS = 768
B_COLS = 2304
A_CUT = 384
B_CUT = 1152
SCORE = HEAD ** -0.5
SCORE2 = HEAD ** -0.5 * 1.4426950408889634
VMEM_BYTES = 63 * 2**20


class Place:
    def __init__(self):
        dp = lax.axis_index("dp")
        tensor = lax.axis_index("tensor")
        self.dp = dp
        self.xlo = lax.div(dp, 8)
        self.z = lax.rem(lax.div(dp, 2), 4)
        self.c = lax.rem(dp, 2)
        self.y = lax.div(tensor, 2)
        self.xhi = lax.rem(tensor, 2)
        self.x = self.xhi * 2 + self.xlo

    def at(self, x=None, y=None, z=None, c=None):
        x = self.x if x is None else x
        y = self.y if y is None else y
        z = self.z if z is None else z
        c = self.c if c is None else c
        return (lax.rem(x, 2) * 8 + z * 2 + c, y * 2 + lax.div(x, 2))

    def sibling(self):
        return self.at(c=1 - self.c)


def ring(v, k):
    return lax.rem(v + k, 4)


def remote(src, dst, send_sem, recv_sem, target):
    return pltpu.make_async_remote_copy(
        src_ref=src, dst_ref=dst, send_sem=send_sem, recv_sem=recv_sem,
        device_id=target, device_id_type=MESH,
    )


def settle(ref, sem):
    pltpu.make_async_copy(ref, ref, sem).wait()


def rows_at(start, size):
    return pl.ds(pl.multiple_of(start, 128), size)


def greet(me, both_cores=False):
    barrier = pltpu.get_barrier_semaphore()
    others = [me.sibling()]
    for k in (1, 2, 3):
        others.append(me.at(y=ring(me.y, k)))
        if both_cores:
            others.append(me.at(y=ring(me.y, k), c=1 - me.c))
        for c in (0, 1):
            others.append(me.at(x=ring(me.x, k), c=c))
            others.append(me.at(z=ring(me.z, k), c=c))
    for other in others:
        pl.semaphore_signal(barrier, inc=1, device_id=other, device_id_type=MESH)
    return barrier, len(others)


class GatherRows:
    sems = 14

    def __init__(self, me, buf, send, recv):
        self.me, self.buf, self.send, self.recv = me, buf, send, recv

    def slot(self, c, y):
        return self.buf.at[rows_at((c * 4 + y) * BLOCK, BLOCK)]

    def to_sibling(self, y, k):
        me = self.me
        ref = self.slot(me.c, y)
        remote(ref, ref, self.send.at[4 + k], self.recv.at[4 + k], me.sibling()).start()

    def start(self):
        me = self.me
        own = self.slot(me.c, me.y)
        for k in (1, 3, 2):
            remote(own, own, self.send.at[k], self.recv.at[k], me.at(y=ring(me.y, k))).start()
        self.to_sibling(me.y, 0)

    def relay(self):
        me = self.me
        for k in (1, 3, 2):
            source = ring(me.y, 4 - k)
            settle(self.slot(me.c, source), self.recv.at[k])
            self.to_sibling(source, k)

    def finish(self):
        me = self.me
        own = self.slot(me.c, me.y)
        for k in (1, 2, 3):
            settle(own, self.send.at[k])
        for k in range(4):
            settle(own, self.send.at[4 + k])
            settle(self.slot(1 - me.c, ring(me.y, 4 - k)), self.recv.at[4 + k])


class ReduceRows:
    def __init__(self, me, sib_out, held, arrive, send, recv):
        self.me = me
        self.sib_out, self.held, self.arrive = sib_out, held, arrive
        self.send, self.recv = send, recv
        first = 1 - lax.div(me.y, 2)
        self.halves = (first, 1 - first)

    def other(self, tile):
        me = self.me
        for p, half in enumerate(self.halves):
            rows = rows_at(half * 256, 256)

            def step(j, _):
                cols = rows_at(j * 512, 512)
                self.sib_out[rows, cols] = tile((1 - me.c) * 512 + half * 256, j).astype(BF)
                return 0

            lax.fori_loop(0, 4, step, 0, unroll=True)
            remote(self.sib_out.at[rows], self.held.at[rows], self.send.at[4 + p], self.recv.at[4 + p],
                   me.sibling()).start()

    def mine(self, tile):
        me = self.me
        for p, half in enumerate(self.halves):
            rows = rows_at(half * 256, 256)
            settle(self.held.at[rows], self.recv.at[4 + p])

            def step(j, _):
                cols = rows_at(j * 512, 512)
                total = tile(me.c * 512 + half * 256, j) + self.held[rows, cols].astype(F32)
                self.held[rows, cols] = total.astype(BF)
                return 0

            lax.fori_loop(0, 4, step, 0, unroll=True)
            for q in (0, 1):
                block = half * 2 + q
                k = ring(block + 4 - me.y, 0)

                def go(block=block, k=k):
                    remote(self.held.at[rows_at(block * BLOCK, BLOCK)], self.arrive.at[k - 1], self.send.at[k],
                           self.recv.at[k], me.at(y=block)).start()

                if p == 0:
                    go()
                else:
                    pl.when(block != me.y)(go)

    def wait(self):
        for k in (1, 2, 3):
            settle(self.arrive.at[k - 1], self.recv.at[k])

    def total(self, r):
        total = self.held[pl.ds(pl.multiple_of(self.me.y * BLOCK + r, 16), 16), :].astype(F32)
        for k in (1, 2, 3):
            total = total + self.arrive[k - 1, pl.ds(pl.multiple_of(r, 16), 16), :].astype(F32)
        return total

    def finish(self):
        for k in (1, 2, 3):
            settle(self.arrive.at[k - 1], self.send.at[k])
        for p in (0, 1):
            settle(self.sib_out.at[rows_at(0, 256)], self.send.at[4 + p])


class GatherWeights:
    def __init__(self, me, shard, full, cut, send, recv):
        self.me, self.shard, self.full = me, shard, full
        self.cols = (pl.ds(0, cut), pl.ds(cut, shard.shape[1] - cut))
        self.send, self.recv = send, recv

    def slot(self, way, dp):
        return self.full.at[rows_at(dp * BLOCK, BLOCK), self.cols[way]]

    def first(self):
        me = self.me
        home = me.xhi
        for way in (0, 1):
            src = self.shard.at[:, self.cols[way]]
            dst = self.slot(way, me.dp)
            inbox = self.recv.at[(me.xlo * 2 + me.c) if way == 0 else (10 + me.z * 2 + me.c)]
            base = 0 if way == 0 else 10
            for k in (1, 3, 2):
                target = me.at(x=ring(me.x, k), c=home) if way == 0 else me.at(z=ring(me.z, k), c=home)
                remote(src, dst, self.send.at[base + k], inbox, target).start()

            @pl.when(me.c == home)
            def _():
                pltpu.make_async_copy(src, dst, inbox).start()

            @pl.when(me.c != home)
            def _():
                remote(src, dst, self.send.at[base], inbox, me.sibling()).start()

    def second(self):
        me = self.me
        for xlo in (0, 1):
            for c in (0, 1):
                settle(self.slot(0, xlo * 8 + me.z * 2 + c), self.recv.at[xlo * 2 + c])
        for k in (1, 3, 2):
            for xlo in (0, 1):
                ref = self.pair(xlo, me.z)
                i = 4 + xlo * 3 + k - 1
                remote(ref, ref, self.send.at[i], self.recv.at[i], me.at(z=ring(me.z, k))).start()

        @pl.when(me.c == me.xhi)
        def _():
            for z in range(4):
                for c in (0, 1):
                    settle(self.slot(1, me.xlo * 8 + z * 2 + c), self.recv.at[10 + z * 2 + c])
            ref = self.half(me.xlo)
            for k in (1, 3, 2):
                remote(ref, ref, self.send.at[18 + k], self.recv.at[18 + me.xlo], me.at(x=ring(me.x, k))).start()

    def pair(self, xlo, z):
        return self.full.at[rows_at(xlo * 1024 + z * 256, 256), self.cols[0]]

    def half(self, xlo):
        return self.full.at[rows_at(xlo * 1024, 1024), self.cols[1]]

    def arrived(self):
        me = self.me
        for k in (1, 2, 3):
            for xlo in (0, 1):
                settle(self.pair(xlo, ring(me.z, 4 - k)), self.recv.at[4 + xlo * 3 + k - 1])
        for xlo in (0, 1):
            @pl.when(jnp.logical_or(me.c != me.xhi, me.xlo != xlo))
            def _():
                settle(self.half(xlo), self.recv.at[18 + xlo])

    def finish(self):
        me = self.me
        for way in (0, 1):
            src = self.shard.at[:, self.cols[way]]
            base = 0 if way == 0 else 10
            for k in (1, 2, 3):
                settle(src, self.send.at[base + k])

            @pl.when(me.c != me.xhi)
            def _():
                settle(src, self.send.at[base])
        for k in (1, 2, 3):
            for xlo in (0, 1):
                settle(self.pair(xlo, me.z), self.send.at[4 + xlo * 3 + k - 1])

        @pl.when(me.c == me.xhi)
        def _():
            for k in (1, 2, 3):
                settle(self.half(me.xlo), self.send.at[18 + k])


def dot(left, right):
    return jnp.dot(left, right, preferred_element_type=F32)


def dot_t(left, right):
    return lax.dot_general(left, right, (((1,), (1,)), ((), ())), preferred_element_type=F32)


def inverse_of(values):
    return lax.rsqrt(jnp.mean(values * values, axis=-1, keepdims=True) + EPS)


def turn(values, cosine, sine):
    return values * cosine + pltpu.roll(values, 64, 1) * sine


def forward_kernel(
    tokens, cot, attn_gain, mlp_gain, query_gain, key_gain, wq, wk, wv, wo, wg, wu, wd, cosine, sine,
    n_out, cot_out, n2_out, a_out, b_out, qlin_out, klin_out, qrot_out, kv_out, o_out, mid_out,
    n, cota, n2, a, b, a_shard, b_shard, qlin, klin, qrot, kv, o, mid, sib_out, held, arrive,
    n_send, n_recv, c_send, c_recv, n2_send, n2_recv, a_send, a_recv, b_send, b_recv, r_send, r_recv,
    kv_sem, out_sem,
):
    me = Place()
    barrier, count = greet(me)
    a_shard[:, 0:256] = wq[...]
    a_shard[:, 256:384] = wk[...]
    a_shard[:, 384:512] = wv[...]
    a_shard[:, 512:768] = wo[...]
    b_shard[:, 0:768] = wg[...]
    b_shard[:, 768:1536] = wu[...]
    b_shard[:, 1536:2304] = wd[...]
    own = (me.c * 4 + me.y) * BLOCK

    def norm_one(i, _):
        rows = pl.ds(pl.multiple_of(i * 16, 16), 16)
        x = tokens[rows, :].astype(F32)
        n[pl.ds(pl.multiple_of(own + i * 16, 16), 16), :] = (x * inverse_of(x) * attn_gain[...]).astype(BF)
        return 0

    lax.fori_loop(0, 8, norm_one, 0)
    cota[rows_at(own, BLOCK), :] = cot[...]
    pl.semaphore_wait(barrier, count)

    weights_a = GatherWeights(me, a_shard, a, A_CUT, a_send, a_recv)
    weights_b = GatherWeights(me, b_shard, b, B_CUT, b_send, b_recv)
    rows_n = GatherRows(me, n, n_send, n_recv)
    rows_c = GatherRows(me, cota, c_send, c_recv)
    rows_n2 = GatherRows(me, n2, n2_send, n2_recv)
    weights_a.first()
    rows_n.start()
    weights_a.second()
    weights_b.first()
    rows_n.relay()
    rows_n.finish()
    rows_c.start()
    weights_a.arrived()
    outs = []

    def out(src, dst):
        copy = pltpu.make_async_copy(src, dst, out_sem.at[len(outs)])
        copy.start()
        outs.append(copy)

    out(n, n_out)
    out(a, a_out)

    def project(s, _):
        rows = rows_at(s * 512, 512)
        x = n[rows, :]
        cos, sin = cosine[me.xhi], sine[me.xhi]
        q = dot(x, a[:, 0:256])
        qlin[rows, :] = q
        for g in (0, 1):
            u = q[:, g * 128:(g + 1) * 128]
            u = turn(u * inverse_of(u) * query_gain[...], cos, sin).astype(BF)
            for block in range(4):
                qrot[rows_at(s * 1024 + block * 256 + g * 128, 128), :] = u[block * 128:(block + 1) * 128]
        k = dot(x, a[:, 256:512])
        klin[rows, :] = k[:, 0:128]
        u = k[:, 0:128]
        kv[0, rows, :] = turn(u * inverse_of(u) * key_gain[...], cos, sin).astype(BF)
        kv[1, rows, :] = k[:, 128:256].astype(BF)
        return 0

    lax.fori_loop(0, 2, project, 0)
    swap = remote(kv.at[0:2], kv.at[2:4], kv_sem.at[0], kv_sem.at[1], me.at(x=ring(me.x, 2)))
    swap.start()
    out(qlin, qlin_out)
    out(klin, klin_out)
    out(qrot, qrot_out)
    weights_b.second()
    swap.wait()
    out(kv, kv_out)

    def attend(s, _):
        for block in range(4):
            keys = rows_at(s * 512, (block + 1) * 128)
            q = qrot[rows_at(s * 1024 + block * 256, 256), :]
            shape = (256, (block + 1) * 128)
            row = lax.rem(lax.broadcasted_iota(jnp.int32, shape, 0), 128)
            col = lax.broadcasted_iota(jnp.int32, shape, 1)
            near = jnp.where(col <= row + block * 128, jnp.exp2(dot_t(q, kv[0, keys, :]) * SCORE2), 0.0)
            far = jnp.where(col < (block + me.xhi) * 128, jnp.exp2(dot_t(q, kv[2, keys, :]) * SCORE2), 0.0)
            total = jnp.sum(near, axis=-1, keepdims=True) + jnp.sum(far, axis=-1, keepdims=True)
            got = dot(near.astype(BF), kv[1, keys, :]) + dot(far.astype(BF), kv[3, keys, :])
            got = (got / total).astype(BF)
            rows = rows_at(s * 512 + block * 128, 128)
            o[rows, 0:128] = got[0:128]
            o[rows, 128:256] = got[128:256]
        return 0

    lax.fori_loop(0, 2, attend, 0)
    rows_c.relay()
    out(o, o_out)
    sums = ReduceRows(me, sib_out, held, arrive, r_send, r_recv)

    def branch(row, j):
        return dot_t(o[rows_at(row, 256), :], a[rows_at(j * 512, 512), 512:768])

    sums.other(branch)
    sums.mine(branch)
    rows_c.finish()
    out(cota, cot_out)
    sums.wait()

    def norm_two(i, _):
        rows = pl.ds(pl.multiple_of(i * 16, 16), 16)
        x = tokens[rows, :].astype(F32) + sums.total(i * 16)
        mid[rows, :] = x
        n2[pl.ds(pl.multiple_of(own + i * 16, 16), 16), :] = (x * inverse_of(x) * mlp_gain[...]).astype(BF)
        return 0

    lax.fori_loop(0, 8, norm_two, 0)
    rows_n2.start()
    out(mid, mid_out)
    weights_b.arrived()
    out(b, b_out)
    rows_n2.relay()
    rows_n2.finish()
    out(n2, n2_out)
    sums.finish()
    weights_a.finish()
    weights_b.finish()
    for copy in outs:
        copy.wait()


def forward(*args):
    shapes = [
        ((ROWS, WIDTH), BF), ((ROWS, WIDTH), BF), ((ROWS, WIDTH), BF), ((WIDTH, A_COLS), BF), ((WIDTH, B_COLS), BF),
        ((ROWS, 256), F32), ((ROWS, 128), F32), ((2 * ROWS, 128), BF), ((4, ROWS, 128), BF), ((ROWS, 256), BF),
        ((BLOCK, WIDTH), F32),
    ]
    scratch = [pltpu.VMEM(s, d) for s, d in shapes[:5]]
    scratch += [pltpu.VMEM((BLOCK, A_COLS), BF), pltpu.VMEM((BLOCK, B_COLS), BF)]
    scratch += [pltpu.VMEM(s, d) for s, d in shapes[5:]]
    scratch += [pltpu.VMEM((512, WIDTH), BF)] * 2 + [pltpu.VMEM((3, BLOCK, WIDTH), BF)]
    dma = pltpu.SemaphoreType.DMA
    scratch += [dma((8,))] * 6 + [dma((22,))] * 4 + [dma((6,))] * 2 + [dma((2,)), dma((len(shapes),))]
    return pl.pallas_call(
        forward_kernel,
        out_shape=[jax.ShapeDtypeStruct(s, d) for s, d in shapes],
        in_specs=[pl.BlockSpec(memory_space=pltpu.VMEM)] * len(args),
        out_specs=[pl.BlockSpec(memory_space=pl.ANY)] * len(shapes),
        scratch_shapes=scratch,
        compiler_params=pltpu.CompilerParams(
            collective_id=1, has_side_effects=True, vmem_limit_bytes=VMEM_BYTES),
        name="forward_part",
    )(*args)


def rope_tables():
    frequency = ROPE_BASE ** (-2.0 * np.arange(64, dtype=np.float64) / HEAD)
    angle = np.arange(1024, dtype=np.float64)[:, None] * frequency[None, :]
    cos = np.concatenate([np.cos(angle), np.cos(angle)], axis=1).astype(np.float32)
    sin = np.concatenate([-np.sin(angle), np.sin(angle)], axis=1).astype(np.float32)
    pick = lambda t: t.reshape(4, 2, 128, 128).transpose(1, 0, 2, 3).reshape(2, 512, 128)
    return pick(cos), pick(sin)


class ReduceWeights:
    sems = 14

    def __init__(self, me, grad, first_col, width, inbox, stage, part, left, right, send, recv, load):
        self.me, self.grad, self.width = me, grad, width
        self.cols = (pl.ds(first_col, width), pl.ds(first_col + width, width))
        self.inbox, self.stage, self.part, self.left, self.right = inbox, stage, part, left, right
        self.send, self.recv, self.load = send, recv, load

    def store(self, i, value):
        xlo, z = lax.div(i, 4), lax.rem(i, 4)
        value = value.astype(BF)
        self.grad[rows_at(z * 512 + xlo * 256, 256), self.cols[0]] = value[:, :self.width]
        for c in (0, 1):
            self.grad[rows_at((xlo * 2 + c) * 512 + z * 128, 128), self.cols[1]] = value[
                c * 128:(c + 1) * 128, self.width:]

    def block(self, way, i):
        return self.grad.at[rows_at(i * 512, 512), self.cols[way]]

    def over_x(self, sources, dst, base):
        me = self.me
        for xlo in (0, 1):
            for c in (0, 1):
                src = sources(xlo, c)
                x = me.c * 2 + xlo
                self_too = jnp.logical_and(me.x == x, me.c == c)

                @pl.when(self_too)
                def _():
                    pltpu.make_async_copy(src, dst, self.recv.at[base + me.x]).start()

                @pl.when(jnp.logical_not(self_too))
                def _():
                    remote(src, dst, self.send.at[base + xlo * 2 + c], self.recv.at[base + me.x],
                           me.at(x=x, c=c)).start()

    def over_x_sent(self, ref, base):
        me = self.me
        for xlo in (0, 1):
            for c in (0, 1):
                @pl.when(jnp.logical_or(me.x != me.c * 2 + xlo, me.c != c))
                def _():
                    settle(ref, self.send.at[base + xlo * 2 + c])

    def first(self):
        me = self.me
        for k in (1, 3, 2):
            z = ring(me.z, k)
            remote(self.block(0, z), self.inbox.at[k - 1], self.send.at[k - 1], self.recv.at[k - 1],
                   me.at(z=z)).start()
        self.over_x(lambda xlo, c: self.block(1, xlo * 2 + c), self.inbox.at[3 + me.x], 3)

    def second(self):
        me = self.me
        for i in range(7):
            settle(self.inbox.at[i], self.recv.at[i])
            pltpu.make_async_copy(self.inbox.at[i], self.stage[i], self.load.at[i]).start()
        for i in range(7):
            settle(self.stage[i], self.load.at[i])

        def add_z(i, _):
            rows = pl.ds(pl.multiple_of(i * 32, 32), 32)
            here = pl.ds(pl.multiple_of(me.z * 512 + i * 32, 32), 32)
            total = self.grad[here, self.cols[0]].astype(F32)
            for k in range(3):
                total = total + self.stage[k][rows, :].astype(F32)
            self.grad[here, self.cols[0]] = total.astype(BF)
            total = self.stage[3][rows, :].astype(F32)
            for k in range(4, 7):
                total = total + self.stage[k][rows, :].astype(F32)
            self.part[rows, :] = total.astype(BF)
            return 0

        lax.fori_loop(0, 16, add_z, 0)
        self.over_x(lambda xlo, c: self.grad.at[rows_at(me.z * 512 + xlo * 256 + c * 128, 128), self.cols[0]],
                    self.left.at[me.x], 7)
        for k in (1, 3, 2):
            z = ring(me.z, k)
            remote(self.part.at[rows_at(z * 128, 128)], self.right.at[k - 1], self.send.at[10 + k],
                   self.recv.at[10 + k], me.at(z=z)).start()

    def third(self, store):
        me = self.me
        for i in range(4):
            settle(self.left.at[i], self.recv.at[7 + i])
        for k in (1, 2, 3):
            settle(self.right.at[k - 1], self.recv.at[10 + k])

        def add(i, _):
            rows = pl.ds(pl.multiple_of(i * 32, 32), 32)
            left = self.left[0, rows, :].astype(F32)
            for x in range(1, 4):
                left = left + self.left[x, rows, :].astype(F32)
            right = self.part[pl.ds(pl.multiple_of(me.z * 128 + i * 32, 32), 32), :].astype(F32)
            for k in range(3):
                right = right + self.right[k, rows, :].astype(F32)
            store(rows, left, right)
            return 0

        lax.fori_loop(0, 4, add, 0)

    def finish(self):
        me = self.me
        for k in (1, 2, 3):
            settle(self.inbox.at[k - 1], self.send.at[k - 1])
            settle(self.right.at[k - 1], self.send.at[10 + k])
        self.over_x_sent(self.inbox.at[3], 3)
        self.over_x_sent(self.left.at[0], 7)


def dot_rows(left, right):
    return lax.dot_general(left, right, (((0,), (0,)), ((), ())), preferred_element_type=F32)


def back_norm(values, gain, upstream):
    entries = values.shape[-1]
    inverse = inverse_of(values)
    scaled = upstream * gain
    folded = jnp.sum(scaled * values, axis=-1, keepdims=True)
    grad = inverse * scaled - values * (inverse * inverse * inverse) * folded / entries
    return grad, jnp.sum(upstream * values * inverse, axis=0, keepdims=True)


def backward_kernel(
    tokens, cot, attn_gain, mlp_gain, query_gain, key_gain,
    n_in, cot_in, n2_in, a_in, b_in, qlin_in, klin_in, qrot_in, kv_in, o_in, mid_in, cosine, sine,
    result, tokens_grad, gains_out, qkv_grad, out_grad, gate_grad, up_grad, down_grad, box_q, box_o, box_g, box_u, box_d,
    n2, cota, a, b, da, h, dg, du, qlin, klin, qrot, kv, o, mid, dmid, cos, sin, dqkv, d_o, acc, acc_out, acc_in,
    sib_out, held, arrive, held2, arrive2,
    part_q, left_q, right_q, part_o, left_o, right_o, part_g, left_g, right_g, part_u, left_u, right_u,
    part_d, left_d, right_d, gain8, gainx, gainz,
    load, r1_send, r1_recv, r2_send, r2_recv, r3_send, r3_recv, da_send, da_recv,
    q_send, q_recv, o_send, o_recv, g_send, g_recv, u_send, u_recv, d_send, d_recv, stage_load, swap_sem, v_send, v_recv,
):
    me = Place()
    barrier, count = greet(me, True)
    waits = {}

    def fetch(name, src, dst):
        waits[name] = pltpu.make_async_copy(src, dst, load.at[len(waits)])
        waits[name].start()

    fetch("n2", n2_in, n2)
    fetch("b", b_in, b)
    fetch("cot", cot_in, cota)
    fetch("mid", mid_in, mid)
    fetch("a", a_in, a)
    fetch("o", o_in, o)
    fetch("qrot", qrot_in, qrot)
    fetch("kv", kv_in, kv)
    fetch("qlin", qlin_in, qlin)
    fetch("klin", klin_in, klin)
    fetch("cos", cosine.at[me.xhi], cos)
    fetch("sin", sine.at[me.xhi], sin)
    pl.semaphore_wait(barrier, count)
    waits["n2"].wait()
    waits["b"].wait()
    waits["cot"].wait()

    def hidden(i, _):
        rows = rows_at(lax.div(i, 3) * 512, 512)
        j = lax.rem(i, 3) * 256
        cols = rows_at(j, 256)
        gate = dot(n2[rows, :], b[:, cols])
        up = dot(n2[rows, :], b[:, rows_at(768 + j, 256)])
        d_hidden = dot(cota[rows, :], b[:, rows_at(1536 + j, 256)])
        sg = jax.nn.sigmoid(gate)
        active = gate * sg
        h[rows, cols] = (active * up).astype(BF)
        dg[rows, cols] = (d_hidden * up * sg * (1.0 + gate * (1.0 - sg))).astype(BF)
        du[rows, cols] = (d_hidden * active).astype(BF)
        return 0

    lax.fori_loop(0, 6, hidden, 0)
    sum_n2 = ReduceRows(me, sib_out, held, arrive, r1_send, r1_recv)
    sum_result = ReduceRows(me, sib_out, held2, arrive2, r2_send, r2_recv)
    sum_n = ReduceRows(me, sib_out, held, arrive, r3_send, r3_recv)

    def back_n2(row, j):
        rows, model = rows_at(row, 256), rows_at(j * 512, 512)
        return dot_t(dg[rows, :], b[model, 0:768]) + dot_t(du[rows, :], b[model, 768:1536])

    def down(row, j):
        return dot_t(h[rows_at(row, 256), :], b[rows_at(j * 512, 512), 1536:2304])

    sum_n2.other(back_n2)
    sum_n2.mine(back_n2)
    stage = [buf.at[pl.ds(r * 512, 512), pl.ds(q * 384, 384)] for buf in (dg, du) for r in (0, 1) for q in (0, 1)]
    stage_small = [buf.at[pl.ds(r * 512, 512), pl.ds(q * 384, 256)] for buf in (dg, du) for r in (0, 1) for q in (0, 1)]
    stage_o = [buf.at[pl.ds(r * 512, 512), pl.ds(q * 384, 128)] for buf in (dg, du) for r in (0, 1) for q in (0, 1)]
    red_g = ReduceWeights(me, b, 0, 384, box_g, stage, part_g, left_g, right_g, g_send, g_recv, stage_load)
    red_u = ReduceWeights(me, b, 768, 384, box_u, stage, part_u, left_u, right_u, u_send, u_recv, stage_load)
    red_d = ReduceWeights(me, b, 1536, 384, box_d, stage, part_d, left_d, right_d, d_send, d_recv, stage_load)
    red_o = ReduceWeights(me, a, 512, 128, box_o, stage_o, part_o, left_o, right_o, o_send, o_recv, stage_load)
    red_q = ReduceWeights(me, a, 0, 256, box_q, stage_small, part_q, left_q, right_q, q_send, q_recv, stage_load)

    def weight_grad(red, left, right):
        def step(i, _):
            red.store(i, dot_rows(left[:, rows_at(i * 256, 256)], right[...]))
            return 0

        lax.fori_loop(0, 8, step, 0)
        red.first()

    weight_grad(red_g, n2, dg)
    weight_grad(red_u, n2, du)
    sum_n2.finish()
    sum_result.other(down)
    sum_n2.wait()
    waits["mid"].wait()
    rows_da = GatherRows(me, da, da_send, da_recv)
    own = (me.c * 4 + me.y) * BLOCK

    def back_two(i, total):
        rows = pl.ds(pl.multiple_of(i * 16, 16), 16)
        grad, gain = back_norm(mid[rows, :], mlp_gain[...], sum_n2.total(i * 16))
        grad = grad + cot[rows, :].astype(F32)
        dmid[rows, :] = grad
        da[pl.ds(pl.multiple_of(own + i * 16, 16), 16), :] = grad.astype(BF)
        return total + gain

    mlp_part = lax.fori_loop(0, 8, back_two, jnp.zeros((1, WIDTH), F32))
    rows_da.start()
    slot = me.c * 4 + me.y
    gain8[slot, 1:2, :] = mlp_part
    rows_da.relay()
    sum_result.mine(down)
    weight_grad(red_d, cota, h)
    rows_da.finish()
    n_load = pltpu.make_async_copy(n_in, cota, load.at[12])
    n_load.start()
    for name in ("a", "o", "qrot", "kv", "qlin", "klin", "cos", "sin"):
        waits[name].wait()

    def back_o(i, _):
        rows = rows_at(i * 512, 512)
        d_o[rows, :] = dot(da[rows, :], a[:, 512:768]).astype(BF)
        return 0

    lax.fori_loop(0, 2, back_o, 0)
    weight_grad(red_o, da, o)

    swaps = []
    q_gain = jnp.zeros((1, HEAD), F32)
    for turn_ in (0, 1):
        s = 1 - me.c if turn_ == 0 else me.c
        for block in (3, 2, 1, 0):
            keys = rows_at(s * 512, (block + 1) * 128)
            rows = rows_at(s * 512 + block * 128, 128)
            q = qrot[rows_at(s * 1024 + block * 256, 256), :]
            g = jnp.concatenate([d_o[rows, 0:128], d_o[rows, 128:256]], axis=0)
            shape = (256, (block + 1) * 128)
            row = lax.rem(lax.broadcasted_iota(jnp.int32, shape, 0), 128)
            col = lax.broadcasted_iota(jnp.int32, shape, 1)
            near = jnp.where(col <= row + block * 128, jnp.exp2(dot_t(q, kv[0, keys, :]) * SCORE2), 0.0)
            far = jnp.where(col < (block + me.xhi) * 128, jnp.exp2(dot_t(q, kv[2, keys, :]) * SCORE2), 0.0)
            scale = 1.0 / (jnp.sum(near, axis=-1, keepdims=True) + jnp.sum(far, axis=-1, keepdims=True))
            near, far = near * scale, far * scale
            d_near, d_far = dot_t(g, kv[1, keys, :]), dot_t(g, kv[3, keys, :])
            delta = jnp.sum(d_near * near, axis=-1, keepdims=True) + jnp.sum(d_far * far, axis=-1, keepdims=True)
            s_near, s_far = (near * (d_near - delta)).astype(BF), (far * (d_far - delta)).astype(BF)
            dq = (dot(s_near, kv[0, keys, :]) + dot(s_far, kv[2, keys, :])) * SCORE
            parts = (dot_rows(s_near, q) * SCORE, dot_rows(near.astype(BF), g),
                     dot_rows(s_far, q) * SCORE, dot_rows(far.astype(BF), g))
            for i, value in enumerate(parts):
                if block == 3:
                    acc[i, keys, :] = value
                else:
                    acc[i, keys, :] += value
            turn_rows = pl.ds(block * 128, 128)
            for head in (0, 1):
                up = turn(dq[head * 128:(head + 1) * 128], cos[turn_rows, :], -sin[turn_rows, :])
                grad, gain = back_norm(qlin[rows, head * 128:(head + 1) * 128], query_gain[...], up)
                dqkv[rows, head * 128:(head + 1) * 128] = grad.astype(BF)
                q_gain = q_gain + gain
        rows = rows_at(s * 512, 512)
        for i in (0, 1):
            acc_out[turn_, i] = acc[2 + i, rows, :].astype(BF)
        swap = remote(acc_out.at[turn_], acc_in.at[turn_], swap_sem.at[turn_], swap_sem.at[2 + turn_],
                      me.at(x=ring(me.x, 2)))
        swap.start()
        swaps.append(swap)

    k_gain = jnp.zeros((1, HEAD), F32)

    def back_n(row, j):
        rows, model = rows_at(row, 256), rows_at(j * 512, 512)
        return dot_t(dqkv[rows, 0:256], a[model, 0:256]) + dot_t(dqkv[rows, 256:512], a[model, 256:512])

    for turn_ in (0, 1):
        s = 1 - me.c if turn_ == 0 else me.c
        rows = rows_at(s * 512, 512)
        swaps[turn_].wait()
        dk = acc[0, rows, :] + acc_in[turn_, 0].astype(F32)
        dv = acc[1, rows, :] + acc_in[turn_, 1].astype(F32)
        grad, gain = back_norm(klin[rows, :], key_gain[...], turn(dk, cos[...], -sin[...]))
        k_gain = k_gain + gain
        dqkv[rows, 256:384] = grad.astype(BF)
        dqkv[rows, 384:512] = dv.astype(BF)
        if turn_ == 0:
            sum_result.finish()
            sum_n.other(back_n)
        else:
            sum_n.mine(back_n)
    gain8[slot, 2:3, 0:128] = q_gain
    gain8[slot, 2:3, 128:256] = k_gain
    n_load.wait()
    weight_grad(red_q, cota, dqkv)

    def put(ref):
        def store(rows, left, right):
            width = left.shape[1]
            ref[rows, 0:width] = left
            ref[rows, width:2 * width] = right
        return store

    reds = ((red_g, gate_grad), (red_u, up_grad), (red_d, down_grad), (red_o, out_grad), (red_q, qkv_grad))
    for red, _ in reds[:4]:
        red.second()
    sum_result.wait()

    def finish_result(i, _):
        rows = pl.ds(pl.multiple_of(i * 16, 16), 16)
        result[rows, :] = (mid[rows, :] + sum_result.total(i * 16)).astype(BF)
        return 0

    lax.fori_loop(0, 8, finish_result, 0)
    sum_n.wait()

    def back_one(i, total):
        rows = pl.ds(pl.multiple_of(i * 16, 16), 16)
        grad, gain = back_norm(tokens[rows, :].astype(F32), attn_gain[...], sum_n.total(i * 16))
        tokens_grad[rows, :] = dmid[rows, :] + grad
        return total + gain

    gain8[slot, 0:1, :] = lax.fori_loop(0, 8, back_one, jnp.zeros((1, WIDTH), F32))

    peers = [(me.y, 1 - me.c)] + [(ring(me.y, k), c) for k in (1, 2, 3) for c in (0, 1)]
    for i, (y, c) in enumerate(peers):
        remote(gain8.at[slot], gain8.at[slot], v_send.at[i], v_recv.at[slot], me.at(y=y, c=c)).start()
    red_q.second()
    for i in range(8):
        @pl.when(slot != i)
        def _():
            settle(gain8.at[i], v_recv.at[i])
    total = gain8[0]
    for i in range(1, 8):
        total = total + gain8[i]
    gainx[me.x] = total
    for k in (1, 2, 3):
        remote(gainx.at[me.x], gainx.at[me.x], v_send.at[6 + k], v_recv.at[8 + me.x], me.at(x=ring(me.x, k))).start()
    for red, ref in reds[:3]:
        red.third(put(ref))
    for i in range(4):
        @pl.when(me.x != i)
        def _():
            settle(gainx.at[i], v_recv.at[8 + i])
    gainz[me.z] = gainx[0] + gainx[1] + gainx[2] + gainx[3]
    for k in (1, 2, 3):
        remote(gainz.at[me.z], gainz.at[me.z], v_send.at[9 + k], v_recv.at[12 + me.z], me.at(z=ring(me.z, k))).start()
    for red, ref in reds[3:]:
        red.third(put(ref))
    for i in range(4):
        @pl.when(me.z != i)
        def _():
            settle(gainz.at[i], v_recv.at[12 + i])
    gains_out[...] = gainz[0] + gainz[1] + gainz[2] + gainz[3]
    for i in range(13):
        settle(gain8.at[0], v_send.at[i])
    sum_n.finish()
    for red, _ in reds:
        red.finish()


def backward(tokens, cot, gains, saved, cos, sin):
    n, cota, n2, a, b, qlin, klin, qrot, kv, o, mid = saved
    args = (tokens, cot) + gains + saved + (cos, sin)
    vmem = pl.BlockSpec(memory_space=pltpu.VMEM)
    hbm = pl.BlockSpec(memory_space=pl.ANY)
    outs = [((BLOCK, WIDTH), BF), ((BLOCK, WIDTH), F32), ((8, WIDTH), F32), ((BLOCK, 512), F32), ((BLOCK, 256), F32)]
    outs += [((BLOCK, 768), F32)] * 3
    widths = (256, 128, 384, 384, 384)
    boxes = [((7, 512, w), BF) for w in widths]
    scratch = [
        ((ROWS, WIDTH), BF), ((ROWS, WIDTH), BF), ((WIDTH, A_COLS), BF), ((WIDTH, B_COLS), BF), ((ROWS, WIDTH), BF),
        ((ROWS, 768), BF), ((ROWS, 768), BF), ((ROWS, 768), BF), ((ROWS, 256), F32), ((ROWS, 128), F32),
        ((2 * ROWS, 128), BF), ((4, ROWS, 128), BF), ((ROWS, 256), BF), ((BLOCK, WIDTH), F32), ((BLOCK, WIDTH), F32),
        ((512, 128), F32), ((512, 128), F32), ((ROWS, 512), BF), ((ROWS, 256), BF), ((4, ROWS, 128), F32),
        ((2, 2, 512, 128), BF), ((2, 2, 512, 128), BF),
        ((512, WIDTH), BF), ((512, WIDTH), BF), ((3, BLOCK, WIDTH), BF), ((512, WIDTH), BF), ((3, BLOCK, WIDTH), BF),
    ]
    for w in widths:
        scratch += [((512, w), BF), ((4, BLOCK, w), BF), ((3, BLOCK, w), BF)]
    scratch += [((8, 8, WIDTH), F32), ((4, 8, WIDTH), F32), ((4, 8, WIDTH), F32)]
    scratch = [pltpu.VMEM(s, d) for s, d in scratch]
    dma = pltpu.SemaphoreType.DMA
    scratch += [dma((13,))] + [dma((6,))] * 6 + [dma((8,))] * 2 + [dma((14,))] * 10 + [dma((7,)), dma((4,))]
    scratch += [dma((13,)), dma((16,))]
    got = pl.pallas_call(
        backward_kernel,
        out_shape=[jax.ShapeDtypeStruct(s, d) for s, d in outs + boxes],
        in_specs=[vmem] * 6 + [hbm] * 13,
        out_specs=[vmem] * len(outs) + [hbm] * len(boxes),
        scratch_shapes=scratch,
        compiler_params=pltpu.CompilerParams(
            collective_id=2, has_side_effects=True, vmem_limit_bytes=VMEM_BYTES),
        name="backward_part",
    )(*args)
    return got[:len(outs)]


def local(tokens, cotangent, attn_gain, mlp_gain, query_gain, key_gain, *weights):
    cos, sin = rope_tables()
    gains = (attn_gain[None], mlp_gain[None], query_gain[None], key_gain[None])
    saved = forward(tokens, cotangent, *gains, *weights, cos, sin)
    result, tokens_grad, gains_out, qkv, out, gate, up, down = backward(tokens, cotangent, gains, tuple(saved), cos, sin)
    return (
        result, tokens_grad, gains_out[0], gains_out[1], gains_out[2, 0:128], gains_out[2, 128:256],
        qkv[:, 0:256], qkv[:, 256:384], qkv[:, 384:512], out, gate, up, down,
    )


def solution(mesh):
    rows, plane = P(("dp", "tensor"), None), P("dp", "tensor")
    return jax.shard_map(
        local,
        mesh=mesh,
        in_specs=(rows, rows, P(), P(), P(), P()) + (plane,) * 7,
        out_specs=(rows, rows, P(), P(), P(), P()) + (plane,) * 7,
        check_vma=False,
    )
```

```python
import functools

import numpy as np
import jax
import jax.numpy as jnp
from jax import lax
from jax.experimental import pallas as pl
from jax.experimental.pallas import tpu as pltpu
from jax.sharding import PartitionSpec as P

EPS = 1e-06
ROPE_BASE = 1000000.0
MESH = pl.DeviceIdType.MESH
BF = jnp.bfloat16
F32 = jnp.float32
HEAD = 128
WIDTH = 2048
BLOCK = 128
ROWS = 1024
A_COLS = 768
B_COLS = 2304
B_CUT = 1280
SCORE = HEAD ** -0.5
KV_SHAPE = (2, 2, 4, 2, 128, 128)
SCORE2 = HEAD ** -0.5 * 1.4426950408889634
VMEM_BYTES = 63 * 2**20


class Place:
    def __init__(self):
        dp = lax.axis_index("dp")
        tensor = lax.axis_index("tensor")
        self.dp = dp
        self.xlo = lax.div(dp, 8)
        self.z = lax.rem(lax.div(dp, 2), 4)
        self.c = lax.rem(dp, 2)
        self.y = lax.div(tensor, 2)
        self.xhi = lax.rem(tensor, 2)
        self.x = self.xhi * 2 + self.xlo

    def at(self, x=None, y=None, z=None, c=None):
        x = self.x if x is None else x
        y = self.y if y is None else y
        z = self.z if z is None else z
        c = self.c if c is None else c
        return (lax.rem(x, 2) * 8 + z * 2 + c, y * 2 + lax.div(x, 2))

    def sibling(self):
        return self.at(c=1 - self.c)


def ring(v, k):
    return lax.rem(v + k, 4)


def remote(src, dst, send_sem, recv_sem, target):
    return pltpu.make_async_remote_copy(
        src_ref=src, dst_ref=dst, send_sem=send_sem, recv_sem=recv_sem,
        device_id=target, device_id_type=MESH,
    )


def settle(ref, sem):
    pltpu.make_async_copy(ref, ref, sem).wait()


def rows_at(start, size):
    return pl.ds(pl.multiple_of(start, 128), size)


def greet(me, both_cores=False):
    barrier = pltpu.get_barrier_semaphore()
    others = [me.sibling()]
    for k in (1, 2, 3):
        others.append(me.at(y=ring(me.y, k)))
        if both_cores:
            others.append(me.at(y=ring(me.y, k), c=1 - me.c))
        for c in (0, 1):
            others.append(me.at(x=ring(me.x, k), c=c))
            others.append(me.at(z=ring(me.z, k), c=c))
    for other in others:
        pl.semaphore_signal(barrier, inc=1, device_id=other, device_id_type=MESH)
    return barrier, len(others)


class GatherRows:
    sems = 13

    def __init__(self, me, buf, send, recv):
        self.me, self.buf, self.send, self.recv = me, buf, send, recv

    def piece(self, c, y, half):
        return self.buf.at[pl.ds(pl.multiple_of((c * 4 + y) * BLOCK + half * 64, 64), 64)]

    def go(self, y, half, i, target):
        ref = self.piece(self.me.c, y, half)
        remote(ref, ref, self.send.at[i], self.recv.at[i], target).start()

    def start(self):
        me = self.me
        up, down = me.at(y=ring(me.y, 1)), me.at(y=ring(me.y, 3))
        self.go(me.y, 0, 0, up)
        self.go(me.y, 1, 2, down)
        own = self.buf.at[rows_at((me.c * 4 + me.y) * BLOCK, BLOCK)]
        remote(own, own, self.send.at[6], self.recv.at[6], me.sibling()).start()

    def heard(self, i, k, half):
        me = self.me
        y = ring(me.y, 4 - k)
        settle(self.piece(me.c, y, half), self.recv.at[i])
        self.go(y, half, 7 + i, me.sibling())
        return y

    def relay(self):
        me = self.me
        up, down = me.at(y=ring(me.y, 1)), me.at(y=ring(me.y, 3))
        half = self.piece(me.c, me.y, 0)
        settle(half, self.send.at[0])
        self.go(me.y, 1, 1, up)
        settle(half, self.send.at[2])
        self.go(me.y, 0, 3, down)
        y = self.heard(0, 1, 0)
        self.go(y, 0, 4, up)
        y = self.heard(2, 3, 1)
        self.go(y, 1, 5, down)

    def finish(self):
        me = self.me
        self.heard(1, 1, 1)
        self.heard(3, 3, 0)
        self.heard(4, 2, 0)
        self.heard(5, 2, 1)
        half = self.piece(me.c, me.y, 0)
        own = self.buf.at[rows_at((me.c * 4 + me.y) * BLOCK, BLOCK)]
        for i in (1, 3, 4, 5, 6, 7, 8, 9, 10, 11, 12):
            settle(own if i == 6 else half, self.send.at[i])
        for i in range(6, 13):
            settle(own if i == 6 else half, self.recv.at[i])


class ReduceRows:
    def __init__(self, me, sib_out, held, arrive, send, recv):
        self.me = me
        self.sib_out, self.held, self.arrive = sib_out, held, arrive
        self.send, self.recv = send, recv
        first = 1 - lax.div(me.y, 2)
        self.halves = (first, 1 - first)

    def other(self, tile):
        me = self.me
        for p, half in enumerate(self.halves):
            rows = rows_at(half * 256, 256)

            def step(j, _):
                cols = rows_at(j * 512, 512)
                self.sib_out[rows, cols] = tile((1 - me.c) * 512 + half * 256, j).astype(BF)
                return 0

            lax.fori_loop(0, 4, step, 0, unroll=True)
            remote(self.sib_out.at[rows], self.held.at[rows], self.send.at[6 + p], self.recv.at[6 + p],
                   me.sibling()).start()

    def piece(self, k, half):
        return pl.ds(pl.multiple_of(ring(self.me.y, k) * BLOCK + half * 64, 64), 64)

    def go(self, i, k, half, step):
        remote(self.held.at[self.piece(k, half)], self.arrive.at[i], self.send.at[i], self.recv.at[i],
               self.me.at(y=ring(self.me.y, step))).start()

    def mine(self, tile, send=True):
        me = self.me
        for p, half in enumerate(self.halves):
            rows = rows_at(half * 256, 256)
            settle(self.held.at[rows], self.recv.at[6 + p])

            def step(j, _):
                cols = rows_at(j * 512, 512)
                total = tile(me.c * 512 + half * 256, j) + self.held[rows, cols].astype(F32)
                self.held[rows, cols] = total.astype(BF)
                return 0

            lax.fori_loop(0, 4, step, 0, unroll=True)
            if not send:
                continue
            even = lax.rem(me.y, 2) == 0
            if p == 0:
                self.go(0, 2, 0, 1)
                self.go(1, 2, 1, 3)
            pl.when(even if p == 0 else jnp.logical_not(even))(lambda: self.go(3, 3, 0, 3))
            pl.when(jnp.logical_not(even) if p == 0 else even)(lambda: self.go(2, 1, 1, 1))

    def send_all(self):
        self.go(0, 2, 0, 1)
        self.go(1, 2, 1, 3)
        self.go(2, 1, 1, 1)
        self.go(3, 3, 0, 3)

    def relay(self):
        for i, k, half, step in ((0, 1, 0, 1), (1, 3, 1, 3)):
            settle(self.arrive.at[i], self.recv.at[i])
            rows = self.piece(k, half)
            self.held[rows, :] = (self.held[rows, :].astype(F32) + self.arrive[i].astype(F32)).astype(BF)
            self.go(4 + i, k, half, step)

    def wait(self):
        for i in range(2, 6):
            settle(self.arrive.at[i], self.recv.at[i])

    def total(self, r):
        half = lax.div(r, 64)
        rows = pl.ds(pl.multiple_of(r - half * 64, 16), 16)
        total = self.held[pl.ds(pl.multiple_of(self.me.y * BLOCK + r, 16), 16), :].astype(F32)
        return total + self.arrive[3 - half, rows, :].astype(F32) + self.arrive[4 + half, rows, :].astype(F32)

    def finish(self):
        for i in range(6):
            settle(self.arrive.at[i], self.send.at[i])
        for p in (0, 1):
            settle(self.sib_out.at[rows_at(0, 256)], self.send.at[6 + p])


class GatherWeights:
    sems = 23

    def __init__(self, me, shard, full, col, cut, width, send, recv):
        self.me, self.shard, self.full = me, shard, full
        self.cols = (pl.ds(col, cut), pl.ds(col + cut, width - cut))
        self.from_cols = (pl.ds(0, cut), pl.ds(cut, width - cut))
        self.send, self.recv = send, recv
        self.ways = (0, 1) if cut < width else (0,)

    def slot(self, way, dp):
        return self.full.at[rows_at(dp * BLOCK, BLOCK), self.cols[way]]

    def first(self, way):
        me = self.me
        home = me.xhi
        src = self.shard.at[:, self.from_cols[way]]
        dst = self.slot(way, me.dp)
        inbox = self.recv.at[(me.xlo * 2 + me.c) if way == 0 else (10 + me.z * 2 + me.c)]
        base = 0 if way == 0 else 10
        for k in (1, 3, 2):
            target = me.at(x=ring(me.x, k), c=home) if way == 0 else me.at(z=ring(me.z, k), c=home)
            remote(src, dst, self.send.at[base + k], inbox, target).start()

        @pl.when(me.c == home)
        def _():
            pltpu.make_async_copy(src, dst, inbox).start()

        @pl.when(me.c != home)
        def _():
            remote(src, dst, self.send.at[base], inbox, me.sibling()).start()

    def second_z(self):
        me = self.me
        for xlo in (0, 1):
            for c in (0, 1):
                settle(self.slot(0, xlo * 8 + me.z * 2 + c), self.recv.at[xlo * 2 + c])
        self.go(0, me.z, 4, 1)
        self.go(1, me.z, 6, 3)
        self.go(1, me.z, 5, 1)
        self.go(0, me.z, 7, 3)

    def go(self, xlo, z, i, step):
        ref = self.pair(xlo, z)
        remote(ref, ref, self.send.at[i], self.recv.at[i], self.me.at(z=ring(self.me.z, step))).start()

    def relay(self):
        me = self.me
        for i, xlo, step in ((4, 0, 1), (6, 1, 3)):
            z = ring(me.z, 4 - step)
            settle(self.pair(xlo, z), self.recv.at[i])
            self.go(xlo, z, 8 + xlo, step)

    def second_x(self):
        me = self.me
        if 1 not in self.ways:
            return

        @pl.when(me.c == me.xhi)
        def _():
            for z in range(4):
                for c in (0, 1):
                    settle(self.slot(1, me.xlo * 8 + z * 2 + c), self.recv.at[10 + z * 2 + c])
            for i, (part, step) in enumerate(((0, 1), (1, 3), (1, 1), (0, 3))):
                self.go_x(me.xlo, part, 18 + i, ring(me.x, step))

    def go_x(self, xlo, part, i, x):
        ref = self.quarter(xlo, part)
        remote(ref, ref, self.send.at[i], self.recv.at[18 + xlo * 2 + part], self.me.at(x=x)).start()

    def near_x(self):
        me = self.me
        below = lax.div(ring(me.x, 3), 2)
        up = 1 - (below + me.c - 2 * below * me.c)
        return up, lax.rem(ring(me.x, 1 + 2 * up), 2), 1 - up

    def relay_x(self):
        if 1 not in self.ways:
            return
        up, xlo, part = self.near_x()
        settle(self.quarter(0, 0), self.recv.at[18 + xlo * 2 + part])
        self.go_x(xlo, part, 22, ring(self.me.x, 3 - 2 * up))

    def pair(self, xlo, z):
        return self.full.at[rows_at(xlo * 1024 + z * 256, 256), self.cols[0]]

    def quarter(self, xlo, part):
        return self.full.at[rows_at(xlo * 1024 + part * 512, 512), self.cols[1]]

    def arrived(self):
        me = self.me
        for i in (5, 7, 8, 9):
            settle(self.pair(0, me.z), self.recv.at[i])
        if 1 not in self.ways:
            return
        _, near, near_part = self.near_x()
        for xlo in (0, 1):
            for part in (0, 1):
                here = jnp.logical_and(me.c == me.xhi, me.xlo == xlo)
                done = jnp.logical_and(near == xlo, near_part == part)

                @pl.when(jnp.logical_not(jnp.logical_or(here, done)))
                def _():
                    settle(self.quarter(0, 0), self.recv.at[18 + xlo * 2 + part])

    def finish(self):
        me = self.me
        for way in self.ways:
            src = self.shard.at[:, self.from_cols[way]]
            base = 0 if way == 0 else 10
            for k in (1, 2, 3):
                settle(src, self.send.at[base + k])

            @pl.when(me.c != me.xhi)
            def _():
                settle(src, self.send.at[base])
        for i in range(4, 10):
            settle(self.pair(0, me.z), self.send.at[i])

        if 1 not in self.ways:
            return

        @pl.when(me.c == me.xhi)
        def _():
            for i in range(18, 22):
                settle(self.quarter(0, 0), self.send.at[i])

        settle(self.quarter(0, 0), self.send.at[22])


def dot(left, right):
    return jnp.dot(left, right, preferred_element_type=F32)


def dot_t(left, right):
    return lax.dot_general(left, right, (((1,), (1,)), ((), ())), preferred_element_type=F32)


def inverse_of(values):
    return lax.rsqrt(jnp.mean(values * values, axis=-1, keepdims=True) + EPS)


def turn(values, cosine, sine):
    return values * cosine + pltpu.roll(values, 64, 1) * sine


def mask_last(values, keep, axis):
    size = values.shape[axis]
    last = jnp.where(keep, lax.slice_in_dim(values, size - 256, size, axis=axis), 0.0)
    if size == 256:
        return last
    return jnp.concatenate([lax.slice_in_dim(values, 0, size - 256, axis=axis), last], axis=axis)


def forward_kernel(
    tokens, cot, attn_gain, mlp_gain, query_gain, key_gain, wq, wk, wv, wo, wg, wu, wd, cosine, sine,
    n_out, cot_out, n2_out, a_out, b_out, qlin_out, klin_out, qrot_out, kv_out, o_out, mid_out,
    n, cota, n2, a, b, a_shard, b_shard, qlin, klin, qrot, kv, o, mid, sib_out, held, arrive,
    n_send, n_recv, c_send, c_recv, n2_send, n2_recv, a_send, a_recv, o_send, o_recv, b_send, b_recv, r_send, r_recv,
    kv_sem, out_sem,
):
    me = Place()
    barrier, count = greet(me)
    a_shard[:, 0:256] = wq[...]
    a_shard[:, 256:384] = wk[...]
    a_shard[:, 384:512] = wv[...]
    b_shard[:, 0:768] = wg[...]
    b_shard[:, 768:1536] = wu[...]
    b_shard[:, 1536:2304] = wd[...]
    own = (me.c * 4 + me.y) * BLOCK

    def norm_one(i, _):
        rows = pl.ds(pl.multiple_of(i * 16, 16), 16)
        x = tokens[rows, :].astype(F32)
        n[pl.ds(pl.multiple_of(own + i * 16, 16), 16), :] = (x * inverse_of(x) * attn_gain[...]).astype(BF)
        return 0

    lax.fori_loop(0, 8, norm_one, 0)
    cota[rows_at(own, BLOCK), :] = cot[...]
    pl.semaphore_wait(barrier, count)

    weights_a = GatherWeights(me, a_shard, a, 0, 384, 512, a_send, a_recv)
    weights_o = GatherWeights(me, wo, a, 512, 256, 256, o_send, o_recv)
    weights_b = GatherWeights(me, b_shard, b, 0, B_CUT, B_COLS, b_send, b_recv)
    rows_n = GatherRows(me, n, n_send, n_recv)
    rows_c = GatherRows(me, cota, c_send, c_recv)
    rows_n2 = GatherRows(me, n2, n2_send, n2_recv)
    rows_n.start()
    weights_a.first(0)
    weights_a.first(1)
    weights_o.first(0)
    weights_a.second_z()
    weights_b.first(0)
    weights_a.second_x()
    rows_n.relay()
    weights_a.relay()
    weights_o.second_z()
    weights_a.relay_x()
    rows_n.finish()
    rows_c.start()
    weights_a.arrived()
    weights_o.relay()
    weights_b.first(1)
    outs = []

    def out(src, dst):
        copy = pltpu.make_async_copy(src, dst, out_sem.at[len(outs)])
        copy.start()
        outs.append(copy)

    out(n, n_out)

    def project(s):
        rows = rows_at(s * 512, 512)
        x = n[rows, :]
        cos, sin = cosine[me.xhi], sine[me.xhi]
        k = dot(x, a[:, 256:512])
        klin[rows, :] = k[:, 0:128]
        u = k[:, 0:128]
        u = turn(u * inverse_of(u) * key_gain[...], cos, sin).astype(BF)
        v = k[:, 128:256].astype(BF)
        for block in range(4):
            kv[0, s, block, 0] = u[block * 128:(block + 1) * 128]
            kv[1, s, block, 0] = v[block * 128:(block + 1) * 128]

    def project_q(s):
        rows = rows_at(s * 512, 512)
        cos, sin = cosine[me.xhi], sine[me.xhi]
        q = dot(n[rows, :], a[:, 0:256])
        qlin[rows, :] = q
        for g in (0, 1):
            u = q[:, g * 128:(g + 1) * 128]
            u = turn(u * inverse_of(u) * query_gain[...], cos, sin).astype(BF)
            for block in range(4):
                qrot[rows_at(s * 1024 + block * 256 + g * 128, 128), :] = u[block * 128:(block + 1) * 128]

    order = (1 - me.c, me.c)
    swaps = []
    for i, s in enumerate(order):
        project(s)
        swap = remote(kv.at[:, s, :, 0], kv.at[:, s, :, 1], kv_sem.at[i], kv_sem.at[2 + i], me.at(x=ring(me.x, 2)))
        swap.start()
        swaps.append(swap)
    for s in order:
        project_q(s)
    out(qlin, qlin_out)
    out(klin, klin_out)
    out(qrot, qrot_out)
    rows_c.relay()
    weights_b.second_z()

    def attend(s):
        for block in range(4):
            size = (block + 1) * 256
            q = qrot[rows_at(s * 1024 + block * 256, 256), :]
            weights = jnp.exp2(dot_t(q, kv[0, s, 0:block + 1].reshape(size, 128)) * SCORE2)
            row = lax.rem(lax.broadcasted_iota(jnp.int32, (256, 256), 0), 128)
            col = lax.broadcasted_iota(jnp.int32, (256, 256), 1)
            weights = mask_last(weights, jnp.logical_or(col <= row, col >= 256 - 128 * me.xhi), 1)
            total = jnp.sum(weights, axis=-1, keepdims=True)
            got = dot(weights.astype(BF), kv[1, s, 0:block + 1].reshape(size, 128))
            got = (got / total).astype(BF)
            rows = rows_at(s * 512 + block * 128, 128)
            o[rows, 0:128] = got[0:128]
            o[rows, 128:256] = got[128:256]

    sums = ReduceRows(me, sib_out, held, arrive, r_send, r_recv)

    def branch(row, j):
        return dot_t(o[rows_at(row, 256), :], a[rows_at(j * 512, 512), 512:768])

    swaps[0].wait()
    attend(order[0])
    weights_o.arrived()
    out(a, a_out)
    sums.other(branch)
    swaps[1].wait()
    weights_b.second_x()
    out(kv, kv_out)
    attend(order[1])
    out(o, o_out)
    sums.mine(branch)
    sums.relay()
    rows_c.finish()
    out(cota, cot_out)
    weights_b.relay()
    weights_b.relay_x()
    sums.wait()

    def norm_two(i, _):
        rows = pl.ds(pl.multiple_of(i * 16, 16), 16)
        x = tokens[rows, :].astype(F32) + sums.total(i * 16)
        mid[rows, :] = x
        n2[pl.ds(pl.multiple_of(own + i * 16, 16), 16), :] = (x * inverse_of(x) * mlp_gain[...]).astype(BF)
        return 0

    lax.fori_loop(0, 8, norm_two, 0)
    rows_n2.start()
    out(mid, mid_out)
    rows_n2.relay()
    rows_n2.finish()
    out(n2, n2_out)
    weights_b.arrived()
    out(b, b_out)
    sums.finish()
    weights_a.finish()
    weights_o.finish()
    weights_b.finish()
    for copy in outs:
        copy.wait()


def forward(*args):
    shapes = [
        ((ROWS, WIDTH), BF), ((ROWS, WIDTH), BF), ((ROWS, WIDTH), BF), ((WIDTH, A_COLS), BF), ((WIDTH, B_COLS), BF),
        ((ROWS, 256), F32), ((ROWS, 128), F32), ((2 * ROWS, 128), BF), (KV_SHAPE, BF), ((ROWS, 256), BF),
        ((BLOCK, WIDTH), F32),
    ]
    scratch = [pltpu.VMEM(s, d) for s, d in shapes[:5]]
    scratch += [pltpu.VMEM((BLOCK, 512), BF), pltpu.VMEM((BLOCK, B_COLS), BF)]
    scratch += [pltpu.VMEM(s, d) for s, d in shapes[5:]]
    scratch += [pltpu.VMEM((512, WIDTH), BF)] * 2 + [pltpu.VMEM((6, 64, WIDTH), BF)]
    dma = pltpu.SemaphoreType.DMA
    scratch += [dma((GatherRows.sems,))] * 6 + [dma((GatherWeights.sems,))] * 6 + [dma((8,))] * 2
    scratch += [dma((4,)), dma((len(shapes),))]
    return pl.pallas_call(
        forward_kernel,
        out_shape=[jax.ShapeDtypeStruct(s, d) for s, d in shapes],
        in_specs=[pl.BlockSpec(memory_space=pltpu.VMEM)] * len(args),
        out_specs=[pl.BlockSpec(memory_space=pl.ANY)] * len(shapes),
        scratch_shapes=scratch,
        compiler_params=pltpu.CompilerParams(
            collective_id=1, has_side_effects=True, vmem_limit_bytes=VMEM_BYTES),
        name="forward_part",
    )(*args)


def rope_tables():
    frequency = ROPE_BASE ** (-2.0 * np.arange(64, dtype=np.float64) / HEAD)
    angle = np.arange(1024, dtype=np.float64)[:, None] * frequency[None, :]
    cos = np.concatenate([np.cos(angle), np.cos(angle)], axis=1).astype(np.float32)
    sin = np.concatenate([-np.sin(angle), np.sin(angle)], axis=1).astype(np.float32)
    pick = lambda t: t.reshape(4, 2, 128, 128).transpose(1, 0, 2, 3).reshape(2, 512, 128)
    return pick(cos), pick(sin)


WIDE, NARROW = (512, 256), (128, 128)


class ReduceWeights:
    sems = 17

    def __init__(self, me, grad, first_col, widths, inbox, stage, part, left, right, send, recv, load, fold=0):
        self.me, self.grad, self.widths, self.fold = me, grad, widths, fold
        self.first_cols = (first_col, first_col + widths[0])
        self.inbox, self.stage, self.part, self.left, self.right = inbox, stage, part, left, right
        self.send, self.recv, self.load = send, recv, load

    def place(self, way, start, size):
        col = self.first_cols[way]
        if self.fold:
            high = lax.div(start, 1024)
            start = start - high * 1024
            col = pl.multiple_of(col + high * self.fold, 128)
        return pl.ds(pl.multiple_of(start, 32), size), pl.ds(col, self.widths[way])

    def store(self, i, value):
        xlo, z = lax.div(i, 4), lax.rem(i, 4)
        value = value.astype(BF)
        self.grad[self.place(0, z * 512 + xlo * 256, 256)] = value[:, :self.widths[0]]
        for c in (0, 1):
            self.grad[self.place(1, (xlo * 2 + c) * 512 + z * 128, 128)] = value[
                c * 128:(c + 1) * 128, self.widths[0]:]

    def piece(self, k, half):
        return self.grad.at[self.place(0, ring(self.me.z, k) * 512 + half * 256, 256)]

    def go(self, i, k, half, step):
        remote(self.piece(k, half), self.inbox[0].at[i], self.send.at[i], self.recv.at[i],
               self.me.at(z=ring(self.me.z, step))).start()

    def over_x(self, sources, dst, base):
        me = self.me
        for xlo in (0, 1):
            for c in (0, 1):
                src = sources(xlo, c)
                x = me.c * 2 + xlo
                self_too = jnp.logical_and(me.x == x, me.c == c)

                @pl.when(self_too)
                def _():
                    pltpu.make_async_copy(src, dst, self.recv.at[base + me.x]).start()

                @pl.when(jnp.logical_not(self_too))
                def _():
                    remote(src, dst, self.send.at[base + xlo * 2 + c], self.recv.at[base + me.x],
                           me.at(x=x, c=c)).start()

    def over_x_sent(self, ref, base):
        me = self.me
        for xlo in (0, 1):
            for c in (0, 1):
                @pl.when(jnp.logical_or(me.x != me.c * 2 + xlo, me.c != c))
                def _():
                    settle(ref, self.send.at[base + xlo * 2 + c])

    def first(self):
        self.go(0, 2, 0, 1)
        self.go(1, 2, 1, 3)
        self.go(2, 1, 1, 1)
        self.go(3, 3, 0, 3)
        self.over_x(lambda xlo, c: self.grad.at[self.place(1, jnp.int32((xlo * 2 + c) * 512), 512)],
                    self.inbox[1].at[self.me.x], 6)

    def fetch(self, i):
        way, slot = (0, i) if i < 6 else (1, i - 6)
        settle(self.inbox[way].at[slot], self.recv.at[i])
        pltpu.make_async_copy(self.inbox[way].at[slot], self.stage[way][slot], self.load.at[i]).start()

    def fetched(self, i):
        way, slot = (0, i) if i < 6 else (1, i - 6)
        settle(self.stage[way][slot], self.load.at[i])

    def relay(self):
        self.fetch(0)
        self.fetch(1)
        for i, k, half, step in ((0, 1, 0, 1), (1, 3, 1, 3)):
            self.fetched(i)
            base = ring(self.me.z, k) * 512 + half * 256

            def add(r, _):
                here = self.place(0, base + r * 64, 64)
                more = self.stage[0][i][pl.ds(pl.multiple_of(r * 64, 64), 64), :]
                self.grad[here] = (self.grad[here].astype(F32) + more.astype(F32)).astype(BF)
                return 0

            lax.fori_loop(0, 4, add, 0)
            self.go(4 + i, k, half, step)

    def second(self):
        me = self.me
        for i in range(2, 10):
            self.fetch(i)
        for i in range(2, 10):
            self.fetched(i)

        def add_z(r, _):
            rows = pl.ds(pl.multiple_of(r * 32, 32), 32)
            for half in (0, 1):
                here = self.place(0, me.z * 512 + half * 256 + r * 32, 32)
                total = self.grad[here].astype(F32)
                for i in (3 - half, 4 + half):
                    total = total + self.stage[0][i][rows, :].astype(F32)
                self.grad[here] = total.astype(BF)
                rows_x = pl.ds(pl.multiple_of(half * 256 + r * 32, 32), 32)
                total = self.stage[1][0][rows_x, :].astype(F32)
                for i in range(1, 4):
                    total = total + self.stage[1][i][rows_x, :].astype(F32)
                self.part[rows_x, :] = total.astype(BF)
            return 0

        lax.fori_loop(0, 8, add_z, 0)
        self.over_x(lambda xlo, c: self.grad.at[self.place(0, me.z * 512 + xlo * 256 + c * 128, 128)],
                    self.left.at[me.x], 10)
        for k in (1, 3, 2):
            z = ring(me.z, k)
            remote(self.part.at[rows_at(z * 128, 128)], self.right.at[k - 1], self.send.at[13 + k],
                   self.recv.at[13 + k], me.at(z=z)).start()

    def third(self, store):
        me = self.me
        for i in range(4):
            settle(self.left.at[i], self.recv.at[10 + i])
        for k in (1, 2, 3):
            settle(self.right.at[k - 1], self.recv.at[13 + k])

        def add(i, _):
            rows = pl.ds(pl.multiple_of(i * 32, 32), 32)
            left = self.left[0, rows, :].astype(F32)
            for x in range(1, 4):
                left = left + self.left[x, rows, :].astype(F32)
            right = self.part[pl.ds(pl.multiple_of(me.z * 128 + i * 32, 32), 32), :].astype(F32)
            for k in range(3):
                right = right + self.right[k, rows, :].astype(F32)
            store(rows, left, right)
            return 0

        lax.fori_loop(0, 4, add, 0)

    def finish(self):
        for i in range(6):
            settle(self.inbox[0].at[i], self.send.at[i])
        for k in (1, 2, 3):
            settle(self.right.at[k - 1], self.send.at[13 + k])
        self.over_x_sent(self.inbox[1].at[0], 6)
        self.over_x_sent(self.left.at[0], 10)


def dot_rows(left, right):
    return lax.dot_general(left, right, (((0,), (0,)), ((), ())), preferred_element_type=F32)


def back_norm(values, gain, upstream):
    entries = values.shape[-1]
    inverse = inverse_of(values)
    scaled = upstream * gain
    folded = jnp.sum(scaled * values, axis=-1, keepdims=True)
    grad = inverse * scaled - values * (inverse * inverse * inverse) * folded / entries
    return grad, jnp.sum(upstream * values * inverse, axis=0, keepdims=True)


def backward_kernel(
    tokens, cot, attn_gain, mlp_gain, query_gain, key_gain,
    n_in, cot_in, n2_in, a_in, b_in, qlin_in, klin_in, qrot_in, kv_in, o_in, mid_in, cosine, sine,
    result, tokens_grad, attn_gain_grad, mlp_gain_grad, query_gain_grad, key_gain_grad, qkv_grad, out_grad, gate_grad, up_grad, down_grad,
    box_q0, box_q1, box_k0, box_k1, box_o0, box_o1, box_g0, box_g1, box_u0, box_u1, box_d0, box_d1,
    n2, cota, a, b, da, h, dg, du, qlin, klin, qrot, kv, o, mid, dmid, cos, sin, dqkv, d_o, acc, acc_out, acc_in,
    sib_out, held, arrive, held2, arrive2,
    part_q, left_q, right_q, part_k, left_k, right_k, part_o, left_o, right_o, part_g, left_g, right_g, part_u, left_u, right_u,
    part_d, left_d, right_d, gain8, gainx, gainz, gacc,
    load, r1_send, r1_recv, r2_send, r2_recv, r3_send, r3_recv, da_send, da_recv,
    q_send, q_recv, k_send, k_recv, o_send, o_recv, g_send, g_recv, u_send, u_recv, d_send, d_recv, stage_load, swap_sem, v_send, v_recv,
):
    me = Place()
    barrier, count = greet(me, True)
    waits = {}

    def fetch(name, src, dst):
        waits[name] = pltpu.make_async_copy(src, dst, load.at[len(waits)])
        waits[name].start()

    fetch("n2", n2_in, n2)
    for j in range(3):
        for part in range(3):
            cols = pl.ds(part * 768 + j * 256, 256)
            fetch("b%d%d" % (j, part), b_in.at[:, cols], b.at[:, cols])
        if j == 0:
            fetch("cot", cot_in, cota)
    fetch("mid", mid_in, mid)
    fetch("a", a_in, a)
    fetch("o", o_in, o)
    fetch("qrot", qrot_in, qrot)
    fetch("kv", kv_in, kv)
    fetch("qlin", qlin_in, qlin)
    fetch("klin", klin_in, klin)
    fetch("cos", cosine.at[me.xhi], cos)
    fetch("sin", sine.at[me.xhi], sin)
    waits["n2"].wait()

    def hidden(j, i):
        rows = rows_at(i * 512, 512)
        cols = slice(j * 256, j * 256 + 256)
        gate = dot(n2[rows, :], b[:, cols])
        up = dot(n2[rows, :], b[:, 768 + j * 256:1024 + j * 256])
        d_hidden = dot(cota[rows, :], b[:, 1536 + j * 256:1792 + j * 256])
        sg = jax.nn.sigmoid(gate)
        active = gate * sg
        h[rows, cols] = (active * up).astype(BF)
        dg[rows, cols] = (d_hidden * up * sg * (1.0 + gate * (1.0 - sg))).astype(BF)
        du[rows, cols] = (d_hidden * active).astype(BF)

    for j in range(3):
        for part in range(3):
            waits["b%d%d" % (j, part)].wait()
        if j == 0:
            waits["cot"].wait()
        lax.fori_loop(0, 2, lambda i, _, j=j: (hidden(j, i), 0)[1], 0)
    pl.semaphore_wait(barrier, count)
    sum_n2 = ReduceRows(me, sib_out, held, arrive, r1_send, r1_recv)
    sum_result = ReduceRows(me, sib_out, held2, arrive2, r2_send, r2_recv)
    sum_n = ReduceRows(me, sib_out, held, arrive, r3_send, r3_recv)

    def back_n2(row, j):
        rows, model = rows_at(row, 256), rows_at(j * 512, 512)
        return dot_t(dg[rows, :], b[model, 0:768]) + dot_t(du[rows, :], b[model, 768:1536])

    def down(row, j):
        return dot_t(h[rows_at(row, 256), :], b[rows_at(j * 512, 512), 1536:2304])

    sum_n2.other(back_n2)
    sum_n2.mine(back_n2)
    def stages(first, second):
        quarter = [(buf, r) for buf in (dg, du) for r in range(4)]
        return ([buf.at[pl.ds(r * 256, 256), pl.ds(0, first)] for buf, r in quarter[:6]],
                [buf.at[pl.ds(r * 512, 512), pl.ds(512, second)] for buf in (dg, du) for r in (0, 1)])

    def reduction(grad, col, widths, boxes, sums, sems, fold=0):
        return ReduceWeights(me, grad, col, widths, boxes, stages(*widths), *sums, *sems, stage_load, fold)

    red_g = reduction(b, 0, WIDE, (box_g0, box_g1), (part_g, left_g, right_g), (g_send, g_recv))
    red_u = reduction(b, 768, WIDE, (box_u0, box_u1), (part_u, left_u, right_u), (u_send, u_recv))
    red_d = reduction(b, 1536, WIDE, (box_d0, box_d1), (part_d, left_d, right_d), (d_send, d_recv))
    red_o = reduction(a, 512, NARROW, (box_o0, box_o1), (part_o, left_o, right_o), (o_send, o_recv))
    red_q = reduction(n2, 0, NARROW, (box_q0, box_q1), (part_q, left_q, right_q), (q_send, q_recv), 256)
    red_k = reduction(a, 256, NARROW, (box_k0, box_k1), (part_k, left_k, right_k), (k_send, k_recv))

    def weight_grad(red, left, right, unroll=False):
        def step(i, _):
            red.store(i, dot_rows(left[:, rows_at(i * 256, 256)], right[...]))
            return 0

        lax.fori_loop(0, 8, step, 0, unroll=unroll)
        red.first()

    weight_grad(red_g, n2, dg)
    sum_n2.relay()
    weight_grad(red_u, n2, du)
    waits["mid"].wait()
    sum_n2.wait()
    rows_da = GatherRows(me, da, da_send, da_recv)
    own = (me.c * 4 + me.y) * BLOCK

    def back_two(i, total):
        rows = pl.ds(pl.multiple_of(i * 16, 16), 16)
        grad, gain = back_norm(mid[rows, :], mlp_gain[...], sum_n2.total(i * 16))
        grad = grad + cot[rows, :].astype(F32)
        dmid[rows, :] = grad
        da[pl.ds(pl.multiple_of(own + i * 16, 16), 16), :] = grad.astype(BF)
        return total + gain

    mlp_part = lax.fori_loop(0, 8, back_two, jnp.zeros((1, WIDTH), F32))
    rows_da.start()
    slot = me.c * 4 + me.y

    def spread(value, col):
        for i in range(8):
            gainx[me.x, i:i + 1, col:col + 256] = value[:, i * 256:(i + 1) * 256]

    gainx[me.x] = jnp.zeros((8, 640), F32)
    spread(mlp_part, 256)
    gacc[...] = jnp.zeros_like(gacc)
    sum_n2.finish()
    sum_result.other(down)
    sum_result.mine(down, send=False)
    rows_da.relay()
    red_g.relay()
    weight_grad(red_d, cota, h)
    n_load = pltpu.make_async_copy(n_in, cota, load.at[20])
    n_load.start()
    for name in ("a", "o", "qrot", "kv", "qlin", "klin", "cos", "sin"):
        waits[name].wait()
    red_u.relay()
    rows_da.finish()

    def back_o(i, _):
        rows = rows_at(i * 512, 512)
        d_o[rows, :] = dot(da[rows, :], a[:, 512:768]).astype(BF)
        return 0

    lax.fori_loop(0, 2, back_o, 0)
    sum_result.send_all()

    swaps = []
    q_gain = jnp.zeros((1, HEAD), F32)
    for turn_ in (0, 1):
        s = 1 - me.c if turn_ == 0 else me.c
        flat = kv[0, s].reshape(1024, 128).T
        key = lax.broadcasted_iota(jnp.int32, (256, 256), 0)
        query = lax.rem(lax.broadcasted_iota(jnp.int32, (256, 256), 1), 128)
        keep = jnp.logical_or(key <= query, key >= 256 - 128 * me.xhi)
        dqs = {}
        for pair in ((3, 0), (2, 1)):
            sizes = [(block + 1) * 256 for block in pair]
            qs = [qrot[rows_at(s * 1024 + block * 256, 256), :] for block in pair]
            gs = []
            for block in pair:
                rows = rows_at(s * 512 + block * 128, 128)
                gs.append(jnp.concatenate([d_o[rows, 0:128], d_o[rows, 128:256]], axis=0))
            ks = [kv[0, s, 0:block + 1].reshape(size, 128) for block, size in zip(pair, sizes)]
            vs = [kv[1, s, 0:block + 1].reshape(size, 128) for block, size in zip(pair, sizes)]
            ps = [mask_last(jnp.exp2(dot_t(k, q) * SCORE2), keep, 0) for k, q in zip(ks, qs)]
            dps = [dot_t(v, g) for v, g in zip(vs, gs)]
            ps = [p * (1.0 / jnp.sum(p, axis=0, keepdims=True)) for p in ps]
            dss = [(p * (dp - jnp.sum(dp * p, axis=0, keepdims=True))).astype(BF) for p, dp in zip(ps, dps)]
            for block, size, ds in zip(pair, sizes, dss):
                dqs[block] = (dot(flat[:, :size], ds) * SCORE).T
            dks = [dot(ds, q) * SCORE for ds, q in zip(dss, qs)]
            dvs = [dot(p.astype(BF), g) for p, g in zip(ps, gs)]
            for block, dk, dv in zip(pair, dks, dvs):
                for i, value in enumerate((dk, dv)):
                    value = value.reshape(block + 1, 2, 128, 128)
                    if block == 3:
                        acc[i, s] = value
                    else:
                        acc[i, s, 0:block + 1] += value
        rows = rows_at(s * 512, 512)
        for head in (0, 1):
            dq = jnp.concatenate([dqs[block][head * 128:(head + 1) * 128] for block in range(4)], axis=0)
            up = turn(dq, cos[...], -sin[...])
            grad, gain = back_norm(qlin[rows, head * 128:(head + 1) * 128], query_gain[...], up)
            dqkv[rows, head * 128:(head + 1) * 128] = grad.astype(BF)
            q_gain = q_gain + gain
        for i in (0, 1):
            acc_out[turn_, i] = acc[i, s, :, 1].astype(BF)
        swap = remote(acc_out.at[turn_], acc_in.at[turn_], swap_sem.at[turn_], swap_sem.at[2 + turn_],
                      me.at(x=ring(me.x, 2)))
        swap.start()
        swaps.append(swap)
        if turn_ == 0:
            sum_result.relay()
            red_g.second()
            red_d.relay()
    weight_grad(red_o, da, o, True)
    n_load.wait()
    weight_grad(red_q, cota, dqkv.at[:, pl.ds(0, 256)], True)
    red_u.second()

    k_gain = jnp.zeros((1, HEAD), F32)

    def back_n(row, j):
        rows, model = rows_at(row, 256), rows_at(j * 512, 512)
        term = dot_t(dqkv[rows, 0:256], a[model, 0:256]) + dot_t(dqkv[rows, 256:512], a[model, 256:512])
        cols = rows_at(j * 512, 512)
        gacc[:, cols] += jnp.sum(term * cota[rows, cols].astype(F32), axis=0, keepdims=True)
        return term

    for turn_ in (0, 1):
        s = 1 - me.c if turn_ == 0 else me.c
        rows = rows_at(s * 512, 512)
        swaps[turn_].wait()
        dk = (acc[0, s, :, 0] + acc_in[turn_, 0].astype(F32)).reshape(512, 128)
        dv = (acc[1, s, :, 0] + acc_in[turn_, 1].astype(F32)).reshape(512, 128)
        grad, gain = back_norm(klin[rows, :], key_gain[...], turn(dk, cos[...], -sin[...]))
        k_gain = k_gain + gain
        dqkv[rows, 256:384] = grad.astype(BF)
        dqkv[rows, 384:512] = dv.astype(BF)
        if turn_ == 0:
            sum_result.finish()
            sum_n.other(back_n)
            red_d.second()
            red_o.relay()
            red_q.relay()
        else:
            sum_n.mine(back_n)
    spread(gacc[...] / attn_gain[...], 0)
    gainx[me.x, 0:1, 512:640] = q_gain
    gainx[me.x, 1:2, 512:640] = k_gain
    for k in (1, 2, 3):
        remote(gainx.at[me.x], gainx.at[me.x], v_send.at[6 + k], v_recv.at[8 + me.x], me.at(x=ring(me.x, k))).start()
    weight_grad(red_k, cota, dqkv.at[:, pl.ds(256, 256)])
    sum_n.relay()
    red_o.second()
    for i in range(4):
        @pl.when(me.x != i)
        def _():
            settle(gainx.at[i], v_recv.at[8 + i])
    gainz[me.z] = gainx[0] + gainx[1] + gainx[2] + gainx[3]
    for k in (1, 2, 3):
        remote(gainz.at[me.z], gainz.at[me.z], v_send.at[9 + k], v_recv.at[12 + me.z], me.at(z=ring(me.z, k))).start()
    red_k.relay()
    red_q.second()

    def put(ref, col=0):
        def store(rows, left, right):
            middle = col + left.shape[1]
            ref[rows, col:middle] = left
            ref[rows, middle:middle + right.shape[1]] = right
        return store

    red_g.third(put(gate_grad))
    red_u.third(put(up_grad))
    for i in range(4):
        @pl.when(me.z != i)
        def _():
            settle(gainz.at[i], v_recv.at[12 + i])
    gain8[slot] = gainz[0] + gainz[1] + gainz[2] + gainz[3]
    peers = [(me.y, 1 - me.c)] + [(ring(me.y, k), c) for k in (1, 2, 3) for c in (0, 1)]
    for i, (y, c) in enumerate(peers):
        remote(gain8.at[slot], gain8.at[slot], v_send.at[i], v_recv.at[slot], me.at(y=y, c=c)).start()
    red_d.third(put(down_grad))
    sum_result.wait()

    def finish_result(i, _):
        rows = pl.ds(pl.multiple_of(i * 16, 16), 16)
        result[rows, :] = (mid[rows, :] + sum_result.total(i * 16)).astype(BF)
        return 0

    lax.fori_loop(0, 8, finish_result, 0)
    red_k.second()
    red_o.third(put(out_grad))
    sum_n.wait()

    def back_one(i, _):
        rows = pl.ds(pl.multiple_of(i * 16, 16), 16)
        grad, _ = back_norm(tokens[rows, :].astype(F32), attn_gain[...], sum_n.total(i * 16))
        tokens_grad[rows, :] = dmid[rows, :] + grad
        return 0

    lax.fori_loop(0, 8, back_one, 0)
    for i in range(8):
        @pl.when(slot != i)
        def _():
            settle(gain8.at[i], v_recv.at[i])
    total = gain8[0]
    for i in range(1, 8):
        total = total + gain8[i]
    for i in range(8):
        cols = slice(i * 256, i * 256 + 256)
        attn_gain_grad[:, cols] = total[i:i + 1, 0:256]
        mlp_gain_grad[:, cols] = total[i:i + 1, 256:512]
    query_gain_grad[...] = total[0:1, 512:640]
    key_gain_grad[...] = total[1:2, 512:640]
    red_q.third(put(qkv_grad))
    red_k.third(put(qkv_grad, 256))
    for i in range(13):
        settle(gain8.at[0], v_send.at[i])
    sum_n.finish()
    for red in (red_g, red_u, red_d, red_o, red_q, red_k):
        red.finish()


def backward(tokens, cot, gains, saved, cos, sin):
    n, cota, n2, a, b, qlin, klin, qrot, kv, o, mid = saved
    args = (tokens, cot) + gains + saved + (cos, sin)
    vmem = pl.BlockSpec(memory_space=pltpu.VMEM)
    hbm = pl.BlockSpec(memory_space=pl.ANY)
    outs = [((BLOCK, WIDTH), BF), ((BLOCK, WIDTH), F32), ((1, WIDTH), F32), ((1, WIDTH), F32)]
    outs += [((1, HEAD), F32), ((1, HEAD), F32), ((BLOCK, 512), F32), ((BLOCK, 256), F32)]
    outs += [((BLOCK, 768), F32)] * 3
    widths = (NARROW, NARROW, NARROW, WIDE, WIDE, WIDE)
    boxes = [box for w in widths for box in (((6, 256, w[0]), BF), ((4, 512, w[1]), BF))]
    scratch = [
        ((ROWS, WIDTH), BF), ((ROWS, WIDTH), BF), ((WIDTH, A_COLS), BF), ((WIDTH, B_COLS), BF), ((ROWS, WIDTH), BF),
        ((ROWS, 768), BF), ((ROWS, 768), BF), ((ROWS, 768), BF), ((ROWS, 256), F32), ((ROWS, 128), F32),
        ((2 * ROWS, 128), BF), (KV_SHAPE, BF), ((ROWS, 256), BF), ((BLOCK, WIDTH), F32), ((BLOCK, WIDTH), F32),
        ((512, 128), F32), ((512, 128), F32), ((ROWS, 512), BF), ((ROWS, 256), BF), (KV_SHAPE, F32),
        ((2, 2, 4, 128, 128), BF), ((2, 2, 4, 128, 128), BF),
        ((512, WIDTH), BF), ((512, WIDTH), BF), ((6, 64, WIDTH), BF), ((512, WIDTH), BF), ((6, 64, WIDTH), BF),
    ]
    for w in widths:
        scratch += [((512, w[1]), BF), ((4, BLOCK, w[0]), BF), ((3, BLOCK, w[1]), BF)]
    scratch += [((8, 8, 640), F32), ((4, 8, 640), F32), ((4, 8, 640), F32), ((1, WIDTH), F32)]
    scratch = [pltpu.VMEM(s, d) for s, d in scratch]
    dma = pltpu.SemaphoreType.DMA
    scratch += [dma((21,))] + [dma((8,))] * 6 + [dma((GatherRows.sems,))] * 2 + [dma((ReduceWeights.sems,))] * 12 + [dma((10,)), dma((4,))]
    scratch += [dma((13,)), dma((16,))]
    got = pl.pallas_call(
        backward_kernel,
        out_shape=[jax.ShapeDtypeStruct(s, d) for s, d in outs + boxes],
        in_specs=[vmem] * 6 + [hbm] * 13,
        out_specs=[vmem] * len(outs) + [hbm] * len(boxes),
        scratch_shapes=scratch,
        compiler_params=pltpu.CompilerParams(
            collective_id=2, has_side_effects=True, vmem_limit_bytes=VMEM_BYTES),
        name="backward_part",
    )(*args)
    return got[:len(outs)]


def finish_kernel(*refs):
    parts, outs, sem = refs[:11], refs[11:24], refs[24]
    qkv = parts[6]
    sources = parts[:6] + tuple(qkv.at[:, pl.ds(*cols)] for cols in ((0, 256), (256, 128), (384, 128))) + parts[7:]
    copies = [pltpu.make_async_copy(src, dst, sem.at[i]) for i, (src, dst) in enumerate(zip(sources, outs))]
    for copy in copies:
        copy.start()
    for copy in copies:
        copy.wait()


def finish(parts):
    shapes = [((BLOCK, WIDTH), BF), ((BLOCK, WIDTH), F32), ((1, WIDTH), F32), ((1, WIDTH), F32), ((1, HEAD), F32)]
    shapes += [((1, HEAD), F32), ((BLOCK, 256), F32), ((BLOCK, 128), F32), ((BLOCK, 128), F32), ((BLOCK, 256), F32)]
    shapes += [((BLOCK, 768), F32)] * 3
    return pl.pallas_call(
        finish_kernel,
        out_shape=[jax.ShapeDtypeStruct(s, d) for s, d in shapes],
        in_specs=[pl.BlockSpec(memory_space=pl.ANY)] * len(parts),
        out_specs=[pl.BlockSpec(memory_space=pltpu.VMEM)] * len(shapes),
        scratch_shapes=[pltpu.SemaphoreType.DMA((13,))],
        compiler_params=pltpu.CompilerParams(vmem_limit_bytes=VMEM_BYTES),
        name="finish_part",
    )(*parts)


def local(tokens, cotangent, attn_gain, mlp_gain, query_gain, key_gain, *weights):
    cos, sin = rope_tables()
    gains = (attn_gain[None], mlp_gain[None], query_gain[None], key_gain[None])
    saved = forward(tokens, cotangent, *gains, *weights, cos, sin)
    outs = finish(backward(tokens, cotangent, gains, tuple(saved), cos, sin))
    return tuple(outs[:2]) + tuple(g[0] for g in outs[2:6]) + tuple(outs[6:])


def solution(mesh):
    rows, plane = P(("dp", "tensor"), None), P("dp", "tensor")
    return jax.shard_map(
        local,
        mesh=mesh,
        in_specs=(rows, rows, P(), P(), P(), P()) + (plane,) * 7,
        out_specs=(rows, rows, P(), P(), P(), P()) + (plane,) * 7,
        check_vma=False,
    )
```

```python
import functools

import numpy as np
import jax
import jax.numpy as jnp
from jax import lax
from jax.experimental import pallas as pl
from jax.experimental.pallas import tpu as pltpu
from jax.sharding import PartitionSpec as P

EPS = 1e-06
ROPE_BASE = 1000000.0
MESH = pl.DeviceIdType.MESH
BF = jnp.bfloat16
F32 = jnp.float32
HEAD = 128
WIDTH = 2048
BLOCK = 128
ROWS = 1024
A_COLS = 768
B_COLS = 2304
B_CUT = 1280
SCORE = HEAD ** -0.5
KV_SHAPE = (2, 2, 4, 2, 128, 128)
SCORE2 = HEAD ** -0.5 * 1.4426950408889634
VMEM_BYTES = 63 * 2**20


class Place:
    def __init__(self):
        dp = lax.axis_index("dp")
        tensor = lax.axis_index("tensor")
        self.dp = dp
        self.xlo = lax.div(dp, 8)
        self.z = lax.rem(lax.div(dp, 2), 4)
        self.c = lax.rem(dp, 2)
        self.y = lax.div(tensor, 2)
        self.xhi = lax.rem(tensor, 2)
        self.x = self.xhi * 2 + self.xlo

    def at(self, x=None, y=None, z=None, c=None):
        x = self.x if x is None else x
        y = self.y if y is None else y
        z = self.z if z is None else z
        c = self.c if c is None else c
        return (lax.rem(x, 2) * 8 + z * 2 + c, y * 2 + lax.div(x, 2))

    def sibling(self):
        return self.at(c=1 - self.c)


def ring(v, k):
    return lax.rem(v + k, 4)


def remote(src, dst, send_sem, recv_sem, target):
    return pltpu.make_async_remote_copy(
        src_ref=src, dst_ref=dst, send_sem=send_sem, recv_sem=recv_sem,
        device_id=target, device_id_type=MESH,
    )


def settle(ref, sem):
    pltpu.make_async_copy(ref, ref, sem).wait()


def rows_at(start, size):
    return pl.ds(pl.multiple_of(start, 128), size)


def greet(me):
    barrier = pltpu.get_barrier_semaphore()
    others = [me.sibling()]
    for k in (1, 2, 3):
        others.append(me.at(y=ring(me.y, k)))
        others.append(me.at(y=ring(me.y, k), c=1 - me.c))
        for c in (0, 1):
            others.append(me.at(x=ring(me.x, k), c=c))
            others.append(me.at(z=ring(me.z, k), c=c))
    for other in others:
        pl.semaphore_signal(barrier, inc=1, device_id=other, device_id_type=MESH)
    return barrier, len(others)


class GatherRows:
    sems = 13

    def __init__(self, me, buf, send, recv):
        self.me, self.buf, self.send, self.recv = me, buf, send, recv

    def piece(self, c, y, half):
        return self.buf.at[pl.ds(pl.multiple_of((c * 4 + y) * BLOCK + half * 64, 64), 64)]

    def go(self, y, half, i, target):
        ref = self.piece(self.me.c, y, half)
        remote(ref, ref, self.send.at[i], self.recv.at[i], target).start()

    def start(self):
        me = self.me
        up, down = me.at(y=ring(me.y, 1)), me.at(y=ring(me.y, 3))
        self.go(me.y, 0, 0, up)
        self.go(me.y, 1, 2, down)
        own = self.buf.at[rows_at((me.c * 4 + me.y) * BLOCK, BLOCK)]
        remote(own, own, self.send.at[6], self.recv.at[6], me.sibling()).start()

    def heard(self, i, k, half):
        me = self.me
        y = ring(me.y, 4 - k)
        settle(self.piece(me.c, y, half), self.recv.at[i])
        self.go(y, half, 7 + i, me.sibling())
        return y

    def relay(self):
        me = self.me
        up, down = me.at(y=ring(me.y, 1)), me.at(y=ring(me.y, 3))
        half = self.piece(me.c, me.y, 0)
        settle(half, self.send.at[0])
        self.go(me.y, 1, 1, up)
        settle(half, self.send.at[2])
        self.go(me.y, 0, 3, down)
        y = self.heard(0, 1, 0)
        self.go(y, 0, 4, up)
        y = self.heard(2, 3, 1)
        self.go(y, 1, 5, down)

    def finish(self):
        me = self.me
        self.heard(1, 1, 1)
        self.heard(3, 3, 0)
        self.heard(4, 2, 0)
        self.heard(5, 2, 1)
        half = self.piece(me.c, me.y, 0)
        own = self.buf.at[rows_at((me.c * 4 + me.y) * BLOCK, BLOCK)]
        for i in (1, 3, 4, 5, 6, 7, 8, 9, 10, 11, 12):
            settle(own if i == 6 else half, self.send.at[i])
        for i in range(6, 13):
            settle(own if i == 6 else half, self.recv.at[i])


class ReduceRows:
    def __init__(self, me, sib_out, held, arrive, send, recv):
        self.me = me
        self.sib_out, self.held, self.arrive = sib_out, held, arrive
        self.send, self.recv = send, recv
        first = 1 - lax.div(me.y, 2)
        self.halves = (first, 1 - first)

    def other(self, tile):
        me = self.me
        for p, half in enumerate(self.halves):
            rows = rows_at(half * 256, 256)

            def step(j, _):
                cols = rows_at(j * 512, 512)
                self.sib_out[rows, cols] = tile((1 - me.c) * 512 + half * 256, j).astype(BF)
                return 0

            lax.fori_loop(0, 4, step, 0, unroll=True)
            remote(self.sib_out.at[rows], self.held.at[rows], self.send.at[6 + p], self.recv.at[6 + p],
                   me.sibling()).start()

    def piece(self, k, half):
        return pl.ds(pl.multiple_of(ring(self.me.y, k) * BLOCK + half * 64, 64), 64)

    def go(self, i, k, half, step):
        remote(self.held.at[self.piece(k, half)], self.arrive.at[i], self.send.at[i], self.recv.at[i],
               self.me.at(y=ring(self.me.y, step))).start()

    def mine(self, tile, send=True):
        me = self.me
        for p, half in enumerate(self.halves):
            rows = rows_at(half * 256, 256)
            settle(self.held.at[rows], self.recv.at[6 + p])

            def step(j, _):
                cols = rows_at(j * 512, 512)
                total = tile(me.c * 512 + half * 256, j) + self.held[rows, cols].astype(F32)
                self.held[rows, cols] = total.astype(BF)
                return 0

            lax.fori_loop(0, 4, step, 0, unroll=True)
            if not send:
                continue
            even = lax.rem(me.y, 2) == 0
            if p == 0:
                self.go(0, 2, 0, 1)
                self.go(1, 2, 1, 3)
            pl.when(even if p == 0 else jnp.logical_not(even))(lambda: self.go(3, 3, 0, 3))
            pl.when(jnp.logical_not(even) if p == 0 else even)(lambda: self.go(2, 1, 1, 1))

    def send_all(self):
        self.go(0, 2, 0, 1)
        self.go(1, 2, 1, 3)
        self.go(2, 1, 1, 1)
        self.go(3, 3, 0, 3)

    def relay(self):
        for i, k, half, step in ((0, 1, 0, 1), (1, 3, 1, 3)):
            settle(self.arrive.at[i], self.recv.at[i])
            rows = self.piece(k, half)
            self.held[rows, :] = (self.held[rows, :].astype(F32) + self.arrive[i].astype(F32)).astype(BF)
            self.go(4 + i, k, half, step)

    def wait(self):
        for i in range(2, 6):
            settle(self.arrive.at[i], self.recv.at[i])

    def total(self, r):
        half = lax.div(r, 64)
        rows = pl.ds(pl.multiple_of(r - half * 64, 16), 16)
        total = self.held[pl.ds(pl.multiple_of(self.me.y * BLOCK + r, 16), 16), :].astype(F32)
        return total + self.arrive[3 - half, rows, :].astype(F32) + self.arrive[4 + half, rows, :].astype(F32)

    def finish(self):
        for i in range(6):
            settle(self.arrive.at[i], self.send.at[i])
        for p in (0, 1):
            settle(self.sib_out.at[rows_at(0, 256)], self.send.at[6 + p])


class GatherWeights:
    sems = 23

    def __init__(self, me, shard, full, col, cut, width, send, recv):
        self.me, self.shard, self.full = me, shard, full
        self.cols = (pl.ds(col, cut), pl.ds(col + cut, width - cut))
        self.from_cols = (pl.ds(0, cut), pl.ds(cut, width - cut))
        self.send, self.recv = send, recv
        self.ways = (0, 1) if cut < width else (0,)

    def slot(self, way, dp):
        return self.full.at[rows_at(dp * BLOCK, BLOCK), self.cols[way]]

    def first(self, way):
        me = self.me
        home = me.xhi
        src = self.shard.at[:, self.from_cols[way]]
        dst = self.slot(way, me.dp)
        inbox = self.recv.at[(me.xlo * 2 + me.c) if way == 0 else (10 + me.z * 2 + me.c)]
        base = 0 if way == 0 else 10
        for k in (1, 3, 2):
            target = me.at(x=ring(me.x, k), c=home) if way == 0 else me.at(z=ring(me.z, k), c=home)
            remote(src, dst, self.send.at[base + k], inbox, target).start()

        @pl.when(me.c == home)
        def _():
            pltpu.make_async_copy(src, dst, inbox).start()

        @pl.when(me.c != home)
        def _():
            remote(src, dst, self.send.at[base], inbox, me.sibling()).start()

    def second_z(self):
        me = self.me
        for xlo in (0, 1):
            for c in (0, 1):
                settle(self.slot(0, xlo * 8 + me.z * 2 + c), self.recv.at[xlo * 2 + c])
        self.go(0, me.z, 4, 1)
        self.go(1, me.z, 6, 3)
        self.go(1, me.z, 5, 1)
        self.go(0, me.z, 7, 3)

    def go(self, xlo, z, i, step):
        ref = self.pair(xlo, z)
        remote(ref, ref, self.send.at[i], self.recv.at[i], self.me.at(z=ring(self.me.z, step))).start()

    def relay(self):
        me = self.me
        for i, xlo, step in ((4, 0, 1), (6, 1, 3)):
            z = ring(me.z, 4 - step)
            settle(self.pair(xlo, z), self.recv.at[i])
            self.go(xlo, z, 8 + xlo, step)

    def second_x(self):
        me = self.me
        if 1 not in self.ways:
            return

        @pl.when(me.c == me.xhi)
        def _():
            for z in range(4):
                for c in (0, 1):
                    settle(self.slot(1, me.xlo * 8 + z * 2 + c), self.recv.at[10 + z * 2 + c])
            for i, (part, step) in enumerate(((0, 1), (1, 3), (1, 1), (0, 3))):
                self.go_x(me.xlo, part, 18 + i, ring(me.x, step))

    def go_x(self, xlo, part, i, x):
        ref = self.quarter(xlo, part)
        remote(ref, ref, self.send.at[i], self.recv.at[18 + xlo * 2 + part], self.me.at(x=x)).start()

    def near_x(self):
        me = self.me
        below = lax.div(ring(me.x, 3), 2)
        up = 1 - (below + me.c - 2 * below * me.c)
        return up, lax.rem(ring(me.x, 1 + 2 * up), 2), 1 - up

    def relay_x(self):
        if 1 not in self.ways:
            return
        up, xlo, part = self.near_x()
        settle(self.quarter(0, 0), self.recv.at[18 + xlo * 2 + part])
        self.go_x(xlo, part, 22, ring(self.me.x, 3 - 2 * up))

    def pair(self, xlo, z):
        return self.full.at[rows_at(xlo * 1024 + z * 256, 256), self.cols[0]]

    def quarter(self, xlo, part):
        return self.full.at[rows_at(xlo * 1024 + part * 512, 512), self.cols[1]]

    def arrived(self):
        me = self.me
        for i in (5, 7, 8, 9):
            settle(self.pair(0, me.z), self.recv.at[i])
        if 1 not in self.ways:
            return
        _, near, near_part = self.near_x()
        for xlo in (0, 1):
            for part in (0, 1):
                here = jnp.logical_and(me.c == me.xhi, me.xlo == xlo)
                done = jnp.logical_and(near == xlo, near_part == part)

                @pl.when(jnp.logical_not(jnp.logical_or(here, done)))
                def _():
                    settle(self.quarter(0, 0), self.recv.at[18 + xlo * 2 + part])

    def finish(self):
        me = self.me
        for way in self.ways:
            src = self.shard.at[:, self.from_cols[way]]
            base = 0 if way == 0 else 10
            for k in (1, 2, 3):
                settle(src, self.send.at[base + k])

            @pl.when(me.c != me.xhi)
            def _():
                settle(src, self.send.at[base])
        for i in range(4, 10):
            settle(self.pair(0, me.z), self.send.at[i])

        if 1 not in self.ways:
            return

        @pl.when(me.c == me.xhi)
        def _():
            for i in range(18, 22):
                settle(self.quarter(0, 0), self.send.at[i])

        settle(self.quarter(0, 0), self.send.at[22])


def dot(left, right):
    return jnp.dot(left, right, preferred_element_type=F32)


def dot_t(left, right):
    return lax.dot_general(left, right, (((1,), (1,)), ((), ())), preferred_element_type=F32)


def inverse_of(values):
    return lax.rsqrt(jnp.mean(values * values, axis=-1, keepdims=True) + EPS)


def turn(values, cosine, sine):
    return values * cosine + pltpu.roll(values, 64, 1) * sine


def mask_last(values, keep, axis):
    size = values.shape[axis]
    last = jnp.where(keep, lax.slice_in_dim(values, size - 256, size, axis=axis), 0.0)
    if size == 256:
        return last
    return jnp.concatenate([lax.slice_in_dim(values, 0, size - 256, axis=axis), last], axis=axis)


def rope_tables():
    frequency = ROPE_BASE ** (-2.0 * np.arange(64, dtype=np.float64) / HEAD)
    angle = np.arange(1024, dtype=np.float64)[:, None] * frequency[None, :]
    cos = np.concatenate([np.cos(angle), np.cos(angle)], axis=1).astype(np.float32)
    sin = np.concatenate([-np.sin(angle), np.sin(angle)], axis=1).astype(np.float32)
    pick = lambda t: t.reshape(4, 2, 128, 128).transpose(1, 0, 2, 3).reshape(2, 512, 128)
    return pick(cos), pick(sin)


WIDE, NARROW = (512, 256), (128, 128)


class ReduceWeights:
    sems = 17

    def __init__(self, me, grad, first_col, widths, inbox, stage, part, left, right, send, recv, load, fold=0):
        self.me, self.grad, self.widths, self.fold = me, grad, widths, fold
        self.first_cols = (first_col, first_col + widths[0])
        self.inbox, self.stage, self.part, self.left, self.right = inbox, stage, part, left, right
        self.send, self.recv, self.load = send, recv, load

    def place(self, way, start, size):
        col = self.first_cols[way]
        if self.fold:
            high = lax.div(start, 1024)
            start = start - high * 1024
            col = pl.multiple_of(col + high * self.fold, 128)
        return pl.ds(pl.multiple_of(start, 32), size), pl.ds(col, self.widths[way])

    def store(self, i, value):
        xlo, z = lax.div(i, 4), lax.rem(i, 4)
        value = value.astype(BF)
        self.grad[self.place(0, z * 512 + xlo * 256, 256)] = value[:, :self.widths[0]]
        for c in (0, 1):
            self.grad[self.place(1, (xlo * 2 + c) * 512 + z * 128, 128)] = value[
                c * 128:(c + 1) * 128, self.widths[0]:]

    def piece(self, k, half):
        return self.grad.at[self.place(0, ring(self.me.z, k) * 512 + half * 256, 256)]

    def go(self, i, k, half, step):
        remote(self.piece(k, half), self.inbox[0].at[i], self.send.at[i], self.recv.at[i],
               self.me.at(z=ring(self.me.z, step))).start()

    def over_x(self, sources, dst, base):
        me = self.me
        for xlo in (0, 1):
            for c in (0, 1):
                src = sources(xlo, c)
                x = me.c * 2 + xlo
                self_too = jnp.logical_and(me.x == x, me.c == c)

                @pl.when(self_too)
                def _():
                    pltpu.make_async_copy(src, dst, self.recv.at[base + me.x]).start()

                @pl.when(jnp.logical_not(self_too))
                def _():
                    remote(src, dst, self.send.at[base + xlo * 2 + c], self.recv.at[base + me.x],
                           me.at(x=x, c=c)).start()

    def over_x_sent(self, ref, base):
        me = self.me
        for xlo in (0, 1):
            for c in (0, 1):
                @pl.when(jnp.logical_or(me.x != me.c * 2 + xlo, me.c != c))
                def _():
                    settle(ref, self.send.at[base + xlo * 2 + c])

    def first(self):
        self.go(0, 2, 0, 1)
        self.go(1, 2, 1, 3)
        self.go(2, 1, 1, 1)
        self.go(3, 3, 0, 3)
        me = self.me
        for xlo in (0, 1):
            x = me.c * 2 + xlo
            away = ring(me.x + 4 - x, 0)
            for c in (0, 1):
                there = me.at(x=x, c=c)

                @pl.when(jnp.logical_and(away == 0, me.c == c))
                def _():
                    pltpu.make_async_copy(self.share(xlo, c), self.inbox[1].at[0], self.recv.at[6]).start()

                @pl.when(jnp.logical_and(away == 0, me.c != c))
                def _():
                    self.go_x(xlo, c, 0, there)

                @pl.when(away == 2)
                def _():
                    self.go_x(xlo, c, 3, me.at(x=ring(me.x, 3 if c == 0 else 1)))

                @pl.when(away == (3 if c == 0 else 1))
                def _():
                    self.go_x(xlo, c, 2 if c == 0 else 1, there)

    def share(self, xlo, c):
        return self.grad.at[self.place(1, jnp.int32(0) + (xlo * 2 + c) * 512, 512)]

    def go_x(self, xlo, c, slot, target):
        remote(self.share(xlo, c), self.inbox[1].at[slot], self.send.at[6 + xlo * 2 + c], self.recv.at[6 + slot],
               target).start()

    def relay_x(self):
        me = self.me
        away = ring(me.x + 4 - me.c * 2, 0)
        xlo = 1 - lax.rem(away, 2)
        c = lax.div(ring(away + 4 - xlo, 0), 2)
        self.fetched(9)

        def add(r, _):
            here = self.place(1, (xlo * 2 + c) * 512 + r * 64, 64)
            more = self.stage[1][3][pl.ds(pl.multiple_of(r * 64, 64), 64), :]
            self.grad[here] = (self.grad[here].astype(F32) + more.astype(F32)).astype(BF)
            return 0

        lax.fori_loop(0, 8, add, 0)
        self.go_x(xlo, c, 1 + c, me.at(x=me.c * 2 + xlo, c=c))

    def fetch(self, i):
        way, slot = (0, i) if i < 6 else (1, i - 6)
        settle(self.inbox[way].at[slot], self.recv.at[i])
        pltpu.make_async_copy(self.inbox[way].at[slot], self.stage[way][slot], self.load.at[i]).start()

    def fetched(self, i):
        way, slot = (0, i) if i < 6 else (1, i - 6)
        settle(self.stage[way][slot], self.load.at[i])

    def relay(self):
        for i in (0, 1, 9):
            self.fetch(i)
        for i, k, half, step in ((0, 1, 0, 1), (1, 3, 1, 3)):
            self.fetched(i)
            base = ring(self.me.z, k) * 512 + half * 256

            def add(r, _):
                here = self.place(0, base + r * 64, 64)
                more = self.stage[0][i][pl.ds(pl.multiple_of(r * 64, 64), 64), :]
                self.grad[here] = (self.grad[here].astype(F32) + more.astype(F32)).astype(BF)
                return 0

            lax.fori_loop(0, 4, add, 0)
            self.go(4 + i, k, half, step)
        self.relay_x()

    def second(self):
        me = self.me
        for i in range(2, 9):
            self.fetch(i)
        for i in range(2, 9):
            self.fetched(i)

        def add_z(r, _):
            rows = pl.ds(pl.multiple_of(r * 32, 32), 32)
            for half in (0, 1):
                here = self.place(0, me.z * 512 + half * 256 + r * 32, 32)
                total = self.grad[here].astype(F32)
                for i in (3 - half, 4 + half):
                    total = total + self.stage[0][i][rows, :].astype(F32)
                self.grad[here] = total.astype(BF)
                rows_x = pl.ds(pl.multiple_of(half * 256 + r * 32, 32), 32)
                total = self.stage[1][0][rows_x, :].astype(F32)
                for i in (1, 2):
                    total = total + self.stage[1][i][rows_x, :].astype(F32)
                self.part[rows_x, :] = total.astype(BF)
            return 0

        lax.fori_loop(0, 8, add_z, 0)
        self.over_x(lambda xlo, c: self.grad.at[self.place(0, me.z * 512 + xlo * 256 + c * 128, 128)],
                    self.left.at[me.x], 10)
        for k in (1, 3, 2):
            z = ring(me.z, k)
            remote(self.part.at[rows_at(z * 128, 128)], self.right.at[k - 1], self.send.at[13 + k],
                   self.recv.at[13 + k], me.at(z=z)).start()

    def third(self, store):
        me = self.me
        for i in range(4):
            settle(self.left.at[i], self.recv.at[10 + i])
        for k in (1, 2, 3):
            settle(self.right.at[k - 1], self.recv.at[13 + k])

        def add(i, _):
            rows = pl.ds(pl.multiple_of(i * 32, 32), 32)
            left = self.left[0, rows, :].astype(F32)
            for x in range(1, 4):
                left = left + self.left[x, rows, :].astype(F32)
            right = self.part[pl.ds(pl.multiple_of(me.z * 128 + i * 32, 32), 32), :].astype(F32)
            for k in range(3):
                right = right + self.right[k, rows, :].astype(F32)
            store(rows, left, right)
            return 0

        lax.fori_loop(0, 4, add, 0)

    def finish(self):
        me = self.me
        for i in range(6):
            settle(self.inbox[0].at[i], self.send.at[i])
        for k in (1, 2, 3):
            settle(self.right.at[k - 1], self.send.at[13 + k])
        for xlo in (0, 1):
            for c in (0, 1):
                @pl.when(jnp.logical_or(me.x != me.c * 2 + xlo, me.c != c))
                def _():
                    settle(self.inbox[1].at[0], self.send.at[6 + xlo * 2 + c])
        self.over_x_sent(self.left.at[0], 10)


def dot_rows(left, right):
    return lax.dot_general(left, right, (((0,), (0,)), ((), ())), preferred_element_type=F32)


def back_norm(values, gain, upstream):
    entries = values.shape[-1]
    inverse = inverse_of(values)
    scaled = upstream * gain
    folded = jnp.sum(scaled * values, axis=-1, keepdims=True)
    grad = inverse * scaled - values * (inverse * inverse * inverse) * folded / entries
    return grad, jnp.sum(upstream * values * inverse, axis=0, keepdims=True)


def layer_kernel(
    tokens, cot, attn_gain, mlp_gain, query_gain, key_gain, wo, wq, wk, wv, wg, wu, wd, cosine, sine,
    result, tokens_grad, attn_gain_grad, mlp_gain_grad, query_gain_grad, key_gain_grad,
    qkv_grad, out_grad, gate_grad, up_grad, down_grad, n_out,
    box_q0, box_q1, box_k0, box_k1, box_o0, box_o1, box_g0, box_g1, box_u0, box_u1, box_d0, box_d1,
    n, cota, a, b, a_shard, b_shard, da, h, dg, du, qlin, klin, qrot, kv, o, mid, cos, sin, dqkv, d_o, acc, acc_out, acc_in,
    sib_out, held, arrive, held2, arrive2,
    part_q, left_q, right_q, part_k, left_k, right_k, part_o, left_o, right_o, part_g, left_g, right_g,
    part_u, left_u, right_u, part_d, left_d, right_d, gain8, gainx, gainz, gacc,
    load, n_send, n_recv, c_send, c_recv, n2_send, n2_recv, da_send, da_recv,
    a_send, a_recv, o_send, o_recv, b_send, b_recv, r_send, r_recv, r1_send, r1_recv, r2_send, r2_recv, r3_send, r3_recv,
    q_send, q_recv, k_send, k_recv, g_send, g_recv, u_send, u_recv, d_send, d_recv, p_send, p_recv,
    stage_load, kv_sem, swap_sem, v_send, v_recv,
):
    me = Place()
    barrier, count = greet(me)
    loads = {}

    def fetch(name, src, dst):
        loads[name] = pltpu.make_async_copy(src, dst, load.at[len(loads)])
        loads[name].start()

    for name, src, dst, col in (("wq", wq, a_shard, 0), ("wk", wk, a_shard, 256), ("wv", wv, a_shard, 384),
                                ("wg", wg, b_shard, 0), ("wu", wu, b_shard, 768), ("wd", wd, b_shard, 1536)):
        fetch(name, src, dst.at[:, pl.ds(col, src.shape[1])])
    fetch("cos", cosine.at[me.xhi], cos)
    fetch("sin", sine.at[me.xhi], sin)
    own = (me.c * 4 + me.y) * BLOCK

    def norm_one(i, _):
        rows = pl.ds(pl.multiple_of(i * 16, 16), 16)
        x = tokens[rows, :].astype(F32)
        n[pl.ds(pl.multiple_of(own + i * 16, 16), 16), :] = (x * inverse_of(x) * attn_gain[...]).astype(BF)
        return 0

    lax.fori_loop(0, 8, norm_one, 0)
    cota[rows_at(own, BLOCK), :] = cot[...]
    for name in ("wq", "wk", "wv", "wg", "wu", "wd"):
        loads[name].wait()
    pl.semaphore_wait(barrier, count)

    weights_a = GatherWeights(me, a_shard, a, 0, 384, 512, a_send, a_recv)
    weights_o = GatherWeights(me, wo, a, 512, 256, 256, o_send, o_recv)
    weights_b = GatherWeights(me, b_shard, b, 0, B_CUT, B_COLS, b_send, b_recv)
    rows_n = GatherRows(me, n, n_send, n_recv)
    rows_c = GatherRows(me, cota, c_send, c_recv)
    rows_n2 = GatherRows(me, n, n2_send, n2_recv)
    rows_n.start()
    weights_a.first(0)
    weights_a.first(1)
    weights_o.first(0)
    weights_a.second_z()
    weights_a.second_x()
    rows_n.relay()
    weights_a.relay()
    weights_a.relay_x()
    weights_o.second_z()
    weights_b.first(0)
    rows_n.finish()
    rows_c.start()
    weights_a.arrived()
    weights_o.relay()
    weights_b.first(1)
    n_save = pltpu.make_async_copy(n, n_out, load.at[8])
    n_save.start()
    loads["cos"].wait()
    loads["sin"].wait()

    def project(s):
        rows = rows_at(s * 512, 512)
        x = n[rows, :]
        k = dot(x, a[:, 256:512])
        klin[rows, :] = k[:, 0:128]
        u = k[:, 0:128]
        u = turn(u * inverse_of(u) * key_gain[...], cos[...], sin[...]).astype(BF)
        v = k[:, 128:256].astype(BF)
        for block in range(4):
            kv[0, s, block, 0] = u[block * 128:(block + 1) * 128]
            kv[1, s, block, 0] = v[block * 128:(block + 1) * 128]

    def project_q(s):
        rows = rows_at(s * 512, 512)
        q = dot(n[rows, :], a[:, 0:256])
        qlin[rows, :] = q
        for g in (0, 1):
            u = q[:, g * 128:(g + 1) * 128]
            u = turn(u * inverse_of(u) * query_gain[...], cos[...], sin[...]).astype(BF)
            for block in range(4):
                qrot[rows_at(s * 1024 + block * 256 + g * 128, 128), :] = u[block * 128:(block + 1) * 128]

    order = (1 - me.c, me.c)
    swaps = []
    for i, s in enumerate(order):
        project(s)
        swap = remote(kv.at[:, s, :, 0], kv.at[:, s, :, 1], kv_sem.at[i], kv_sem.at[2 + i], me.at(x=ring(me.x, 2)))
        swap.start()
        swaps.append(swap)
    for s in order:
        project_q(s)
    weights_b.second_z()

    def attend(s):
        for block in range(4):
            size = (block + 1) * 256
            q = qrot[rows_at(s * 1024 + block * 256, 256), :]
            weights = jnp.exp2(dot_t(q, kv[0, s, 0:block + 1].reshape(size, 128)) * SCORE2)
            row = lax.rem(lax.broadcasted_iota(jnp.int32, (256, 256), 0), 128)
            col = lax.broadcasted_iota(jnp.int32, (256, 256), 1)
            weights = mask_last(weights, jnp.logical_or(col <= row, col >= 256 - 128 * me.xhi), 1)
            total = jnp.sum(weights, axis=-1, keepdims=True)
            got = dot(weights.astype(BF), kv[1, s, 0:block + 1].reshape(size, 128))
            got = (got / total).astype(BF)
            rows = rows_at(s * 512 + block * 128, 128)
            o[rows, 0:128] = got[0:128]
            o[rows, 128:256] = got[128:256]

    sums = ReduceRows(me, sib_out, held, arrive, r_send, r_recv)

    def branch(row, j):
        return dot_t(o[rows_at(row, 256), :], a[rows_at(j * 512, 512), 512:768])

    swaps[0].wait()
    attend(order[0])
    weights_o.arrived()
    n_save.wait()
    sums.other(branch)
    rows_c.relay()
    swaps[1].wait()
    weights_b.second_x()
    attend(order[1])
    sums.mine(branch)
    sums.relay()
    rows_c.finish()
    weights_b.relay()
    weights_b.relay_x()
    sums.wait()

    def norm_two(i, _):
        rows = pl.ds(pl.multiple_of(i * 16, 16), 16)
        x = tokens[rows, :].astype(F32) + sums.total(i * 16)
        mid[rows, :] = x
        n[pl.ds(pl.multiple_of(own + i * 16, 16), 16), :] = (x * inverse_of(x) * mlp_gain[...]).astype(BF)
        return 0

    lax.fori_loop(0, 8, norm_two, 0)
    rows_n2.start()
    sums.finish()
    rows_n2.relay()
    rows_n2.finish()
    weights_b.arrived()
    weights_a.finish()
    weights_o.finish()
    weights_b.finish()

    def hidden(j, i):
        rows = rows_at(i * 512, 512)
        cols = slice(j * 256, j * 256 + 256)
        gate = dot(n[rows, :], b[:, cols])
        up = dot(n[rows, :], b[:, 768 + j * 256:1024 + j * 256])
        d_hidden = dot(cota[rows, :], b[:, 1536 + j * 256:1792 + j * 256])
        sg = jax.nn.sigmoid(gate)
        active = gate * sg
        h[rows, cols] = (active * up).astype(BF)
        dg[rows, cols] = (d_hidden * up * sg * (1.0 + gate * (1.0 - sg))).astype(BF)
        du[rows, cols] = (d_hidden * active).astype(BF)

    for j in range(3):
        lax.fori_loop(0, 2, lambda i, _, j=j: (hidden(j, i), 0)[1], 0)
    sum_n2 = ReduceRows(me, sib_out, held, arrive, r1_send, r1_recv)
    sum_result = ReduceRows(me, sib_out, held2, arrive2, r2_send, r2_recv)
    sum_n = ReduceRows(me, sib_out, held, arrive, r3_send, r3_recv)

    def back_n2(row, j):
        rows, model = rows_at(row, 256), rows_at(j * 512, 512)
        return dot_t(dg[rows, :], b[model, 0:768]) + dot_t(du[rows, :], b[model, 768:1536])

    def down(row, j):
        return dot_t(h[rows_at(row, 256), :], b[rows_at(j * 512, 512), 1536:2304])

    sum_n2.other(back_n2)
    sum_n2.mine(back_n2)
    def stages(first, second):
        quarter = [(buf, r) for buf in (dg, du) for r in range(4)]
        return ([buf.at[pl.ds(r * 256, 256), pl.ds(0, first)] for buf, r in quarter[:6]],
                [buf.at[pl.ds(r * 512, 512), pl.ds(512, second)] for buf in (dg, du) for r in (0, 1)])

    def reduction(grad, col, widths, boxes, sums, sems, fold=0):
        return ReduceWeights(me, grad, col, widths, boxes, stages(*widths), *sums, *sems, stage_load, fold)

    red_g = reduction(b, 0, WIDE, (box_g0, box_g1), (part_g, left_g, right_g), (g_send, g_recv))
    red_u = reduction(b, 768, WIDE, (box_u0, box_u1), (part_u, left_u, right_u), (u_send, u_recv))
    red_d = reduction(b, 1536, WIDE, (box_d0, box_d1), (part_d, left_d, right_d), (d_send, d_recv))
    red_o = reduction(a, 512, NARROW, (box_o0, box_o1), (part_o, left_o, right_o), (p_send, p_recv))
    red_q = reduction(n, 0, NARROW, (box_q0, box_q1), (part_q, left_q, right_q), (q_send, q_recv), 256)
    red_k = reduction(a, 256, NARROW, (box_k0, box_k1), (part_k, left_k, right_k), (k_send, k_recv))

    def weight_grad(red, left, right, unroll=False):
        def step(i, _):
            red.store(i, dot_rows(left[:, rows_at(i * 256, 256)], right[...]))
            return 0

        lax.fori_loop(0, 8, step, 0, unroll=unroll)
        red.first()

    weight_grad(red_g, n, dg)
    sum_n2.relay()
    weight_grad(red_u, n, du)
    sum_n2.wait()
    rows_da = GatherRows(me, da, da_send, da_recv)

    def back_two(i, total):
        rows = pl.ds(pl.multiple_of(i * 16, 16), 16)
        grad, gain = back_norm(mid[rows, :], mlp_gain[...], sum_n2.total(i * 16))
        grad = grad + cot[rows, :].astype(F32)
        tokens_grad[rows, :] = grad
        da[pl.ds(pl.multiple_of(own + i * 16, 16), 16), :] = grad.astype(BF)
        return total + gain

    mlp_part = lax.fori_loop(0, 8, back_two, jnp.zeros((1, WIDTH), F32))
    rows_da.start()
    slot = me.c * 4 + me.y

    def spread(value, col):
        for i in range(8):
            gainx[me.x, i:i + 1, col:col + 256] = value[:, i * 256:(i + 1) * 256]

    gainx[me.x] = jnp.zeros((8, 640), F32)
    spread(mlp_part, 256)
    gacc[...] = jnp.zeros_like(gacc)
    sum_n2.finish()
    sum_result.other(down)
    sum_result.mine(down, send=False)
    rows_da.relay()
    red_g.relay()
    weight_grad(red_d, cota, h)
    n_load = pltpu.make_async_copy(n_out, cota, load.at[9])
    n_load.start()
    red_u.relay()
    rows_da.finish()

    def back_o(i, _):
        rows = rows_at(i * 512, 512)
        d_o[rows, :] = dot(da[rows, :], a[:, 512:768]).astype(BF)
        return 0

    lax.fori_loop(0, 2, back_o, 0)
    sum_result.send_all()

    swaps = []
    q_gain = jnp.zeros((1, HEAD), F32)
    for turn_ in (0, 1):
        s = 1 - me.c if turn_ == 0 else me.c
        flat = kv[0, s].reshape(1024, 128).T
        key = lax.broadcasted_iota(jnp.int32, (256, 256), 0)
        query = lax.rem(lax.broadcasted_iota(jnp.int32, (256, 256), 1), 128)
        keep = jnp.logical_or(key <= query, key >= 256 - 128 * me.xhi)
        dqs = {}
        for pair in ((3, 0), (2, 1)):
            sizes = [(block + 1) * 256 for block in pair]
            qs = [qrot[rows_at(s * 1024 + block * 256, 256), :] for block in pair]
            gs = []
            for block in pair:
                rows = rows_at(s * 512 + block * 128, 128)
                gs.append(jnp.concatenate([d_o[rows, 0:128], d_o[rows, 128:256]], axis=0))
            ks = [kv[0, s, 0:block + 1].reshape(size, 128) for block, size in zip(pair, sizes)]
            vs = [kv[1, s, 0:block + 1].reshape(size, 128) for block, size in zip(pair, sizes)]
            ps = [mask_last(jnp.exp2(dot_t(k, q) * SCORE2), keep, 0) for k, q in zip(ks, qs)]
            dps = [dot_t(v, g) for v, g in zip(vs, gs)]
            ps = [p * (1.0 / jnp.sum(p, axis=0, keepdims=True)) for p in ps]
            dss = [(p * (dp - jnp.sum(dp * p, axis=0, keepdims=True))).astype(BF) for p, dp in zip(ps, dps)]
            for block, size, ds in zip(pair, sizes, dss):
                dqs[block] = (dot(flat[:, :size], ds) * SCORE).T
            dks = [dot(ds, q) * SCORE for ds, q in zip(dss, qs)]
            dvs = [dot(p.astype(BF), g) for p, g in zip(ps, gs)]
            for block, dk, dv in zip(pair, dks, dvs):
                for i, value in enumerate((dk, dv)):
                    value = value.reshape(block + 1, 2, 128, 128)
                    if block == 3:
                        acc[i, s] = value
                    else:
                        acc[i, s, 0:block + 1] += value
        rows = rows_at(s * 512, 512)
        for head in (0, 1):
            dq = jnp.concatenate([dqs[block][head * 128:(head + 1) * 128] for block in range(4)], axis=0)
            up = turn(dq, cos[...], -sin[...])
            grad, gain = back_norm(qlin[rows, head * 128:(head + 1) * 128], query_gain[...], up)
            dqkv[rows, head * 128:(head + 1) * 128] = grad.astype(BF)
            q_gain = q_gain + gain
        for i in (0, 1):
            acc_out[turn_, i] = acc[i, s, :, 1].astype(BF)
        swap = remote(acc_out.at[turn_], acc_in.at[turn_], swap_sem.at[turn_], swap_sem.at[2 + turn_],
                      me.at(x=ring(me.x, 2)))
        swap.start()
        swaps.append(swap)
    red_d.relay()
    weight_grad(red_o, da, o, True)
    n_load.wait()
    weight_grad(red_q, cota, dqkv.at[:, pl.ds(0, 256)], True)
    sum_result.relay()
    red_g.second()
    red_u.second()

    k_gain = jnp.zeros((1, HEAD), F32)

    def back_n(row, j):
        rows, model = rows_at(row, 256), rows_at(j * 512, 512)
        term = dot_t(dqkv[rows, 0:256], a[model, 0:256]) + dot_t(dqkv[rows, 256:512], a[model, 256:512])
        cols = rows_at(j * 512, 512)
        gacc[:, cols] += jnp.sum(term * cota[rows, cols].astype(F32), axis=0, keepdims=True)
        return term

    for turn_ in (0, 1):
        s = 1 - me.c if turn_ == 0 else me.c
        rows = rows_at(s * 512, 512)
        swaps[turn_].wait()
        dk = (acc[0, s, :, 0] + acc_in[turn_, 0].astype(F32)).reshape(512, 128)
        dv = (acc[1, s, :, 0] + acc_in[turn_, 1].astype(F32)).reshape(512, 128)
        grad, gain = back_norm(klin[rows, :], key_gain[...], turn(dk, cos[...], -sin[...]))
        k_gain = k_gain + gain
        dqkv[rows, 256:384] = grad.astype(BF)
        dqkv[rows, 384:512] = dv.astype(BF)
        if turn_ == 0:
            sum_result.finish()
            sum_n.other(back_n)
        else:
            sum_n.mine(back_n)
    spread(gacc[...] / attn_gain[...], 0)
    gainx[me.x, 0:1, 512:640] = q_gain
    gainx[me.x, 1:2, 512:640] = k_gain
    for k in (1, 2, 3):
        remote(gainx.at[me.x], gainx.at[me.x], v_send.at[6 + k], v_recv.at[8 + me.x], me.at(x=ring(me.x, k))).start()
    weight_grad(red_k, cota, dqkv.at[:, pl.ds(256, 256)], True)
    red_o.relay()
    red_q.relay()
    sum_n.relay()
    red_d.second()
    red_o.second()
    for i in range(4):
        @pl.when(me.x != i)
        def _():
            settle(gainx.at[i], v_recv.at[8 + i])
    gainz[me.z] = gainx[0] + gainx[1] + gainx[2] + gainx[3]
    for k in (1, 2, 3):
        remote(gainz.at[me.z], gainz.at[me.z], v_send.at[9 + k], v_recv.at[12 + me.z], me.at(z=ring(me.z, k))).start()
    red_k.relay()
    red_q.second()

    def put(ref, col=0):
        def store(rows, left, right):
            middle = col + left.shape[1]
            ref[rows, col:middle] = left
            ref[rows, middle:middle + right.shape[1]] = right
        return store

    red_g.third(put(gate_grad))
    red_u.third(put(up_grad))
    for i in range(4):
        @pl.when(me.z != i)
        def _():
            settle(gainz.at[i], v_recv.at[12 + i])
    gain8[slot] = gainz[0] + gainz[1] + gainz[2] + gainz[3]
    peers = [(me.y, 1 - me.c)] + [(ring(me.y, k), c) for k in (1, 2, 3) for c in (0, 1)]
    for i, (y, c) in enumerate(peers):
        remote(gain8.at[slot], gain8.at[slot], v_send.at[i], v_recv.at[slot], me.at(y=y, c=c)).start()
    red_d.third(put(down_grad))
    sum_result.wait()

    def finish_result(i, _):
        rows = pl.ds(pl.multiple_of(i * 16, 16), 16)
        result[rows, :] = (mid[rows, :] + sum_result.total(i * 16)).astype(BF)
        return 0

    lax.fori_loop(0, 8, finish_result, 0)
    red_k.second()
    red_o.third(put(out_grad))
    sum_n.wait()

    def back_one(i, _):
        rows = pl.ds(pl.multiple_of(i * 16, 16), 16)
        grad, _ = back_norm(tokens[rows, :].astype(F32), attn_gain[...], sum_n.total(i * 16))
        tokens_grad[rows, :] += grad
        return 0

    lax.fori_loop(0, 8, back_one, 0)
    for i in range(8):
        @pl.when(slot != i)
        def _():
            settle(gain8.at[i], v_recv.at[i])
    total = gain8[0]
    for i in range(1, 8):
        total = total + gain8[i]
    for i in range(8):
        cols = slice(i * 256, i * 256 + 256)
        attn_gain_grad[:, cols] = total[i:i + 1, 0:256]
        mlp_gain_grad[:, cols] = total[i:i + 1, 256:512]
    query_gain_grad[...] = total[0:1, 512:640]
    key_gain_grad[...] = total[1:2, 512:640]
    red_q.third(put(qkv_grad))
    red_k.third(put(qkv_grad, 256))
    for i in range(13):
        settle(gain8.at[0], v_send.at[i])
    sum_n.finish()
    for red in (red_g, red_u, red_d, red_o, red_q, red_k):
        red.finish()


def layer(tokens, cot, gains, weights, cos, sin):
    wq, wk, wv, wo, wg, wu, wd = weights
    args = (tokens, cot) + gains + (wo, wq, wk, wv, wg, wu, wd, cos, sin)
    vmem = pl.BlockSpec(memory_space=pltpu.VMEM)
    hbm = pl.BlockSpec(memory_space=pl.ANY)
    outs = [((BLOCK, WIDTH), BF), ((BLOCK, WIDTH), F32), ((1, WIDTH), F32), ((1, WIDTH), F32)]
    outs += [((1, HEAD), F32), ((1, HEAD), F32), ((BLOCK, 512), F32), ((BLOCK, 256), F32)]
    outs += [((BLOCK, 768), F32)] * 3
    widths = (NARROW, NARROW, NARROW, WIDE, WIDE, WIDE)
    boxes = [((ROWS, WIDTH), BF)]
    boxes += [box for w in widths for box in (((6, 256, w[0]), BF), ((4, 512, w[1]), BF))]
    scratch = [
        ((ROWS, WIDTH), BF), ((ROWS, WIDTH), BF), ((WIDTH, A_COLS), BF), ((WIDTH, B_COLS), BF),
        ((BLOCK, 512), BF), ((BLOCK, B_COLS), BF), ((ROWS, WIDTH), BF),
        ((ROWS, 768), BF), ((ROWS, 768), BF), ((ROWS, 768), BF), ((ROWS, 256), F32), ((ROWS, 128), F32),
        ((2 * ROWS, 128), BF), (KV_SHAPE, BF), ((ROWS, 256), BF), ((BLOCK, WIDTH), F32),
        ((512, 128), F32), ((512, 128), F32), ((ROWS, 512), BF), ((ROWS, 256), BF), (KV_SHAPE, F32),
        ((2, 2, 4, 128, 128), BF), ((2, 2, 4, 128, 128), BF),
        ((512, WIDTH), BF), ((512, WIDTH), BF), ((6, 64, WIDTH), BF), ((512, WIDTH), BF), ((6, 64, WIDTH), BF),
    ]
    for w in widths:
        scratch += [((512, w[1]), BF), ((4, BLOCK, w[0]), BF), ((3, BLOCK, w[1]), BF)]
    scratch += [((8, 8, 640), F32), ((4, 8, 640), F32), ((4, 8, 640), F32), ((1, WIDTH), F32)]
    scratch = [pltpu.VMEM(s, d) for s, d in scratch]
    dma = pltpu.SemaphoreType.DMA
    scratch += [dma((10,))] + [dma((GatherRows.sems,))] * 8 + [dma((GatherWeights.sems,))] * 6 + [dma((8,))] * 8
    scratch += [dma((ReduceWeights.sems,))] * 12 + [dma((10,)), dma((4,)), dma((4,)), dma((13,)), dma((16,))]
    got = pl.pallas_call(
        layer_kernel,
        out_shape=[jax.ShapeDtypeStruct(s, d) for s, d in outs + boxes],
        in_specs=[vmem] * 7 + [hbm] * 8,
        out_specs=[vmem] * len(outs) + [hbm] * len(boxes),
        scratch_shapes=scratch,
        compiler_params=pltpu.CompilerParams(
            collective_id=1, has_side_effects=True, vmem_limit_bytes=VMEM_BYTES),
        name="layer_part",
    )(*args)
    return got[:len(outs)]


def finish_kernel(*refs):
    parts, outs, sem = refs[:11], refs[11:24], refs[24]
    qkv = parts[6]
    sources = parts[:6] + tuple(qkv.at[:, pl.ds(*cols)] for cols in ((0, 256), (256, 128), (384, 128))) + parts[7:]
    copies = [pltpu.make_async_copy(src, dst, sem.at[i]) for i, (src, dst) in enumerate(zip(sources, outs))]
    for copy in copies:
        copy.start()
    for copy in copies:
        copy.wait()


def finish(parts):
    shapes = [((BLOCK, WIDTH), BF), ((BLOCK, WIDTH), F32), ((1, WIDTH), F32), ((1, WIDTH), F32), ((1, HEAD), F32)]
    shapes += [((1, HEAD), F32), ((BLOCK, 256), F32), ((BLOCK, 128), F32), ((BLOCK, 128), F32), ((BLOCK, 256), F32)]
    shapes += [((BLOCK, 768), F32)] * 3
    return pl.pallas_call(
        finish_kernel,
        out_shape=[jax.ShapeDtypeStruct(s, d) for s, d in shapes],
        in_specs=[pl.BlockSpec(memory_space=pl.ANY)] * len(parts),
        out_specs=[pl.BlockSpec(memory_space=pltpu.VMEM)] * len(shapes),
        scratch_shapes=[pltpu.SemaphoreType.DMA((13,))],
        compiler_params=pltpu.CompilerParams(vmem_limit_bytes=VMEM_BYTES),
        name="finish_part",
    )(*parts)


def local(tokens, cotangent, attn_gain, mlp_gain, query_gain, key_gain, *weights):
    cos, sin = rope_tables()
    gains = (attn_gain[None], mlp_gain[None], query_gain[None], key_gain[None])
    outs = finish(layer(tokens, cotangent, gains, weights, cos, sin))
    return tuple(outs[:2]) + tuple(g[0] for g in outs[2:6]) + tuple(outs[6:])


def solution(mesh):
    rows, plane = P(("dp", "tensor"), None), P("dp", "tensor")
    return jax.shard_map(
        local,
        mesh=mesh,
        in_specs=(rows, rows, P(), P(), P(), P()) + (plane,) * 7,
        out_specs=(rows, rows, P(), P(), P(), P()) + (plane,) * 7,
        check_vma=False,
    )
```

```python
import functools

import numpy as np
import jax
import jax.numpy as jnp
from jax import lax
from jax.experimental import pallas as pl
from jax.experimental.pallas import tpu as pltpu
from jax.sharding import PartitionSpec as P

EPS = 1e-06
ROPE_BASE = 1000000.0
MESH = pl.DeviceIdType.MESH
BF = jnp.bfloat16
F32 = jnp.float32
HEAD = 128
WIDTH = 2048
BLOCK = 128
ROWS = 1024
A_COLS = 768
B_COLS = 2304
B_CUT = 896
D_CUT = 384
SCORE = HEAD ** -0.5
KV_SHAPE = (2, 2, 4, 2, 128, 128)
SCORE2 = HEAD ** -0.5 * 1.4426950408889634
VMEM_BYTES = 63 * 2**20


class Place:
    def __init__(self):
        dp = lax.axis_index("dp")
        tensor = lax.axis_index("tensor")
        self.dp = dp
        self.xlo = lax.div(dp, 8)
        self.z = lax.rem(lax.div(dp, 2), 4)
        self.c = lax.rem(dp, 2)
        self.y = lax.div(tensor, 2)
        self.xhi = lax.rem(tensor, 2)
        self.x = self.xhi * 2 + self.xlo

    def at(self, x=None, y=None, z=None, c=None):
        x = self.x if x is None else x
        y = self.y if y is None else y
        z = self.z if z is None else z
        c = self.c if c is None else c
        return (lax.rem(x, 2) * 8 + z * 2 + c, y * 2 + lax.div(x, 2))

    def sibling(self):
        return self.at(c=1 - self.c)


def ring(v, k):
    return lax.rem(v + k, 4)


def remote(src, dst, send_sem, recv_sem, target):
    return pltpu.make_async_remote_copy(
        src_ref=src, dst_ref=dst, send_sem=send_sem, recv_sem=recv_sem,
        device_id=target, device_id_type=MESH,
    )


def settle(ref, sem):
    pltpu.make_async_copy(ref, ref, sem).wait()


def rows_at(start, size):
    return pl.ds(pl.multiple_of(start, 128), size)


def greet(me):
    barrier = pltpu.get_barrier_semaphore()
    others = [me.sibling()]
    for k in (1, 2, 3):
        others.append(me.at(y=ring(me.y, k)))
        others.append(me.at(y=ring(me.y, k), c=1 - me.c))
        for c in (0, 1):
            others.append(me.at(x=ring(me.x, k), c=c))
            others.append(me.at(z=ring(me.z, k), c=c))
    for other in others:
        pl.semaphore_signal(barrier, inc=1, device_id=other, device_id_type=MESH)
    return barrier, len(others)


class GatherRows:
    sems = 13

    def __init__(self, me, buf, send, recv):
        self.me, self.buf, self.send, self.recv = me, buf, send, recv

    def piece(self, c, y, half):
        return self.buf.at[pl.ds(pl.multiple_of((c * 4 + y) * BLOCK + half * 64, 64), 64)]

    def go(self, y, half, i, target):
        ref = self.piece(self.me.c, y, half)
        remote(ref, ref, self.send.at[i], self.recv.at[i], target).start()

    def start(self):
        me = self.me
        up, down = me.at(y=ring(me.y, 1)), me.at(y=ring(me.y, 3))
        self.go(me.y, 0, 0, up)
        self.go(me.y, 1, 2, down)
        own = self.buf.at[rows_at((me.c * 4 + me.y) * BLOCK, BLOCK)]
        remote(own, own, self.send.at[6], self.recv.at[6], me.sibling()).start()

    def heard(self, i, k, half):
        me = self.me
        y = ring(me.y, 4 - k)
        settle(self.piece(me.c, y, half), self.recv.at[i])
        self.go(y, half, 7 + i, me.sibling())
        return y

    def relay(self):
        me = self.me
        up, down = me.at(y=ring(me.y, 1)), me.at(y=ring(me.y, 3))
        half = self.piece(me.c, me.y, 0)
        settle(half, self.send.at[0])
        self.go(me.y, 1, 1, up)
        settle(half, self.send.at[2])
        self.go(me.y, 0, 3, down)
        y = self.heard(0, 1, 0)
        self.go(y, 0, 4, up)
        y = self.heard(2, 3, 1)
        self.go(y, 1, 5, down)

    def finish(self):
        me = self.me
        self.heard(1, 1, 1)
        self.heard(3, 3, 0)
        self.heard(4, 2, 0)
        self.heard(5, 2, 1)
        half = self.piece(me.c, me.y, 0)
        own = self.buf.at[rows_at((me.c * 4 + me.y) * BLOCK, BLOCK)]
        for i in (1, 3, 4, 5, 6, 7, 8, 9, 10, 11, 12):
            settle(own if i == 6 else half, self.send.at[i])
        for i in range(6, 13):
            settle(own if i == 6 else half, self.recv.at[i])


class ReduceRows:
    def __init__(self, me, sib_out, held, arrive, send, recv):
        self.me = me
        self.sib_out, self.held, self.arrive = sib_out, held, arrive
        self.send, self.recv = send, recv
        first = 1 - lax.div(me.y, 2)
        self.halves = (first, 1 - first)

    def other(self, tile):
        me = self.me
        for p, half in enumerate(self.halves):
            rows = rows_at(half * 256, 256)

            def step(j, _):
                cols = rows_at(j * 512, 512)
                self.sib_out[rows, cols] = tile((1 - me.c) * 512 + half * 256, j).astype(BF)
                return 0

            lax.fori_loop(0, 4, step, 0, unroll=True)
            remote(self.sib_out.at[rows], self.held.at[rows], self.send.at[6 + p], self.recv.at[6 + p],
                   me.sibling()).start()

    def piece(self, k, half):
        return pl.ds(pl.multiple_of(ring(self.me.y, k) * BLOCK + half * 64, 64), 64)

    def go(self, i, k, half, step):
        remote(self.held.at[self.piece(k, half)], self.arrive.at[i], self.send.at[i], self.recv.at[i],
               self.me.at(y=ring(self.me.y, step))).start()

    def mine(self, tile, send=True):
        me = self.me
        for p, half in enumerate(self.halves):
            rows = rows_at(half * 256, 256)
            settle(self.held.at[rows], self.recv.at[6 + p])

            def step(j, _):
                cols = rows_at(j * 512, 512)
                total = tile(me.c * 512 + half * 256, j) + self.held[rows, cols].astype(F32)
                self.held[rows, cols] = total.astype(BF)
                return 0

            lax.fori_loop(0, 4, step, 0, unroll=True)
            if not send:
                continue
            even = lax.rem(me.y, 2) == 0
            if p == 0:
                self.go(0, 2, 0, 1)
                self.go(1, 2, 1, 3)
            pl.when(even if p == 0 else jnp.logical_not(even))(lambda: self.go(3, 3, 0, 3))
            pl.when(jnp.logical_not(even) if p == 0 else even)(lambda: self.go(2, 1, 1, 1))

    def send_all(self):
        self.go(0, 2, 0, 1)
        self.go(1, 2, 1, 3)
        self.go(2, 1, 1, 1)
        self.go(3, 3, 0, 3)

    def relay(self):
        for i, k, half, step in ((0, 1, 0, 1), (1, 3, 1, 3)):
            settle(self.arrive.at[i], self.recv.at[i])
            rows = self.piece(k, half)
            self.held[rows, :] = (self.held[rows, :].astype(F32) + self.arrive[i].astype(F32)).astype(BF)
            self.go(4 + i, k, half, step)

    def wait(self):
        for i in range(2, 6):
            settle(self.arrive.at[i], self.recv.at[i])

    def total(self, r):
        half = lax.div(r, 64)
        rows = pl.ds(pl.multiple_of(r - half * 64, 16), 16)
        total = self.held[pl.ds(pl.multiple_of(self.me.y * BLOCK + r, 16), 16), :].astype(F32)
        return total + self.arrive[3 - half, rows, :].astype(F32) + self.arrive[4 + half, rows, :].astype(F32)

    def free(self):
        for p in (0, 1):
            settle(self.sib_out.at[rows_at(0, 256)], self.send.at[6 + p])

    def finish(self):
        for i in range(6):
            settle(self.arrive.at[i], self.send.at[i])


class GatherWeights:
    sems = 23

    def __init__(self, me, shard, full, col, cut, width, send, recv):
        self.me, self.shard, self.full = me, shard, full
        self.cols = (pl.ds(col, cut), pl.ds(col + cut, width - cut))
        self.from_cols = (pl.ds(0, cut), pl.ds(cut, width - cut))
        self.send, self.recv = send, recv
        self.ways = (0, 1) if cut < width else (0,)

    def slot(self, way, dp):
        return self.full.at[rows_at(dp * BLOCK, BLOCK), self.cols[way]]

    def first(self, way):
        me = self.me
        home = me.xhi
        src = self.shard.at[:, self.from_cols[way]]
        dst = self.slot(way, me.dp)
        inbox = self.recv.at[(me.xlo * 2 + me.c) if way == 0 else (10 + me.z * 2 + me.c)]
        base = 0 if way == 0 else 10
        for k in (1, 3, 2):
            target = me.at(x=ring(me.x, k), c=home) if way == 0 else me.at(z=ring(me.z, k), c=home)
            remote(src, dst, self.send.at[base + k], inbox, target).start()

        @pl.when(me.c == home)
        def _():
            pltpu.make_async_copy(src, dst, inbox).start()

        @pl.when(me.c != home)
        def _():
            remote(src, dst, self.send.at[base], inbox, me.sibling()).start()

    def second_z(self):
        me = self.me
        for xlo in (0, 1):
            for c in (0, 1):
                settle(self.slot(0, xlo * 8 + me.z * 2 + c), self.recv.at[xlo * 2 + c])
        self.go(0, me.z, 4, 1)
        self.go(1, me.z, 6, 3)
        self.go(1, me.z, 5, 1)
        self.go(0, me.z, 7, 3)

    def go(self, xlo, z, i, step):
        ref = self.pair(xlo, z)
        remote(ref, ref, self.send.at[i], self.recv.at[i], self.me.at(z=ring(self.me.z, step))).start()

    def relay(self):
        me = self.me
        for i, xlo, step in ((4, 0, 1), (6, 1, 3)):
            z = ring(me.z, 4 - step)
            settle(self.pair(xlo, z), self.recv.at[i])
            self.go(xlo, z, 8 + xlo, step)

    def second_x(self):
        me = self.me
        if 1 not in self.ways:
            return

        @pl.when(me.c == me.xhi)
        def _():
            for z in range(4):
                for c in (0, 1):
                    settle(self.slot(1, me.xlo * 8 + z * 2 + c), self.recv.at[10 + z * 2 + c])
            for i, (part, step) in enumerate(((0, 1), (1, 3), (1, 1), (0, 3))):
                self.go_x(me.xlo, part, 18 + i, ring(me.x, step))

    def go_x(self, xlo, part, i, x):
        ref = self.quarter(xlo, part)
        remote(ref, ref, self.send.at[i], self.recv.at[18 + xlo * 2 + part], self.me.at(x=x)).start()

    def near_x(self):
        me = self.me
        below = lax.div(ring(me.x, 3), 2)
        up = 1 - (below + me.c - 2 * below * me.c)
        return up, lax.rem(ring(me.x, 1 + 2 * up), 2), 1 - up

    def relay_x(self):
        if 1 not in self.ways:
            return
        up, xlo, part = self.near_x()
        settle(self.quarter(0, 0), self.recv.at[18 + xlo * 2 + part])
        self.go_x(xlo, part, 22, ring(self.me.x, 3 - 2 * up))

    def pair(self, xlo, z):
        return self.full.at[rows_at(xlo * 1024 + z * 256, 256), self.cols[0]]

    def quarter(self, xlo, part):
        return self.full.at[rows_at(xlo * 1024 + part * 512, 512), self.cols[1]]

    def arrived(self):
        me = self.me
        for i in (5, 7, 8, 9):
            settle(self.pair(0, me.z), self.recv.at[i])
        if 1 not in self.ways:
            return
        _, near, near_part = self.near_x()
        for xlo in (0, 1):
            for part in (0, 1):
                here = jnp.logical_and(me.c == me.xhi, me.xlo == xlo)
                done = jnp.logical_and(near == xlo, near_part == part)

                @pl.when(jnp.logical_not(jnp.logical_or(here, done)))
                def _():
                    settle(self.quarter(0, 0), self.recv.at[18 + xlo * 2 + part])

    def finish(self):
        me = self.me
        for way in self.ways:
            src = self.shard.at[:, self.from_cols[way]]
            base = 0 if way == 0 else 10
            for k in (1, 2, 3):
                settle(src, self.send.at[base + k])

            @pl.when(me.c != me.xhi)
            def _():
                settle(src, self.send.at[base])
        for i in range(4, 10):
            settle(self.pair(0, me.z), self.send.at[i])

        if 1 not in self.ways:
            return

        @pl.when(me.c == me.xhi)
        def _():
            for i in range(18, 22):
                settle(self.quarter(0, 0), self.send.at[i])

        settle(self.quarter(0, 0), self.send.at[22])


def dot(left, right):
    return jnp.dot(left, right, preferred_element_type=F32)


def dot_t(left, right):
    return lax.dot_general(left, right, (((1,), (1,)), ((), ())), preferred_element_type=F32)


def inverse_of(values):
    return lax.rsqrt(jnp.mean(values * values, axis=-1, keepdims=True) + EPS)


def turn(values, cosine, sine):
    return values * cosine + pltpu.roll(values, 64, 1) * sine


def mask_last(values, keep, axis):
    size = values.shape[axis]
    last = jnp.where(keep, lax.slice_in_dim(values, size - 256, size, axis=axis), 0.0)
    if size == 256:
        return last
    return jnp.concatenate([lax.slice_in_dim(values, 0, size - 256, axis=axis), last], axis=axis)


def rope_tables():
    frequency = ROPE_BASE ** (-2.0 * np.arange(64, dtype=np.float64) / HEAD)
    angle = np.arange(1024, dtype=np.float64)[:, None] * frequency[None, :]
    cos = np.concatenate([np.cos(angle), np.cos(angle)], axis=1).astype(np.float32)
    sin = np.concatenate([-np.sin(angle), np.sin(angle)], axis=1).astype(np.float32)
    pick = lambda t: t.reshape(4, 2, 128, 128).transpose(1, 0, 2, 3).reshape(2, 512, 128)
    return pick(cos), pick(sin)


WIDE, NARROW, ONE_WAY = (384, 384), (128, 128), (256, 0)


class ReduceWeights:
    sems = 17

    def __init__(self, me, grad, first_col, widths, inbox, stage, part, left, right, send, recv, load, fold=0):
        self.me, self.grad, self.widths, self.fold = me, grad, widths, fold
        self.first_cols = (first_col, first_col + widths[0])
        self.both = widths[1] > 0
        self.inbox, self.stage, self.part, self.left, self.right = inbox, stage, part, left, right
        self.send, self.recv, self.load = send, recv, load

    def place(self, way, start, size):
        col = self.first_cols[way]
        if self.fold:
            high = lax.div(start, 1024)
            start = start - high * 1024
            col = pl.multiple_of(col + high * self.fold, 128)
        return pl.ds(pl.multiple_of(start, 32), size), pl.ds(col, self.widths[way])

    def store(self, i, value):
        xlo, z = lax.div(i, 4), lax.rem(i, 4)
        value = value.astype(BF)
        self.grad[self.place(0, z * 512 + xlo * 256, 256)] = value[:, :self.widths[0]]
        for c in (0, 1) if self.both else ():
            self.grad[self.place(1, (xlo * 2 + c) * 512 + z * 128, 128)] = value[
                c * 128:(c + 1) * 128, self.widths[0]:]

    def piece(self, k, half):
        return self.grad.at[self.place(0, ring(self.me.z, k) * 512 + half * 256, 256)]

    def go(self, i, k, half, step):
        remote(self.piece(k, half), self.inbox[0].at[i], self.send.at[i], self.recv.at[i],
               self.me.at(z=ring(self.me.z, step))).start()

    def over_x(self, sources, dst, base):
        me = self.me
        for xlo in (0, 1):
            for c in (0, 1):
                src = sources(xlo, c)
                x = me.c * 2 + xlo
                self_too = jnp.logical_and(me.x == x, me.c == c)

                @pl.when(self_too)
                def _():
                    pltpu.make_async_copy(src, dst, self.recv.at[base + me.x]).start()

                @pl.when(jnp.logical_not(self_too))
                def _():
                    remote(src, dst, self.send.at[base + xlo * 2 + c], self.recv.at[base + me.x],
                           me.at(x=x, c=c)).start()

    def over_x_sent(self, ref, base):
        me = self.me
        for xlo in (0, 1):
            for c in (0, 1):
                @pl.when(jnp.logical_or(me.x != me.c * 2 + xlo, me.c != c))
                def _():
                    settle(ref, self.send.at[base + xlo * 2 + c])

    def first(self):
        self.go(0, 2, 0, 1)
        self.go(1, 2, 1, 3)
        self.go(2, 1, 1, 1)
        self.go(3, 3, 0, 3)
        if not self.both:
            return
        me = self.me
        for xlo in (0, 1):
            x = me.c * 2 + xlo
            away = ring(me.x + 4 - x, 0)
            for c in (0, 1):
                there = me.at(x=x, c=c)

                @pl.when(jnp.logical_and(away == 0, me.c == c))
                def _():
                    pltpu.make_async_copy(self.share(xlo, c), self.inbox[1].at[0], self.recv.at[6]).start()

                @pl.when(jnp.logical_and(away == 0, me.c != c))
                def _():
                    self.go_x(xlo, c, 0, there)

                @pl.when(away == 2)
                def _():
                    self.go_x(xlo, c, 3, me.at(x=ring(me.x, 3 if c == 0 else 1)))

                @pl.when(away == (3 if c == 0 else 1))
                def _():
                    self.go_x(xlo, c, 2 if c == 0 else 1, there)

    def share(self, xlo, c):
        return self.grad.at[self.place(1, jnp.int32(0) + (xlo * 2 + c) * 512, 512)]

    def go_x(self, xlo, c, slot, target):
        remote(self.share(xlo, c), self.inbox[1].at[slot], self.send.at[6 + xlo * 2 + c], self.recv.at[6 + slot],
               target).start()

    def relay_x(self):
        me = self.me
        away = ring(me.x + 4 - me.c * 2, 0)
        xlo = 1 - lax.rem(away, 2)
        c = lax.div(ring(away + 4 - xlo, 0), 2)
        self.fetched(9)

        def add(r, _):
            here = self.place(1, (xlo * 2 + c) * 512 + r * 64, 64)
            more = self.stage[1][3][pl.ds(pl.multiple_of(r * 64, 64), 64), :]
            self.grad[here] = (self.grad[here].astype(F32) + more.astype(F32)).astype(BF)
            return 0

        lax.fori_loop(0, 8, add, 0)
        self.go_x(xlo, c, 1 + c, me.at(x=me.c * 2 + xlo, c=c))

    def fetch(self, i):
        way, slot = (0, i) if i < 6 else (1, i - 6)
        settle(self.inbox[way].at[slot], self.recv.at[i])
        pltpu.make_async_copy(self.inbox[way].at[slot], self.stage[way][slot], self.load.at[i]).start()

    def fetched(self, i):
        way, slot = (0, i) if i < 6 else (1, i - 6)
        settle(self.stage[way][slot], self.load.at[i])

    def relay(self):
        for i in (0, 1, 9) if self.both else (0, 1):
            self.fetch(i)
        for i, k, half, step in ((0, 1, 0, 1), (1, 3, 1, 3)):
            self.fetched(i)
            base = ring(self.me.z, k) * 512 + half * 256

            def add(r, _):
                here = self.place(0, base + r * 64, 64)
                more = self.stage[0][i][pl.ds(pl.multiple_of(r * 64, 64), 64), :]
                self.grad[here] = (self.grad[here].astype(F32) + more.astype(F32)).astype(BF)
                return 0

            lax.fori_loop(0, 4, add, 0)
            self.go(4 + i, k, half, step)
        if self.both:
            self.relay_x()

    def second(self):
        me = self.me
        arrivals = range(2, 9 if self.both else 6)
        for i in arrivals:
            self.fetch(i)
        for i in arrivals:
            self.fetched(i)

        def add_z(r, _):
            rows = pl.ds(pl.multiple_of(r * 32, 32), 32)
            for half in (0, 1):
                here = self.place(0, me.z * 512 + half * 256 + r * 32, 32)
                total = self.grad[here].astype(F32)
                for i in (3 - half, 4 + half):
                    total = total + self.stage[0][i][rows, :].astype(F32)
                self.grad[here] = total.astype(BF)
                if not self.both:
                    continue
                rows_x = pl.ds(pl.multiple_of(half * 256 + r * 32, 32), 32)
                total = self.stage[1][0][rows_x, :].astype(F32)
                for i in (1, 2):
                    total = total + self.stage[1][i][rows_x, :].astype(F32)
                self.part[rows_x, :] = total.astype(BF)
            return 0

        lax.fori_loop(0, 8, add_z, 0)
        self.over_x(lambda xlo, c: self.grad.at[self.place(0, me.z * 512 + xlo * 256 + c * 128, 128)],
                    self.left.at[me.x], 10)
        for k in (1, 3, 2) if self.both else ():
            z = ring(me.z, k)
            remote(self.part.at[rows_at(z * 128, 128)], self.right.at[k - 1], self.send.at[13 + k],
                   self.recv.at[13 + k], me.at(z=z)).start()

    def third(self, store):
        me = self.me
        for i in range(4):
            settle(self.left.at[i], self.recv.at[10 + i])
        for k in (1, 2, 3) if self.both else ():
            settle(self.right.at[k - 1], self.recv.at[13 + k])

        def add(i, _):
            rows = pl.ds(pl.multiple_of(i * 32, 32), 32)
            left = self.left[0, rows, :].astype(F32)
            for x in range(1, 4):
                left = left + self.left[x, rows, :].astype(F32)
            store(rows, 0, left)
            if self.both:
                right = self.part[pl.ds(pl.multiple_of(me.z * 128 + i * 32, 32), 32), :].astype(F32)
                for k in range(3):
                    right = right + self.right[k, rows, :].astype(F32)
                store(rows, self.widths[0], right)
            return 0

        lax.fori_loop(0, 4, add, 0)

    def finish(self):
        me = self.me
        for i in range(6):
            settle(self.inbox[0].at[i], self.send.at[i])
        self.over_x_sent(self.left.at[0], 10)
        if not self.both:
            return
        for k in (1, 2, 3):
            settle(self.right.at[k - 1], self.send.at[13 + k])
        for xlo in (0, 1):
            for c in (0, 1):
                @pl.when(jnp.logical_or(me.x != me.c * 2 + xlo, me.c != c))
                def _():
                    settle(self.inbox[1].at[0], self.send.at[6 + xlo * 2 + c])


def dot_rows(left, right):
    return lax.dot_general(left, right, (((0,), (0,)), ((), ())), preferred_element_type=F32)


def back_norm(values, gain, upstream):
    entries = values.shape[-1]
    inverse = inverse_of(values)
    scaled = upstream * gain
    folded = jnp.sum(scaled * values, axis=-1, keepdims=True)
    grad = inverse * scaled - values * (inverse * inverse * inverse) * folded / entries
    return grad, jnp.sum(upstream * values * inverse, axis=0, keepdims=True)


def layer_kernel(
    tokens, cot, attn_gain, mlp_gain, query_gain, key_gain, wo, wq, wk, wv, wg, wu, wd, cosine, sine,
    result, tokens_grad, attn_gain_grad, mlp_gain_grad, query_gain_grad, key_gain_grad,
    qkv_grad, out_grad, gate_grad, up_grad, down_grad, n_out,
    box_q0, box_q1, box_k0, box_k1, box_o0, box_o1, box_g0, box_g1, box_u0, box_u1, box_d0, box_d1,
    n, cota, a, b, a_shard, b_shard, d_shard, da, h, dg, du, qlin, klin, qrot, kv, o, mid, cos, sin, dqkv, d_o, acc, acc_out, acc_in,
    sib_out, held, arrive, held2, arrive2,
    part_q, left_q, right_q, part_k, left_k, right_k, part_o, left_o, right_o, part_g, left_g, right_g,
    part_u, left_u, right_u, part_d, left_d, right_d, gain8, gainx, gainz, gacc,
    load, n_send, n_recv, c_send, c_recv, n2_send, n2_recv, da_send, da_recv,
    a_send, a_recv, o_send, o_recv, b_send, b_recv, w_send, w_recv, r_send, r_recv, r1_send, r1_recv, r2_send, r2_recv, r3_send, r3_recv,
    q_send, q_recv, k_send, k_recv, g_send, g_recv, u_send, u_recv, d_send, d_recv, p_send, p_recv,
    stage_load, kv_sem, swap_sem, v_send, v_recv,
):
    me = Place()
    barrier, count = greet(me)
    loads = {}

    def fetch(name, src, dst):
        loads[name] = pltpu.make_async_copy(src, dst, load.at[len(loads)])
        loads[name].start()

    for name, src, dst, col in (("wq", wq, a_shard, 0), ("wk", wk, a_shard, 256), ("wv", wv, a_shard, 384),
                                ("wg", wg, b_shard, 0), ("wu", wu, b_shard, 768), ("wd", wd, d_shard, 0)):
        fetch(name, src, dst.at[:, pl.ds(col, src.shape[1])])
    fetch("cos", cosine.at[me.xhi], cos)
    fetch("sin", sine.at[me.xhi], sin)
    own = (me.c * 4 + me.y) * BLOCK

    def norm_one(i, _):
        rows = pl.ds(pl.multiple_of(i * 16, 16), 16)
        x = tokens[rows, :].astype(F32)
        n[pl.ds(pl.multiple_of(own + i * 16, 16), 16), :] = (x * inverse_of(x) * attn_gain[...]).astype(BF)
        return 0

    lax.fori_loop(0, 8, norm_one, 0)
    cota[rows_at(own, BLOCK), :] = cot[...]
    for name in ("wq", "wk", "wv", "wg", "wu", "wd"):
        loads[name].wait()
    pl.semaphore_wait(barrier, count)

    weights_a = GatherWeights(me, a_shard, a, 0, 384, 512, a_send, a_recv)
    weights_o = GatherWeights(me, wo, a, 512, 256, 256, o_send, o_recv)
    weights_b = GatherWeights(me, b_shard, b, 0, B_CUT, 1536, b_send, b_recv)
    weights_d = GatherWeights(me, d_shard, b, 1536, D_CUT, 768, w_send, w_recv)
    rows_n = GatherRows(me, n, n_send, n_recv)
    rows_c = GatherRows(me, cota, c_send, c_recv)
    rows_n2 = GatherRows(me, n, n2_send, n2_recv)
    rows_n.start()
    weights_a.first(0)
    weights_a.first(1)
    weights_o.first(0)
    weights_a.second_z()
    weights_a.second_x()
    rows_n.relay()
    weights_a.relay()
    weights_a.relay_x()
    weights_o.second_z()
    weights_d.first(0)
    weights_b.first(0)
    rows_n.finish()
    rows_c.start()
    weights_a.arrived()
    weights_o.relay()
    weights_d.first(1)
    weights_b.first(1)
    n_save = pltpu.make_async_copy(n, n_out, load.at[8])
    n_save.start()
    loads["cos"].wait()
    loads["sin"].wait()

    def project(s):
        rows = rows_at(s * 512, 512)
        x = n[rows, :]
        k = dot(x, a[:, 256:512])
        klin[rows, :] = k[:, 0:128]
        u = k[:, 0:128]
        u = turn(u * inverse_of(u) * key_gain[...], cos[...], sin[...]).astype(BF)
        v = k[:, 128:256].astype(BF)
        for block in range(4):
            kv[0, s, block, 0] = u[block * 128:(block + 1) * 128]
            kv[1, s, block, 0] = v[block * 128:(block + 1) * 128]

    def project_q(s):
        rows = rows_at(s * 512, 512)
        q = dot(n[rows, :], a[:, 0:256])
        qlin[rows, :] = q
        for g in (0, 1):
            u = q[:, g * 128:(g + 1) * 128]
            u = turn(u * inverse_of(u) * query_gain[...], cos[...], sin[...]).astype(BF)
            for block in range(4):
                qrot[rows_at(s * 1024 + block * 256 + g * 128, 128), :] = u[block * 128:(block + 1) * 128]

    order = (1 - me.c, me.c)
    swaps = []
    for i, s in enumerate(order):
        project(s)
        swap = remote(kv.at[:, s, :, 0], kv.at[:, s, :, 1], kv_sem.at[i], kv_sem.at[2 + i], me.at(x=ring(me.x, 2)))
        swap.start()
        swaps.append(swap)
    for s in order:
        project_q(s)
    rows_c.relay()
    weights_d.second_z()
    weights_b.second_z()

    def attend(s):
        for block in range(4):
            size = (block + 1) * 256
            q = qrot[rows_at(s * 1024 + block * 256, 256), :]
            weights = jnp.exp2(dot_t(q, kv[0, s, 0:block + 1].reshape(size, 128)) * SCORE2)
            row = lax.rem(lax.broadcasted_iota(jnp.int32, (256, 256), 0), 128)
            col = lax.broadcasted_iota(jnp.int32, (256, 256), 1)
            weights = mask_last(weights, jnp.logical_or(col <= row, col >= 256 - 128 * me.xhi), 1)
            total = jnp.sum(weights, axis=-1, keepdims=True)
            got = dot(weights.astype(BF), kv[1, s, 0:block + 1].reshape(size, 128))
            got = (got / total).astype(BF)
            rows = rows_at(s * 512 + block * 128, 128)
            o[rows, 0:128] = got[0:128]
            o[rows, 128:256] = got[128:256]

    sums = ReduceRows(me, sib_out, held, arrive, r_send, r_recv)

    def branch(row, j):
        return dot_t(o[rows_at(row, 256), :], a[rows_at(j * 512, 512), 512:768])

    swaps[0].wait()
    attend(order[0])
    weights_o.arrived()
    n_save.wait()
    sums.other(branch)
    swaps[1].wait()
    attend(order[1])
    sums.mine(branch)
    weights_d.second_x()
    sums.relay()
    weights_b.second_x()
    rows_c.finish()
    weights_d.relay()
    weights_d.relay_x()
    weights_b.relay()
    sums.wait()

    def norm_two(i, _):
        rows = pl.ds(pl.multiple_of(i * 16, 16), 16)
        x = tokens[rows, :].astype(F32) + sums.total(i * 16)
        mid[rows, :] = x
        n[pl.ds(pl.multiple_of(own + i * 16, 16), 16), :] = (x * inverse_of(x) * mlp_gain[...]).astype(BF)
        return 0

    lax.fori_loop(0, 8, norm_two, 0)
    rows_n2.start()
    sums.free()
    sums.finish()
    rows_n2.relay()
    weights_b.relay_x()
    weights_d.arrived()

    def hidden_back(i, _):
        rows = rows_at(i * 512, 512)
        for j in range(3):
            cols = slice(j * 256, j * 256 + 256)
            du[rows, cols] = dot(cota[rows, :], b[:, 1536 + j * 256:1792 + j * 256]).astype(BF)
        return 0

    lax.fori_loop(0, 2, hidden_back, 0)
    rows_n2.finish()
    weights_b.arrived()
    for weights in (weights_a, weights_o, weights_b, weights_d):
        weights.finish()

    def hidden(j, i):
        rows = rows_at(i * 512, 512)
        cols = slice(j * 256, j * 256 + 256)
        gate = dot(n[rows, :], b[:, cols])
        up = dot(n[rows, :], b[:, 768 + j * 256:1024 + j * 256])
        d_hidden = du[rows, cols].astype(F32)
        sg = jax.nn.sigmoid(gate)
        active = gate * sg
        h[rows, cols] = (active * up).astype(BF)
        dg[rows, cols] = (d_hidden * up * sg * (1.0 + gate * (1.0 - sg))).astype(BF)
        du[rows, cols] = (d_hidden * active).astype(BF)

    for j in range(3):
        lax.fori_loop(0, 2, lambda i, _, j=j: (hidden(j, i), 0)[1], 0)
    sum_n2 = ReduceRows(me, sib_out, held, arrive, r1_send, r1_recv)
    sum_result = ReduceRows(me, sib_out, held2, arrive2, r2_send, r2_recv)
    sum_n = ReduceRows(me, sib_out, held, arrive, r3_send, r3_recv)

    def back_n2(row, j):
        rows, model = rows_at(row, 256), rows_at(j * 512, 512)
        return dot_t(dg[rows, :], b[model, 0:768]) + dot_t(du[rows, :], b[model, 768:1536])

    def down(row, j):
        return dot_t(h[rows_at(row, 256), :], b[rows_at(j * 512, 512), 1536:2304])

    sum_n2.other(back_n2)
    sum_n2.mine(back_n2)
    def stages(first, second):
        quarter = [(buf, r) for buf in (dg, du) for r in range(4)]
        return ([buf.at[pl.ds(r * 256, 256), pl.ds(0, first)] for buf, r in quarter[:6]],
                [buf.at[pl.ds(r * 512, 512), pl.ds(384, max(second, 128))] for buf in (dg, du) for r in (0, 1)])

    def reduction(grad, col, widths, boxes, sums, sems, fold=0):
        return ReduceWeights(me, grad, col, widths, boxes, stages(*widths), *sums, *sems, stage_load, fold)

    red_g = reduction(b, 0, WIDE, (box_g0, box_g1), (part_g, left_g, right_g), (g_send, g_recv))
    red_u = reduction(b, 768, WIDE, (box_u0, box_u1), (part_u, left_u, right_u), (u_send, u_recv))
    red_d = reduction(b, 1536, WIDE, (box_d0, box_d1), (part_d, left_d, right_d), (d_send, d_recv))
    red_o = reduction(a, 512, ONE_WAY, (box_o0, box_o1), (part_o, left_o, right_o), (p_send, p_recv))
    red_q = reduction(n, 0, ONE_WAY, (box_q0, box_q1), (part_q, left_q, right_q), (q_send, q_recv), 256)
    red_k = reduction(n, 512, NARROW, (box_k0, box_k1), (part_k, left_k, right_k), (k_send, k_recv), 256)

    def weight_grad(red, left, right, unroll=False, cols=None):
        def step(i, _):
            rows = rows_at(i * 256, 256)
            value = dot_rows(left[:, rows], right[...])
            red.store(i, value)
            if cols is not None:
                terms = value * a[rows, cols].astype(F32)
                terms = terms[:, 0:128] + terms[:, 128:256]
                gacc[:, rows] += jnp.sum(terms.T, axis=0, keepdims=True)
            return 0

        lax.fori_loop(0, 8, step, 0, unroll=unroll)
        red.first()

    weight_grad(red_g, n, dg)
    sum_n2.relay()
    weight_grad(red_u, n, du)
    sum_n2.free()
    sum_result.other(down)
    sum_result.mine(down, send=False)
    sum_n2.wait()
    rows_da = GatherRows(me, da, da_send, da_recv)

    def back_two(i, total):
        rows = pl.ds(pl.multiple_of(i * 16, 16), 16)
        grad, gain = back_norm(mid[rows, :], mlp_gain[...], sum_n2.total(i * 16))
        grad = grad + cot[rows, :].astype(F32)
        tokens_grad[rows, :] = grad
        da[pl.ds(pl.multiple_of(own + i * 16, 16), 16), :] = grad.astype(BF)
        return total + gain

    mlp_part = lax.fori_loop(0, 8, back_two, jnp.zeros((1, WIDTH), F32))
    rows_da.start()
    slot = me.c * 4 + me.y

    def spread(value, col):
        for i in range(8):
            gainx[me.x, i:i + 1, col:col + 256] = value[:, i * 256:(i + 1) * 256]

    gainx[me.x] = jnp.zeros((8, 640), F32)
    spread(mlp_part, 256)
    gacc[...] = jnp.zeros_like(gacc)
    sum_n2.finish()
    red_g.relay()
    weight_grad(red_d, cota, h)
    n_load = pltpu.make_async_copy(n_out, cota, load.at[9])
    n_load.start()
    rows_da.relay()
    red_u.relay()
    red_g.second()
    rows_da.finish()

    def back_o(i, _):
        rows = rows_at(i * 512, 512)
        d_o[rows, :] = dot(da[rows, :], a[:, 512:768]).astype(BF)
        return 0

    lax.fori_loop(0, 2, back_o, 0)
    sum_result.send_all()

    swaps = []
    q_gain = jnp.zeros((1, HEAD), F32)
    for turn_ in (0, 1):
        s = 1 - me.c if turn_ == 0 else me.c
        flat = kv[0, s].reshape(1024, 128).T
        key = lax.broadcasted_iota(jnp.int32, (256, 256), 0)
        query = lax.rem(lax.broadcasted_iota(jnp.int32, (256, 256), 1), 128)
        keep = jnp.logical_or(key <= query, key >= 256 - 128 * me.xhi)
        dqs = {}
        for pair in ((3, 0), (2, 1)):
            sizes = [(block + 1) * 256 for block in pair]
            qs = [qrot[rows_at(s * 1024 + block * 256, 256), :] for block in pair]
            gs = []
            for block in pair:
                rows = rows_at(s * 512 + block * 128, 128)
                gs.append(jnp.concatenate([d_o[rows, 0:128], d_o[rows, 128:256]], axis=0))
            ks = [kv[0, s, 0:block + 1].reshape(size, 128) for block, size in zip(pair, sizes)]
            vs = [kv[1, s, 0:block + 1].reshape(size, 128) for block, size in zip(pair, sizes)]
            ps = [mask_last(jnp.exp2(dot_t(k, q) * SCORE2), keep, 0) for k, q in zip(ks, qs)]
            dps = [dot_t(v, g) for v, g in zip(vs, gs)]
            ps = [p * (1.0 / jnp.sum(p, axis=0, keepdims=True)) for p in ps]
            dss = [(p * (dp - jnp.sum(dp * p, axis=0, keepdims=True))).astype(BF) for p, dp in zip(ps, dps)]
            for block, size, ds in zip(pair, sizes, dss):
                dqs[block] = (dot(flat[:, :size], ds) * SCORE).T
            dks = [dot(ds, q) * SCORE for ds, q in zip(dss, qs)]
            dvs = [dot(p.astype(BF), g) for p, g in zip(ps, gs)]
            for block, dk, dv in zip(pair, dks, dvs):
                for i, value in enumerate((dk, dv)):
                    value = value.reshape(block + 1, 2, 128, 128)
                    if block == 3:
                        acc[i, s] = value
                    else:
                        acc[i, s, 0:block + 1] += value
        rows = rows_at(s * 512, 512)
        for head in (0, 1):
            dq = jnp.concatenate([dqs[block][head * 128:(head + 1) * 128] for block in range(4)], axis=0)
            up = turn(dq, cos[...], -sin[...])
            grad, gain = back_norm(qlin[rows, head * 128:(head + 1) * 128], query_gain[...], up)
            dqkv[rows, head * 128:(head + 1) * 128] = grad.astype(BF)
            q_gain = q_gain + gain
        for i in (0, 1):
            acc_out[turn_, i] = acc[i, s, :, 1].astype(BF)
        swap = remote(acc_out.at[turn_], acc_in.at[turn_], swap_sem.at[turn_], swap_sem.at[2 + turn_],
                      me.at(x=ring(me.x, 2)))
        swap.start()
        swaps.append(swap)
    red_d.relay()
    weight_grad(red_o, da, o, True)
    n_load.wait()
    weight_grad(red_q, cota, dqkv.at[:, pl.ds(0, 256)], True, slice(0, 256))
    sum_result.relay()

    k_gain = jnp.zeros((1, HEAD), F32)

    def back_n(row, j):
        rows, model = rows_at(row, 256), rows_at(j * 512, 512)
        return dot_t(dqkv[rows, 0:256], a[model, 0:256]) + dot_t(dqkv[rows, 256:512], a[model, 256:512])

    for turn_ in (0, 1):
        s = 1 - me.c if turn_ == 0 else me.c
        rows = rows_at(s * 512, 512)
        swaps[turn_].wait()
        dk = (acc[0, s, :, 0] + acc_in[turn_, 0].astype(F32)).reshape(512, 128)
        dv = (acc[1, s, :, 0] + acc_in[turn_, 1].astype(F32)).reshape(512, 128)
        grad, gain = back_norm(klin[rows, :], key_gain[...], turn(dk, cos[...], -sin[...]))
        k_gain = k_gain + gain
        dqkv[rows, 256:384] = grad.astype(BF)
        dqkv[rows, 384:512] = dv.astype(BF)
        if turn_ == 0:
            sum_result.free()
            sum_n.other(back_n)
        else:
            sum_n.mine(back_n)
    weight_grad(red_k, cota, dqkv.at[:, pl.ds(256, 256)], True, slice(256, 512))
    spread(gacc[...] / attn_gain[...], 0)
    gainx[me.x, 0:1, 512:640] = q_gain
    gainx[me.x, 1:2, 512:640] = k_gain
    for k in (1, 2, 3):
        remote(gainx.at[me.x], gainx.at[me.x], v_send.at[6 + k], v_recv.at[8 + me.x], me.at(x=ring(me.x, k))).start()
    red_o.relay()
    red_q.relay()
    red_d.second()
    sum_n.relay()
    for i in range(4):
        @pl.when(me.x != i)
        def _():
            settle(gainx.at[i], v_recv.at[8 + i])
    gainz[me.z] = gainx[0] + gainx[1] + gainx[2] + gainx[3]
    for k in (1, 2, 3):
        remote(gainz.at[me.z], gainz.at[me.z], v_send.at[9 + k], v_recv.at[12 + me.z], me.at(z=ring(me.z, k))).start()
    red_k.relay()
    red_o.second()
    red_u.second()
    for i in range(4):
        @pl.when(me.z != i)
        def _():
            settle(gainz.at[i], v_recv.at[12 + i])
    gain8[slot] = gainz[0] + gainz[1] + gainz[2] + gainz[3]
    peers = [(me.y, 1 - me.c)] + [(ring(me.y, k), c) for k in (1, 2, 3) for c in (0, 1)]
    for i, (y, c) in enumerate(peers):
        remote(gain8.at[slot], gain8.at[slot], v_send.at[i], v_recv.at[slot], me.at(y=y, c=c)).start()
    red_q.second()

    def put(ref, first=0):
        def store(rows, col, value):
            ref[rows, first + col:first + col + value.shape[1]] = value
        return store

    red_k.second()
    sum_result.wait()

    def finish_result(i, _):
        rows = pl.ds(pl.multiple_of(i * 16, 16), 16)
        result[rows, :] = (mid[rows, :] + sum_result.total(i * 16)).astype(BF)
        return 0

    lax.fori_loop(0, 8, finish_result, 0)
    red_g.third(put(gate_grad))
    red_d.third(put(down_grad))
    sum_n.wait()

    def back_one(i, _):
        rows = pl.ds(pl.multiple_of(i * 16, 16), 16)
        grad, _ = back_norm(tokens[rows, :].astype(F32), attn_gain[...], sum_n.total(i * 16))
        tokens_grad[rows, :] += grad
        return 0

    lax.fori_loop(0, 8, back_one, 0)
    red_u.third(put(up_grad))
    red_o.third(put(out_grad))
    red_q.third(put(qkv_grad))
    for i in range(8):
        @pl.when(slot != i)
        def _():
            settle(gain8.at[i], v_recv.at[i])
    total = gain8[0]
    for i in range(1, 8):
        total = total + gain8[i]
    for i in range(8):
        cols = slice(i * 256, i * 256 + 256)
        attn_gain_grad[:, cols] = total[i:i + 1, 0:256]
        mlp_gain_grad[:, cols] = total[i:i + 1, 256:512]
    query_gain_grad[...] = total[0:1, 512:640]
    key_gain_grad[...] = total[1:2, 512:640]
    red_k.third(put(qkv_grad, 256))
    for i in range(13):
        settle(gain8.at[0], v_send.at[i])
    sum_result.finish()
    sum_n.free()
    sum_n.finish()
    for red in (red_g, red_u, red_d, red_o, red_q, red_k):
        red.finish()


def layer(tokens, cot, gains, weights, cos, sin):
    wq, wk, wv, wo, wg, wu, wd = weights
    args = (tokens, cot) + gains + (wo, wq, wk, wv, wg, wu, wd, cos, sin)
    vmem = pl.BlockSpec(memory_space=pltpu.VMEM)
    hbm = pl.BlockSpec(memory_space=pl.ANY)
    outs = [((BLOCK, WIDTH), BF), ((BLOCK, WIDTH), F32), ((1, WIDTH), F32), ((1, WIDTH), F32)]
    outs += [((1, HEAD), F32), ((1, HEAD), F32), ((BLOCK, 512), F32), ((BLOCK, 256), F32)]
    outs += [((BLOCK, 768), F32)] * 3
    widths = [(w[0], max(w[1], 128)) for w in (ONE_WAY, NARROW, ONE_WAY, WIDE, WIDE, WIDE)]
    boxes = [((ROWS, WIDTH), BF)]
    boxes += [box for w in widths for box in (((6, 256, w[0]), BF), ((4, 512, w[1]), BF))]
    scratch = [
        ((ROWS, WIDTH), BF), ((ROWS, WIDTH), BF), ((WIDTH, A_COLS), BF), ((WIDTH, B_COLS), BF),
        ((BLOCK, 512), BF), ((BLOCK, 1536), BF), ((BLOCK, 768), BF), ((ROWS, WIDTH), BF),
        ((ROWS, 768), BF), ((ROWS, 768), BF), ((ROWS, 768), BF), ((ROWS, 256), F32), ((ROWS, 128), F32),
        ((2 * ROWS, 128), BF), (KV_SHAPE, BF), ((ROWS, 256), BF), ((BLOCK, WIDTH), F32),
        ((512, 128), F32), ((512, 128), F32), ((ROWS, 512), BF), ((ROWS, 256), BF), (KV_SHAPE, F32),
        ((2, 2, 4, 128, 128), BF), ((2, 2, 4, 128, 128), BF),
        ((512, WIDTH), BF), ((512, WIDTH), BF), ((6, 64, WIDTH), BF), ((512, WIDTH), BF), ((6, 64, WIDTH), BF),
    ]
    for w in widths:
        scratch += [((512, w[1]), BF), ((4, BLOCK, w[0]), BF), ((3, BLOCK, w[1]), BF)]
    scratch += [((8, 8, 640), F32), ((4, 8, 640), F32), ((4, 8, 640), F32), ((1, WIDTH), F32)]
    scratch = [pltpu.VMEM(s, d) for s, d in scratch]
    dma = pltpu.SemaphoreType.DMA
    scratch += [dma((10,))] + [dma((GatherRows.sems,))] * 8 + [dma((GatherWeights.sems,))] * 8 + [dma((8,))] * 8
    scratch += [dma((ReduceWeights.sems,))] * 12 + [dma((10,)), dma((4,)), dma((4,)), dma((13,)), dma((16,))]
    got = pl.pallas_call(
        layer_kernel,
        out_shape=[jax.ShapeDtypeStruct(s, d) for s, d in outs + boxes],
        in_specs=[vmem] * 7 + [hbm] * 8,
        out_specs=[vmem] * len(outs) + [hbm] * len(boxes),
        scratch_shapes=scratch,
        compiler_params=pltpu.CompilerParams(
            collective_id=1, has_side_effects=True, vmem_limit_bytes=VMEM_BYTES),
        name="layer_part",
    )(*args)
    return got[:len(outs)]


def finish_kernel(*refs):
    parts, outs, held, sem, out_sem = refs[:11], refs[11:24], refs[24:37], refs[37], refs[38]
    qkv = parts[6]
    sources = parts[:6] + tuple(qkv.at[:, pl.ds(*cols)] for cols in ((0, 256), (256, 128), (384, 128))) + parts[7:]
    ins = [pltpu.make_async_copy(src, dst, sem.at[i]) for i, (src, dst) in enumerate(zip(sources, held))]
    backs = [pltpu.make_async_copy(src, dst, out_sem.at[i]) for i, (src, dst) in enumerate(zip(held, outs))]
    for copy in ins:
        copy.start()
    for copy, back in zip(ins, backs):
        copy.wait()
        back.start()
    for back in backs:
        back.wait()


def finish(parts):
    shapes = [((BLOCK, WIDTH), BF), ((BLOCK, WIDTH), F32), ((1, WIDTH), F32), ((1, WIDTH), F32), ((1, HEAD), F32)]
    shapes += [((1, HEAD), F32), ((BLOCK, 256), F32), ((BLOCK, 128), F32), ((BLOCK, 128), F32), ((BLOCK, 256), F32)]
    shapes += [((BLOCK, 768), F32)] * 3
    return pl.pallas_call(
        finish_kernel,
        out_shape=[jax.ShapeDtypeStruct(s, d) for s, d in shapes],
        in_specs=[pl.BlockSpec(memory_space=pl.ANY)] * len(parts),
        out_specs=[pl.BlockSpec(memory_space=pl.ANY)] * len(shapes),
        scratch_shapes=[pltpu.VMEM(s, d) for s, d in shapes] + [pltpu.SemaphoreType.DMA((13,))] * 2,
        compiler_params=pltpu.CompilerParams(vmem_limit_bytes=VMEM_BYTES),
        name="finish_part",
    )(*parts)


def local(tokens, cotangent, attn_gain, mlp_gain, query_gain, key_gain, *weights):
    cos, sin = rope_tables()
    gains = (attn_gain[None], mlp_gain[None], query_gain[None], key_gain[None])
    outs = finish(layer(tokens, cotangent, gains, weights, cos, sin))
    return tuple(outs[:2]) + tuple(g[0] for g in outs[2:6]) + tuple(outs[6:])


def solution(mesh):
    rows, plane = P(("dp", "tensor"), None), P("dp", "tensor")
    return jax.shard_map(
        local,
        mesh=mesh,
        in_specs=(rows, rows, P(), P(), P(), P()) + (plane,) * 7,
        out_specs=(rows, rows, P(), P(), P(), P()) + (plane,) * 7,
        check_vma=False,
    )
```

```python
import functools

import numpy as np
import jax
import jax.numpy as jnp
from jax import lax
from jax.experimental import pallas as pl
from jax.experimental.pallas import tpu as pltpu
from jax.sharding import PartitionSpec as P

EPS = 1e-06
ROPE_BASE = 1000000.0
MESH = pl.DeviceIdType.MESH
BF = jnp.bfloat16
F32 = jnp.float32
HEAD = 128
WIDTH = 2048
BLOCK = 128
ROWS = 1024
A_COLS = 768
B_COLS = 2304
B_CUT = 896
D_CUT = 384
SCORE = HEAD ** -0.5
KV_SHAPE = (2, 2, 4, 2, 128, 128)
SCORE2 = HEAD ** -0.5 * 1.4426950408889634
VMEM_BYTES = 63 * 2**20


class Place:
    def __init__(self):
        dp = lax.axis_index("dp")
        tensor = lax.axis_index("tensor")
        self.dp = dp
        self.xlo = lax.div(dp, 8)
        self.z = lax.rem(lax.div(dp, 2), 4)
        self.c = lax.rem(dp, 2)
        self.y = lax.div(tensor, 2)
        self.xhi = lax.rem(tensor, 2)
        self.x = self.xhi * 2 + self.xlo

    def at(self, x=None, y=None, z=None, c=None):
        x = self.x if x is None else x
        y = self.y if y is None else y
        z = self.z if z is None else z
        c = self.c if c is None else c
        return (lax.rem(x, 2) * 8 + z * 2 + c, y * 2 + lax.div(x, 2))

    def sibling(self):
        return self.at(c=1 - self.c)


def ring(v, k):
    return lax.rem(v + k, 4)


def remote(src, dst, send_sem, recv_sem, target):
    return pltpu.make_async_remote_copy(
        src_ref=src, dst_ref=dst, send_sem=send_sem, recv_sem=recv_sem,
        device_id=target, device_id_type=MESH,
    )


def settle(ref, sem):
    pltpu.make_async_copy(ref, ref, sem).wait()


def rows_at(start, size):
    return pl.ds(pl.multiple_of(start, 128), size)


def greet(me):
    barrier = pltpu.get_barrier_semaphore()
    others = [me.sibling()]
    for k in (1, 2, 3):
        others.append(me.at(y=ring(me.y, k)))
        others.append(me.at(y=ring(me.y, k), c=1 - me.c))
        for c in (0, 1):
            others.append(me.at(x=ring(me.x, k), c=c))
            others.append(me.at(z=ring(me.z, k), c=c))
    for other in others:
        pl.semaphore_signal(barrier, inc=1, device_id=other, device_id_type=MESH)
    return barrier, len(others)


class GatherRows:
    sems = 13

    def __init__(self, me, buf, send, recv):
        self.me, self.buf, self.send, self.recv = me, buf, send, recv

    def piece(self, c, y, half):
        return self.buf.at[pl.ds(pl.multiple_of((c * 4 + y) * BLOCK + half * 64, 64), 64)]

    def go(self, y, half, i, target):
        ref = self.piece(self.me.c, y, half)
        remote(ref, ref, self.send.at[i], self.recv.at[i], target).start()

    def start(self):
        me = self.me
        up, down = me.at(y=ring(me.y, 1)), me.at(y=ring(me.y, 3))
        self.go(me.y, 0, 0, up)
        self.go(me.y, 1, 2, down)
        own = self.buf.at[rows_at((me.c * 4 + me.y) * BLOCK, BLOCK)]
        remote(own, own, self.send.at[6], self.recv.at[6], me.sibling()).start()

    def heard(self, i, k, half):
        me = self.me
        y = ring(me.y, 4 - k)
        settle(self.piece(me.c, y, half), self.recv.at[i])
        self.go(y, half, 7 + i, me.sibling())
        return y

    def relay(self):
        me = self.me
        up, down = me.at(y=ring(me.y, 1)), me.at(y=ring(me.y, 3))
        half = self.piece(me.c, me.y, 0)
        settle(half, self.send.at[0])
        self.go(me.y, 1, 1, up)
        settle(half, self.send.at[2])
        self.go(me.y, 0, 3, down)
        y = self.heard(0, 1, 0)
        self.go(y, 0, 4, up)
        y = self.heard(2, 3, 1)
        self.go(y, 1, 5, down)

    def own_blocks(self):
        self.heard(1, 1, 1)
        self.heard(3, 3, 0)
        self.heard(4, 2, 0)
        self.heard(5, 2, 1)

    def finish(self):
        me = self.me
        half = self.piece(me.c, me.y, 0)
        own = self.buf.at[rows_at((me.c * 4 + me.y) * BLOCK, BLOCK)]
        for i in (1, 3, 4, 5, 6, 7, 8, 9, 10, 11, 12):
            settle(own if i == 6 else half, self.send.at[i])
        for i in range(6, 13):
            settle(own if i == 6 else half, self.recv.at[i])


class ReduceRows:
    def __init__(self, me, sib_out, held, arrive, send, recv):
        self.me = me
        self.sib_out, self.held, self.arrive = sib_out, held, arrive
        self.send, self.recv = send, recv
        first = 1 - lax.div(me.y, 2)
        self.halves = (first, 1 - first)

    def other(self, tile):
        me = self.me
        for p, half in enumerate(self.halves):
            rows = rows_at(half * 256, 256)

            def step(j, _):
                cols = rows_at(j * 512, 512)
                self.sib_out[rows, cols] = tile((1 - me.c) * 512 + half * 256, j).astype(BF)
                return 0

            lax.fori_loop(0, 4, step, 0, unroll=True)
            remote(self.sib_out.at[rows], self.held.at[rows], self.send.at[6 + p], self.recv.at[6 + p],
                   me.sibling()).start()

    def piece(self, k, half):
        return pl.ds(pl.multiple_of(ring(self.me.y, k) * BLOCK + half * 64, 64), 64)

    def go(self, i, k, half, step):
        remote(self.held.at[self.piece(k, half)], self.arrive.at[i], self.send.at[i], self.recv.at[i],
               self.me.at(y=ring(self.me.y, step))).start()

    def mine(self, tile, send=True):
        me = self.me
        for p, half in enumerate(self.halves):
            rows = rows_at(half * 256, 256)
            settle(self.held.at[rows], self.recv.at[6 + p])

            def step(j, _):
                cols = rows_at(j * 512, 512)
                total = tile(me.c * 512 + half * 256, j) + self.held[rows, cols].astype(F32)
                self.held[rows, cols] = total.astype(BF)
                return 0

            lax.fori_loop(0, 4, step, 0, unroll=True)
            if not send:
                continue
            even = lax.rem(me.y, 2) == 0
            if p == 0:
                self.go(0, 2, 0, 1)
                self.go(1, 2, 1, 3)
            pl.when(even if p == 0 else jnp.logical_not(even))(lambda: self.go(3, 3, 0, 3))
            pl.when(jnp.logical_not(even) if p == 0 else even)(lambda: self.go(2, 1, 1, 1))

    def send_all(self):
        self.go(0, 2, 0, 1)
        self.go(1, 2, 1, 3)
        self.go(2, 1, 1, 1)
        self.go(3, 3, 0, 3)

    def relay(self):
        for i, k, half, step in ((0, 1, 0, 1), (1, 3, 1, 3)):
            settle(self.arrive.at[i], self.recv.at[i])
            rows = self.piece(k, half)
            self.held[rows, :] = (self.held[rows, :].astype(F32) + self.arrive[i].astype(F32)).astype(BF)
            self.go(4 + i, k, half, step)

    def wait(self):
        for i in range(2, 6):
            settle(self.arrive.at[i], self.recv.at[i])

    def total(self, r):
        half = lax.div(r, 64)
        rows = pl.ds(pl.multiple_of(r - half * 64, 16), 16)
        total = self.held[pl.ds(pl.multiple_of(self.me.y * BLOCK + r, 16), 16), :].astype(F32)
        return total + self.arrive[3 - half, rows, :].astype(F32) + self.arrive[4 + half, rows, :].astype(F32)

    def free(self):
        for p in (0, 1):
            settle(self.sib_out.at[rows_at(0, 256)], self.send.at[6 + p])

    def finish(self):
        for i in range(6):
            settle(self.arrive.at[i], self.send.at[i])


class GatherWeights:
    sems = 23

    def __init__(self, me, shard, full, col, cut, width, send, recv):
        self.me, self.shard, self.full = me, shard, full
        self.cols = (pl.ds(col, cut), pl.ds(col + cut, width - cut))
        self.from_cols = (pl.ds(0, cut), pl.ds(cut, width - cut))
        self.send, self.recv = send, recv
        self.ways = (0, 1) if cut < width else (0,)

    def slot(self, way, dp):
        return self.full.at[rows_at(dp * BLOCK, BLOCK), self.cols[way]]

    def first(self, way):
        me = self.me
        home = me.xhi
        src = self.shard.at[:, self.from_cols[way]]
        dst = self.slot(way, me.dp)
        inbox = self.recv.at[(me.xlo * 2 + me.c) if way == 0 else (10 + me.z * 2 + me.c)]
        base = 0 if way == 0 else 10
        for k in (1, 3, 2):
            target = me.at(x=ring(me.x, k), c=home) if way == 0 else me.at(z=ring(me.z, k), c=home)
            remote(src, dst, self.send.at[base + k], inbox, target).start()

        @pl.when(me.c == home)
        def _():
            pltpu.make_async_copy(src, dst, inbox).start()

        @pl.when(me.c != home)
        def _():
            remote(src, dst, self.send.at[base], inbox, me.sibling()).start()

    def second_z(self):
        me = self.me
        for xlo in (0, 1):
            for c in (0, 1):
                settle(self.slot(0, xlo * 8 + me.z * 2 + c), self.recv.at[xlo * 2 + c])
        self.go(0, me.z, 4, 1)
        self.go(1, me.z, 6, 3)
        self.go(1, me.z, 5, 1)
        self.go(0, me.z, 7, 3)

    def go(self, xlo, z, i, step):
        ref = self.pair(xlo, z)
        remote(ref, ref, self.send.at[i], self.recv.at[i], self.me.at(z=ring(self.me.z, step))).start()

    def relay(self):
        me = self.me
        for i, xlo, step in ((4, 0, 1), (6, 1, 3)):
            z = ring(me.z, 4 - step)
            settle(self.pair(xlo, z), self.recv.at[i])
            self.go(xlo, z, 8 + xlo, step)

    def second_x(self):
        me = self.me
        if 1 not in self.ways:
            return

        @pl.when(me.c == me.xhi)
        def _():
            for z in range(4):
                for c in (0, 1):
                    settle(self.slot(1, me.xlo * 8 + z * 2 + c), self.recv.at[10 + z * 2 + c])
            for i, (part, step) in enumerate(((0, 1), (1, 3), (1, 1), (0, 3))):
                self.go_x(me.xlo, part, 18 + i, ring(me.x, step))

    def go_x(self, xlo, part, i, x):
        ref = self.quarter(xlo, part)
        remote(ref, ref, self.send.at[i], self.recv.at[18 + xlo * 2 + part], self.me.at(x=x)).start()

    def near_x(self):
        me = self.me
        below = lax.div(ring(me.x, 3), 2)
        up = 1 - (below + me.c - 2 * below * me.c)
        return up, lax.rem(ring(me.x, 1 + 2 * up), 2), 1 - up

    def relay_x(self):
        if 1 not in self.ways:
            return
        up, xlo, part = self.near_x()
        settle(self.quarter(0, 0), self.recv.at[18 + xlo * 2 + part])
        self.go_x(xlo, part, 22, ring(self.me.x, 3 - 2 * up))

    def pair(self, xlo, z):
        return self.full.at[rows_at(xlo * 1024 + z * 256, 256), self.cols[0]]

    def quarter(self, xlo, part):
        return self.full.at[rows_at(xlo * 1024 + part * 512, 512), self.cols[1]]

    def arrived(self):
        me = self.me
        for i in (5, 7, 8, 9):
            settle(self.pair(0, me.z), self.recv.at[i])
        if 1 not in self.ways:
            return
        _, near, near_part = self.near_x()
        for xlo in (0, 1):
            for part in (0, 1):
                here = jnp.logical_and(me.c == me.xhi, me.xlo == xlo)
                done = jnp.logical_and(near == xlo, near_part == part)

                @pl.when(jnp.logical_not(jnp.logical_or(here, done)))
                def _():
                    settle(self.quarter(0, 0), self.recv.at[18 + xlo * 2 + part])

    def finish(self):
        me = self.me
        for way in self.ways:
            src = self.shard.at[:, self.from_cols[way]]
            base = 0 if way == 0 else 10
            for k in (1, 2, 3):
                settle(src, self.send.at[base + k])

            @pl.when(me.c != me.xhi)
            def _():
                settle(src, self.send.at[base])
        for i in range(4, 10):
            settle(self.pair(0, me.z), self.send.at[i])

        if 1 not in self.ways:
            return

        @pl.when(me.c == me.xhi)
        def _():
            for i in range(18, 22):
                settle(self.quarter(0, 0), self.send.at[i])

        settle(self.quarter(0, 0), self.send.at[22])


def dot(left, right):
    return jnp.dot(left, right, preferred_element_type=F32)


def dot_t(left, right):
    return lax.dot_general(left, right, (((1,), (1,)), ((), ())), preferred_element_type=F32)


def inverse_of(values):
    return lax.rsqrt(jnp.mean(values * values, axis=-1, keepdims=True) + EPS)


def turn(values, cosine, sine):
    return values * cosine + pltpu.roll(values, 64, 1) * sine


def mask_last(values, keep, axis):
    size = values.shape[axis]
    last = jnp.where(keep, lax.slice_in_dim(values, size - 256, size, axis=axis), 0.0)
    if size == 256:
        return last
    return jnp.concatenate([lax.slice_in_dim(values, 0, size - 256, axis=axis), last], axis=axis)


def rope_tables():
    frequency = ROPE_BASE ** (-2.0 * np.arange(64, dtype=np.float64) / HEAD)
    angle = np.arange(1024, dtype=np.float64)[:, None] * frequency[None, :]
    cos = np.concatenate([np.cos(angle), np.cos(angle)], axis=1).astype(np.float32)
    sin = np.concatenate([-np.sin(angle), np.sin(angle)], axis=1).astype(np.float32)
    pick = lambda t: t.reshape(4, 2, 128, 128).transpose(1, 0, 2, 3).reshape(2, 512, 128)
    return pick(cos), pick(sin)


WIDE, NARROW, ONE_WAY = (384, 384), (128, 128), (256, 0)


class ReduceWeights:
    sems = 17

    def __init__(self, me, grad, first_col, widths, inbox, stage, part, left, right, send, recv, load, fold=0):
        self.me, self.grad, self.widths, self.fold = me, grad, widths, fold
        self.first_cols = (first_col, first_col + widths[0])
        self.both = widths[1] > 0
        self.inbox, self.stage, self.part, self.left, self.right = inbox, stage, part, left, right
        self.send, self.recv, self.load = send, recv, load

    def place(self, way, start, size):
        col = self.first_cols[way]
        if self.fold:
            high = lax.div(start, 1024)
            start = start - high * 1024
            col = pl.multiple_of(col + high * self.fold, 128)
        return pl.ds(pl.multiple_of(start, 32), size), pl.ds(col, self.widths[way])

    def store(self, i, value):
        xlo, z = lax.div(i, 4), lax.rem(i, 4)
        value = value.astype(BF)
        self.grad[self.place(0, z * 512 + xlo * 256, 256)] = value[:, :self.widths[0]]
        for c in (0, 1) if self.both else ():
            self.grad[self.place(1, (xlo * 2 + c) * 512 + z * 128, 128)] = value[
                c * 128:(c + 1) * 128, self.widths[0]:]

    def piece(self, k, half):
        return self.grad.at[self.place(0, ring(self.me.z, k) * 512 + half * 256, 256)]

    def go(self, i, k, half, step):
        remote(self.piece(k, half), self.inbox[0].at[i], self.send.at[i], self.recv.at[i],
               self.me.at(z=ring(self.me.z, step))).start()

    def over_x(self, sources, dst, base):
        me = self.me
        for xlo in (0, 1):
            for c in (0, 1):
                src = sources(xlo, c)
                x = me.c * 2 + xlo
                self_too = jnp.logical_and(me.x == x, me.c == c)

                @pl.when(self_too)
                def _():
                    pltpu.make_async_copy(src, dst, self.recv.at[base + me.x]).start()

                @pl.when(jnp.logical_not(self_too))
                def _():
                    remote(src, dst, self.send.at[base + xlo * 2 + c], self.recv.at[base + me.x],
                           me.at(x=x, c=c)).start()

    def over_x_sent(self, ref, base):
        me = self.me
        for xlo in (0, 1):
            for c in (0, 1):
                @pl.when(jnp.logical_or(me.x != me.c * 2 + xlo, me.c != c))
                def _():
                    settle(ref, self.send.at[base + xlo * 2 + c])

    def first(self):
        self.go(0, 2, 0, 1)
        self.go(1, 2, 1, 3)
        self.go(2, 1, 1, 1)
        self.go(3, 3, 0, 3)
        if not self.both:
            return
        me = self.me
        for xlo in (0, 1):
            x = me.c * 2 + xlo
            away = ring(me.x + 4 - x, 0)
            for c in (0, 1):
                there = me.at(x=x, c=c)

                @pl.when(jnp.logical_and(away == 0, me.c == c))
                def _():
                    pltpu.make_async_copy(self.share(xlo, c), self.inbox[1].at[0], self.recv.at[6]).start()

                @pl.when(jnp.logical_and(away == 0, me.c != c))
                def _():
                    self.go_x(xlo, c, 0, there)

                @pl.when(away == 2)
                def _():
                    self.go_x(xlo, c, 3, me.at(x=ring(me.x, 3 if c == 0 else 1)))

                @pl.when(away == (3 if c == 0 else 1))
                def _():
                    self.go_x(xlo, c, 2 if c == 0 else 1, there)

    def share(self, xlo, c):
        return self.grad.at[self.place(1, jnp.int32(0) + (xlo * 2 + c) * 512, 512)]

    def go_x(self, xlo, c, slot, target):
        remote(self.share(xlo, c), self.inbox[1].at[slot], self.send.at[6 + xlo * 2 + c], self.recv.at[6 + slot],
               target).start()

    def relay_x(self):
        me = self.me
        away = ring(me.x + 4 - me.c * 2, 0)
        xlo = 1 - lax.rem(away, 2)
        c = lax.div(ring(away + 4 - xlo, 0), 2)
        self.fetched(9)

        def add(r, _):
            here = self.place(1, (xlo * 2 + c) * 512 + r * 64, 64)
            more = self.stage[1][3][pl.ds(pl.multiple_of(r * 64, 64), 64), :]
            self.grad[here] = (self.grad[here].astype(F32) + more.astype(F32)).astype(BF)
            return 0

        lax.fori_loop(0, 8, add, 0)
        self.go_x(xlo, c, 1 + c, me.at(x=me.c * 2 + xlo, c=c))

    def fetch(self, i):
        way, slot = (0, i) if i < 6 else (1, i - 6)
        settle(self.inbox[way].at[slot], self.recv.at[i])
        pltpu.make_async_copy(self.inbox[way].at[slot], self.stage[way][slot], self.load.at[i]).start()

    def fetched(self, i):
        way, slot = (0, i) if i < 6 else (1, i - 6)
        settle(self.stage[way][slot], self.load.at[i])

    def relay(self):
        for i in (0, 1, 9) if self.both else (0, 1):
            self.fetch(i)
        for i, k, half, step in ((0, 1, 0, 1), (1, 3, 1, 3)):
            self.fetched(i)
            base = ring(self.me.z, k) * 512 + half * 256

            def add(r, _):
                here = self.place(0, base + r * 64, 64)
                more = self.stage[0][i][pl.ds(pl.multiple_of(r * 64, 64), 64), :]
                self.grad[here] = (self.grad[here].astype(F32) + more.astype(F32)).astype(BF)
                return 0

            lax.fori_loop(0, 4, add, 0)
            self.go(4 + i, k, half, step)
        if self.both:
            self.relay_x()

    def second(self):
        me = self.me
        arrivals = range(2, 9 if self.both else 6)
        for i in arrivals:
            self.fetch(i)
        for i in arrivals:
            self.fetched(i)

        def add_z(r, _):
            rows = pl.ds(pl.multiple_of(r * 32, 32), 32)
            for half in (0, 1):
                here = self.place(0, me.z * 512 + half * 256 + r * 32, 32)
                total = self.grad[here].astype(F32)
                for i in (3 - half, 4 + half):
                    total = total + self.stage[0][i][rows, :].astype(F32)
                self.grad[here] = total.astype(BF)
                if not self.both:
                    continue
                rows_x = pl.ds(pl.multiple_of(half * 256 + r * 32, 32), 32)
                total = self.stage[1][0][rows_x, :].astype(F32)
                for i in (1, 2):
                    total = total + self.stage[1][i][rows_x, :].astype(F32)
                self.part[rows_x, :] = total.astype(BF)
            return 0

        lax.fori_loop(0, 8, add_z, 0)
        self.over_x(lambda xlo, c: self.grad.at[self.place(0, me.z * 512 + xlo * 256 + c * 128, 128)],
                    self.left.at[me.x], 10)
        for k in (1, 3, 2) if self.both else ():
            z = ring(me.z, k)
            remote(self.part.at[rows_at(z * 128, 128)], self.right.at[k - 1], self.send.at[13 + k],
                   self.recv.at[13 + k], me.at(z=z)).start()

    def third(self, store):
        me = self.me
        for i in range(4):
            settle(self.left.at[i], self.recv.at[10 + i])
        for k in (1, 2, 3) if self.both else ():
            settle(self.right.at[k - 1], self.recv.at[13 + k])

        def add(i, _):
            rows = pl.ds(pl.multiple_of(i * 32, 32), 32)
            left = self.left[0, rows, :].astype(F32)
            for x in range(1, 4):
                left = left + self.left[x, rows, :].astype(F32)
            store(rows, 0, left)
            if self.both:
                right = self.part[pl.ds(pl.multiple_of(me.z * 128 + i * 32, 32), 32), :].astype(F32)
                for k in range(3):
                    right = right + self.right[k, rows, :].astype(F32)
                store(rows, self.widths[0], right)
            return 0

        lax.fori_loop(0, 4, add, 0)

    def finish(self):
        me = self.me
        for i in range(6):
            settle(self.inbox[0].at[i], self.send.at[i])
        self.over_x_sent(self.left.at[0], 10)
        if not self.both:
            return
        for k in (1, 2, 3):
            settle(self.right.at[k - 1], self.send.at[13 + k])
        for xlo in (0, 1):
            for c in (0, 1):
                @pl.when(jnp.logical_or(me.x != me.c * 2 + xlo, me.c != c))
                def _():
                    settle(self.inbox[1].at[0], self.send.at[6 + xlo * 2 + c])


def dot_rows(left, right):
    return lax.dot_general(left, right, (((0,), (0,)), ((), ())), preferred_element_type=F32)


def back_norm(values, gain, upstream):
    entries = values.shape[-1]
    inverse = inverse_of(values)
    scaled = upstream * gain
    folded = jnp.sum(scaled * values, axis=-1, keepdims=True)
    grad = inverse * scaled - values * (inverse * inverse * inverse) * folded / entries
    return grad, jnp.sum(upstream * values * inverse, axis=0, keepdims=True)


def layer_kernel(
    tokens, cot, attn_gain, mlp_gain, query_gain, key_gain, wo, wq, wk, wv, wg, wu, wd, cosine, sine,
    result, tokens_grad, attn_gain_grad, mlp_gain_grad, query_gain_grad, key_gain_grad,
    qkv_grad, out_grad, gate_grad, up_grad, down_grad, n_out,
    box_q0, box_q1, box_k0, box_k1, box_o0, box_o1, box_g0, box_g1, box_u0, box_u1, box_d0, box_d1,
    n, cota, a, b, a_shard, b_shard, d_shard, da, h, dg, du, qlin, klin, qrot, kv, o, mid, cos, sin, dqkv, d_o, acc, acc_out, acc_in,
    sib_out, held, arrive, held2, arrive2,
    part_q, left_q, right_q, part_k, left_k, right_k, part_o, left_o, right_o, part_g, left_g, right_g,
    part_u, left_u, right_u, part_d, left_d, right_d, gain8, gainx, gainz, gacc,
    load, n_send, n_recv, c_send, c_recv, n2_send, n2_recv, da_send, da_recv,
    a_send, a_recv, o_send, o_recv, b_send, b_recv, w_send, w_recv, r_send, r_recv, r1_send, r1_recv, r2_send, r2_recv, r3_send, r3_recv,
    q_send, q_recv, k_send, k_recv, g_send, g_recv, u_send, u_recv, d_send, d_recv, p_send, p_recv,
    stage_load, kv_sem, swap_sem, v_send, v_recv,
):
    me = Place()
    barrier, count = greet(me)
    loads = {}

    def fetch(name, src, dst):
        loads[name] = pltpu.make_async_copy(src, dst, load.at[len(loads)])
        loads[name].start()

    for name, src, dst, col in (("wq", wq, a_shard, 0), ("wk", wk, a_shard, 256), ("wv", wv, a_shard, 384),
                                ("wg", wg, b_shard, 0), ("wu", wu, b_shard, 768), ("wd", wd, d_shard, 0)):
        fetch(name, src, dst.at[:, pl.ds(col, src.shape[1])])
    fetch("cos", cosine.at[me.xhi], cos)
    fetch("sin", sine.at[me.xhi], sin)
    own = (me.c * 4 + me.y) * BLOCK

    def norm_one(i, _):
        rows = pl.ds(pl.multiple_of(i * 16, 16), 16)
        x = tokens[rows, :].astype(F32)
        n[pl.ds(pl.multiple_of(own + i * 16, 16), 16), :] = (x * inverse_of(x) * attn_gain[...]).astype(BF)
        return 0

    lax.fori_loop(0, 8, norm_one, 0)
    cota[rows_at(own, BLOCK), :] = cot[...]
    for name in ("wq", "wk", "wv", "wg", "wu", "wd"):
        loads[name].wait()
    pl.semaphore_wait(barrier, count)

    weights_a = GatherWeights(me, a_shard, a, 0, 384, 512, a_send, a_recv)
    weights_o = GatherWeights(me, wo, a, 512, 256, 256, o_send, o_recv)
    weights_b = GatherWeights(me, b_shard, b, 0, B_CUT, 1536, b_send, b_recv)
    weights_d = GatherWeights(me, d_shard, b, 1536, D_CUT, 768, w_send, w_recv)
    rows_n = GatherRows(me, n, n_send, n_recv)
    rows_c = GatherRows(me, cota, c_send, c_recv)
    rows_n2 = GatherRows(me, n, n2_send, n2_recv)
    rows_n.start()
    weights_a.first(0)
    weights_a.first(1)
    weights_o.first(0)
    weights_a.second_z()
    weights_a.second_x()
    rows_n.relay()
    weights_a.relay()
    weights_a.relay_x()
    weights_o.second_z()
    weights_d.first(0)
    weights_b.first(0)
    rows_n.own_blocks()
    rows_n.finish()
    rows_c.start()
    weights_a.arrived()
    weights_o.relay()
    weights_d.first(1)
    weights_b.first(1)
    n_save = pltpu.make_async_copy(n, n_out, load.at[8])
    n_save.start()
    loads["cos"].wait()
    loads["sin"].wait()

    def project(s):
        rows = rows_at(s * 512, 512)
        x = n[rows, :]
        k = dot(x, a[:, 256:512])
        klin[rows, :] = k[:, 0:128]
        u = k[:, 0:128]
        u = turn(u * inverse_of(u) * key_gain[...], cos[...], sin[...]).astype(BF)
        v = k[:, 128:256].astype(BF)
        for block in range(4):
            kv[0, s, block, 0] = u[block * 128:(block + 1) * 128]
            kv[1, s, block, 0] = v[block * 128:(block + 1) * 128]

    def project_q(s):
        rows = rows_at(s * 512, 512)
        q = dot(n[rows, :], a[:, 0:256])
        qlin[rows, :] = q
        for g in (0, 1):
            u = q[:, g * 128:(g + 1) * 128]
            u = turn(u * inverse_of(u) * query_gain[...], cos[...], sin[...]).astype(BF)
            for block in range(4):
                qrot[rows_at(s * 1024 + block * 256 + g * 128, 128), :] = u[block * 128:(block + 1) * 128]

    order = (1 - me.c, me.c)
    swaps = []
    for i, s in enumerate(order):
        project(s)
        swap = remote(kv.at[:, s, :, 0], kv.at[:, s, :, 1], kv_sem.at[i], kv_sem.at[2 + i], me.at(x=ring(me.x, 2)))
        swap.start()
        swaps.append(swap)
    for s in order:
        project_q(s)
    rows_c.relay()
    weights_d.second_z()
    weights_b.second_z()

    def attend(s):
        for block in range(4):
            size = (block + 1) * 256
            q = qrot[rows_at(s * 1024 + block * 256, 256), :]
            weights = jnp.exp2(dot_t(q, kv[0, s, 0:block + 1].reshape(size, 128)) * SCORE2)
            row = lax.rem(lax.broadcasted_iota(jnp.int32, (256, 256), 0), 128)
            col = lax.broadcasted_iota(jnp.int32, (256, 256), 1)
            weights = mask_last(weights, jnp.logical_or(col <= row, col >= 256 - 128 * me.xhi), 1)
            total = jnp.sum(weights, axis=-1, keepdims=True)
            got = dot(weights.astype(BF), kv[1, s, 0:block + 1].reshape(size, 128))
            got = (got / total).astype(BF)
            rows = rows_at(s * 512 + block * 128, 128)
            o[rows, 0:128] = got[0:128]
            o[rows, 128:256] = got[128:256]

    sums = ReduceRows(me, sib_out, held, arrive, r_send, r_recv)

    def branch(row, j):
        return dot_t(o[rows_at(row, 256), :], a[rows_at(j * 512, 512), 512:768])

    swaps[0].wait()
    attend(order[0])
    weights_o.arrived()
    n_save.wait()
    sums.other(branch)
    swaps[1].wait()
    attend(order[1])
    sums.mine(branch)
    weights_d.second_x()
    sums.relay()
    weights_b.second_x()
    rows_c.own_blocks()
    rows_c.finish()
    weights_d.relay()
    weights_d.relay_x()
    weights_b.relay()
    sums.wait()

    def norm_two(i, _):
        rows = pl.ds(pl.multiple_of(i * 16, 16), 16)
        x = tokens[rows, :].astype(F32) + sums.total(i * 16)
        mid[rows, :] = x
        n[pl.ds(pl.multiple_of(own + i * 16, 16), 16), :] = (x * inverse_of(x) * mlp_gain[...]).astype(BF)
        return 0

    lax.fori_loop(0, 8, norm_two, 0)
    rows_n2.start()
    sums.free()
    sums.finish()
    rows_n2.relay()
    weights_b.relay_x()
    weights_d.arrived()

    def hidden_back(i, _):
        rows = rows_at(i * 512, 512)
        for j in range(3):
            cols = slice(j * 256, j * 256 + 256)
            du[rows, cols] = dot(cota[rows, :], b[:, 1536 + j * 256:1792 + j * 256]).astype(BF)
        return 0

    lax.fori_loop(0, 2, hidden_back, 0)
    rows_n2.own_blocks()
    weights_b.arrived()

    def hidden(s):
        def step(j, _):
            rows = rows_at(s * 512, 512)
            cols = rows_at(j * 256, 256)
            gate = dot(n[rows, :], b[:, cols])
            up = dot(n[rows, :], b[:, rows_at(768 + j * 256, 256)])
            d_hidden = du[rows, cols].astype(F32)
            sg = jax.nn.sigmoid(gate)
            active = gate * sg
            h[rows, cols] = (active * up).astype(BF)
            dg[rows, cols] = (d_hidden * up * sg * (1.0 + gate * (1.0 - sg))).astype(BF)
            du[rows, cols] = (d_hidden * active).astype(BF)
            return 0

        lax.fori_loop(0, 3, step, 0)

    hidden(me.c)
    rows_n2.finish()
    hidden(1 - me.c)
    for weights in (weights_a, weights_o, weights_b, weights_d):
        weights.finish()
    sum_n2 = ReduceRows(me, sib_out, held, arrive, r1_send, r1_recv)
    sum_result = ReduceRows(me, sib_out, held2, arrive2, r2_send, r2_recv)
    sum_n = ReduceRows(me, sib_out, held, arrive, r3_send, r3_recv)

    def back_n2(row, j):
        rows, model = rows_at(row, 256), rows_at(j * 512, 512)
        return dot_t(dg[rows, :], b[model, 0:768]) + dot_t(du[rows, :], b[model, 768:1536])

    def down(row, j):
        return dot_t(h[rows_at(row, 256), :], b[rows_at(j * 512, 512), 1536:2304])

    sum_n2.other(back_n2)
    sum_n2.mine(back_n2)
    def stages(first, second):
        quarter = [(buf, r) for buf in (dg, du) for r in range(4)]
        return ([buf.at[pl.ds(r * 256, 256), pl.ds(0, first)] for buf, r in quarter[:6]],
                [buf.at[pl.ds(r * 512, 512), pl.ds(384, max(second, 128))] for buf in (dg, du) for r in (0, 1)])

    def reduction(grad, col, widths, boxes, sums, sems, fold=0):
        return ReduceWeights(me, grad, col, widths, boxes, stages(*widths), *sums, *sems, stage_load, fold)

    red_g = reduction(b, 0, WIDE, (box_g0, box_g1), (part_g, left_g, right_g), (g_send, g_recv))
    red_u = reduction(b, 768, WIDE, (box_u0, box_u1), (part_u, left_u, right_u), (u_send, u_recv))
    red_d = reduction(b, 1536, WIDE, (box_d0, box_d1), (part_d, left_d, right_d), (d_send, d_recv))
    red_o = reduction(a, 512, ONE_WAY, (box_o0, box_o1), (part_o, left_o, right_o), (p_send, p_recv))
    red_q = reduction(n, 0, NARROW, (box_q0, box_q1), (part_q, left_q, right_q), (q_send, q_recv), 256)
    red_k = reduction(h, 0, NARROW, (box_k0, box_k1), (part_k, left_k, right_k), (k_send, k_recv), 256)

    def weight_grad(red, left, right, unroll=False, cols=None):
        def step(i, _):
            rows = rows_at(i * 256, 256)
            value = dot_rows(left[:, rows], right[...])
            red.store(i, value)
            if cols is not None:
                terms = value * a[rows, cols].astype(F32)
                terms = terms[:, 0:128] + terms[:, 128:256]
                gacc[:, rows] += jnp.sum(terms.T, axis=0, keepdims=True)
            return 0

        lax.fori_loop(0, 8, step, 0, unroll=unroll)
        red.first()

    weight_grad(red_g, n, dg)
    sum_n2.relay()
    weight_grad(red_u, n, du)
    sum_n2.free()
    sum_result.other(down)
    sum_result.mine(down, send=False)
    sum_n2.wait()
    rows_da = GatherRows(me, da, da_send, da_recv)

    def back_two(i, total):
        rows = pl.ds(pl.multiple_of(i * 16, 16), 16)
        grad, gain = back_norm(mid[rows, :], mlp_gain[...], sum_n2.total(i * 16))
        grad = grad + cot[rows, :].astype(F32)
        tokens_grad[rows, :] = grad
        da[pl.ds(pl.multiple_of(own + i * 16, 16), 16), :] = grad.astype(BF)
        return total + gain

    mlp_part = lax.fori_loop(0, 8, back_two, jnp.zeros((1, WIDTH), F32))
    rows_da.start()
    slot = me.c * 4 + me.y

    def spread(value, col):
        for i in range(8):
            gainx[me.x, i:i + 1, col:col + 256] = value[:, i * 256:(i + 1) * 256]

    gainx[me.x] = jnp.zeros((8, 640), F32)
    spread(mlp_part, 256)
    gacc[...] = jnp.zeros_like(gacc)
    sum_n2.finish()
    red_g.relay()
    weight_grad(red_d, cota, h)
    n_load = pltpu.make_async_copy(n_out, cota, load.at[9])
    n_load.start()
    rows_da.relay()
    red_u.relay()
    red_g.second()
    key = lax.broadcasted_iota(jnp.int32, (256, 256), 0)
    query = lax.rem(lax.broadcasted_iota(jnp.int32, (256, 256), 1), 128)
    keep = jnp.logical_or(key <= query, key >= 256 - 128 * me.xhi)

    def weights_at(turn_, block):
        rows, strip = {3: (0, 0), 2: (0, 1), 0: (768, 1), 1: (512 * turn_, 4)}[block]
        strip += 0 if block == 1 else 2 * turn_
        return pl.ds(rows, (block + 1) * 256), pl.ds(512 + strip * 256, 256)

    for turn_, s in enumerate(order):
        for pair in ((3, 0), (2, 1)):
            ps = []
            for block in pair:
                q = qrot[rows_at(s * 1024 + block * 256, 256), :]
                k = kv[0, s, 0:block + 1].reshape((block + 1) * 256, 128)
                ps.append(mask_last(jnp.exp2(dot_t(k, q) * SCORE2), keep, 0))
            ps = [p * (1.0 / jnp.sum(p, axis=0, keepdims=True)) for p in ps]
            for block, p in zip(pair, ps):
                n[weights_at(turn_, block)] = p.astype(BF)

    rows_da.own_blocks()

    def back_o(s):
        rows = rows_at(s * 512, 512)
        d_o[rows, :] = dot(da[rows, :], a[:, 512:768]).astype(BF)

    back_o(me.c)
    rows_da.finish()
    back_o(1 - me.c)
    sum_result.send_all()

    swaps = []
    q_gain = jnp.zeros((1, HEAD), F32)
    for turn_ in (0, 1):
        s = 1 - me.c if turn_ == 0 else me.c
        flat = kv[0, s].reshape(1024, 128).T
        dqs = {}
        for pair in ((3, 0), (2, 1)):
            sizes = [(block + 1) * 256 for block in pair]
            qs = [qrot[rows_at(s * 1024 + block * 256, 256), :] for block in pair]
            gs = []
            for block in pair:
                rows = rows_at(s * 512 + block * 128, 128)
                gs.append(jnp.concatenate([d_o[rows, 0:128], d_o[rows, 128:256]], axis=0))
            vs = [kv[1, s, 0:block + 1].reshape(size, 128) for block, size in zip(pair, sizes)]
            ps = [n[weights_at(turn_, block)] for block in pair]
            dps = [dot_t(v, g) for v, g in zip(vs, gs)]
            dss = []
            for p, dp in zip(ps, dps):
                p = p.astype(F32)
                dss.append((p * (dp - jnp.sum(dp * p, axis=0, keepdims=True))).astype(BF))
            for block, size, ds in zip(pair, sizes, dss):
                dqs[block] = (dot(flat[:, :size], ds) * SCORE).T
            dks = [dot(ds, q) * SCORE for ds, q in zip(dss, qs)]
            dvs = [dot(p, g) for p, g in zip(ps, gs)]
            for block, dk, dv in zip(pair, dks, dvs):
                for i, value in enumerate((dk, dv)):
                    value = value.reshape(block + 1, 2, 128, 128)
                    if block == 3:
                        acc[i, s] = value
                    else:
                        acc[i, s, 0:block + 1] += value
        rows = rows_at(s * 512, 512)
        for head in (0, 1):
            dq = jnp.concatenate([dqs[block][head * 128:(head + 1) * 128] for block in range(4)], axis=0)
            up = turn(dq, cos[...], -sin[...])
            grad, gain = back_norm(qlin[rows, head * 128:(head + 1) * 128], query_gain[...], up)
            dqkv[rows, head * 128:(head + 1) * 128] = grad.astype(BF)
            q_gain = q_gain + gain
        for i in (0, 1):
            acc_out[turn_, i] = acc[i, s, :, 1].astype(BF)
        swap = remote(acc_out.at[turn_], acc_in.at[turn_], swap_sem.at[turn_], swap_sem.at[2 + turn_],
                      me.at(x=ring(me.x, 2)))
        swap.start()
        swaps.append(swap)
    red_d.relay()
    weight_grad(red_o, da, o, True)
    n_load.wait()
    weight_grad(red_q, cota, dqkv.at[:, pl.ds(0, 256)], True, slice(0, 256))
    sum_result.relay()
    red_u.second()

    k_gain = jnp.zeros((1, HEAD), F32)

    def back_n(row, j):
        rows, model = rows_at(row, 256), rows_at(j * 512, 512)
        return dot_t(dqkv[rows, 0:256], a[model, 0:256]) + dot_t(dqkv[rows, 256:512], a[model, 256:512])

    for turn_ in (0, 1):
        s = 1 - me.c if turn_ == 0 else me.c
        rows = rows_at(s * 512, 512)
        swaps[turn_].wait()
        dk = (acc[0, s, :, 0] + acc_in[turn_, 0].astype(F32)).reshape(512, 128)
        dv = (acc[1, s, :, 0] + acc_in[turn_, 1].astype(F32)).reshape(512, 128)
        grad, gain = back_norm(klin[rows, :], key_gain[...], turn(dk, cos[...], -sin[...]))
        k_gain = k_gain + gain
        dqkv[rows, 256:384] = grad.astype(BF)
        dqkv[rows, 384:512] = dv.astype(BF)
        if turn_ == 0:
            sum_result.free()
            sum_n.other(back_n)
        else:
            sum_n.mine(back_n)
    weight_grad(red_k, cota, dqkv.at[:, pl.ds(256, 256)], True, slice(256, 512))
    spread(gacc[...] / attn_gain[...], 0)
    gainx[me.x, 0:1, 512:640] = q_gain
    gainx[me.x, 1:2, 512:640] = k_gain
    for k in (1, 2, 3):
        remote(gainx.at[me.x], gainx.at[me.x], v_send.at[6 + k], v_recv.at[8 + me.x], me.at(x=ring(me.x, k))).start()
    red_o.relay()
    red_q.relay()
    red_k.relay()
    sum_n.relay()
    red_d.second()
    for i in range(4):
        @pl.when(me.x != i)
        def _():
            settle(gainx.at[i], v_recv.at[8 + i])
    gainz[me.z] = gainx[0] + gainx[1] + gainx[2] + gainx[3]
    for k in (1, 2, 3):
        remote(gainz.at[me.z], gainz.at[me.z], v_send.at[9 + k], v_recv.at[12 + me.z], me.at(z=ring(me.z, k))).start()
    red_o.second()
    red_q.second()
    red_k.second()
    for i in range(4):
        @pl.when(me.z != i)
        def _():
            settle(gainz.at[i], v_recv.at[12 + i])
    gain8[slot] = gainz[0] + gainz[1] + gainz[2] + gainz[3]
    peers = [(me.y, 1 - me.c)] + [(ring(me.y, k), c) for k in (1, 2, 3) for c in (0, 1)]
    for i, (y, c) in enumerate(peers):
        remote(gain8.at[slot], gain8.at[slot], v_send.at[i], v_recv.at[slot], me.at(y=y, c=c)).start()

    def put(ref, first=0):
        def store(rows, col, value):
            ref[rows, first + col:first + col + value.shape[1]] = value
        return store

    sum_result.wait()

    def finish_result(i, _):
        rows = pl.ds(pl.multiple_of(i * 16, 16), 16)
        result[rows, :] = (mid[rows, :] + sum_result.total(i * 16)).astype(BF)
        return 0

    lax.fori_loop(0, 8, finish_result, 0)
    red_g.third(put(gate_grad))
    sum_n.wait()

    def back_one(i, _):
        rows = pl.ds(pl.multiple_of(i * 16, 16), 16)
        grad, _ = back_norm(tokens[rows, :].astype(F32), attn_gain[...], sum_n.total(i * 16))
        tokens_grad[rows, :] += grad
        return 0

    lax.fori_loop(0, 8, back_one, 0)
    red_d.third(put(down_grad))
    red_u.third(put(up_grad))
    red_o.third(put(out_grad))
    red_q.third(put(qkv_grad))
    for i in range(8):
        @pl.when(slot != i)
        def _():
            settle(gain8.at[i], v_recv.at[i])
    total = gain8[0]
    for i in range(1, 8):
        total = total + gain8[i]
    for i in range(8):
        cols = slice(i * 256, i * 256 + 256)
        attn_gain_grad[:, cols] = total[i:i + 1, 0:256]
        mlp_gain_grad[:, cols] = total[i:i + 1, 256:512]
    query_gain_grad[...] = total[0:1, 512:640]
    key_gain_grad[...] = total[1:2, 512:640]
    red_k.third(put(qkv_grad, 256))
    for i in range(13):
        settle(gain8.at[0], v_send.at[i])
    sum_result.finish()
    sum_n.free()
    sum_n.finish()
    for red in (red_g, red_u, red_d, red_o, red_q, red_k):
        red.finish()


def layer(tokens, cot, gains, weights, cos, sin):
    wq, wk, wv, wo, wg, wu, wd = weights
    args = (tokens, cot) + gains + (wo, wq, wk, wv, wg, wu, wd, cos, sin)
    vmem = pl.BlockSpec(memory_space=pltpu.VMEM)
    hbm = pl.BlockSpec(memory_space=pl.ANY)
    outs = [((BLOCK, WIDTH), BF), ((BLOCK, WIDTH), F32), ((1, WIDTH), F32), ((1, WIDTH), F32)]
    outs += [((1, HEAD), F32), ((1, HEAD), F32), ((BLOCK, 512), F32), ((BLOCK, 256), F32)]
    outs += [((BLOCK, 768), F32)] * 3
    widths = [(w[0], max(w[1], 128)) for w in (NARROW, NARROW, ONE_WAY, WIDE, WIDE, WIDE)]
    boxes = [((ROWS, WIDTH), BF)]
    boxes += [box for w in widths for box in (((6, 256, w[0]), BF), ((4, 512, w[1]), BF))]
    scratch = [
        ((ROWS, WIDTH), BF), ((ROWS, WIDTH), BF), ((WIDTH, A_COLS), BF), ((WIDTH, B_COLS), BF),
        ((BLOCK, 512), BF), ((BLOCK, 1536), BF), ((BLOCK, 768), BF), ((ROWS, WIDTH), BF),
        ((ROWS, 768), BF), ((ROWS, 768), BF), ((ROWS, 768), BF), ((ROWS, 256), F32), ((ROWS, 128), F32),
        ((2 * ROWS, 128), BF), (KV_SHAPE, BF), ((ROWS, 256), BF), ((BLOCK, WIDTH), F32),
        ((512, 128), F32), ((512, 128), F32), ((ROWS, 512), BF), ((ROWS, 256), BF), (KV_SHAPE, F32),
        ((2, 2, 4, 128, 128), BF), ((2, 2, 4, 128, 128), BF),
        ((512, WIDTH), BF), ((512, WIDTH), BF), ((6, 64, WIDTH), BF), ((512, WIDTH), BF), ((6, 64, WIDTH), BF),
    ]
    for w in widths:
        scratch += [((512, w[1]), BF), ((4, BLOCK, w[0]), BF), ((3, BLOCK, w[1]), BF)]
    scratch += [((8, 8, 640), F32), ((4, 8, 640), F32), ((4, 8, 640), F32), ((1, WIDTH), F32)]
    scratch = [pltpu.VMEM(s, d) for s, d in scratch]
    dma = pltpu.SemaphoreType.DMA
    scratch += [dma((10,))] + [dma((GatherRows.sems,))] * 8 + [dma((GatherWeights.sems,))] * 8 + [dma((8,))] * 8
    scratch += [dma((ReduceWeights.sems,))] * 12 + [dma((10,)), dma((4,)), dma((4,)), dma((13,)), dma((16,))]
    got = pl.pallas_call(
        layer_kernel,
        out_shape=[jax.ShapeDtypeStruct(s, d) for s, d in outs + boxes],
        in_specs=[vmem] * 7 + [hbm] * 8,
        out_specs=[vmem] * len(outs) + [hbm] * len(boxes),
        scratch_shapes=scratch,
        compiler_params=pltpu.CompilerParams(
            collective_id=1, has_side_effects=True, vmem_limit_bytes=VMEM_BYTES),
        name="layer_part",
    )(*args)
    return got[:len(outs)]


def finish_kernel(*refs):
    parts, outs, held, sem, out_sem = refs[:11], refs[11:24], refs[24:37], refs[37], refs[38]
    qkv = parts[6]
    sources = parts[:6] + tuple(qkv.at[:, pl.ds(*cols)] for cols in ((0, 256), (256, 128), (384, 128))) + parts[7:]
    ins = [pltpu.make_async_copy(src, dst, sem.at[i]) for i, (src, dst) in enumerate(zip(sources, held))]
    backs = [pltpu.make_async_copy(src, dst, out_sem.at[i]) for i, (src, dst) in enumerate(zip(held, outs))]
    for copy in ins:
        copy.start()
    for copy, back in zip(ins, backs):
        copy.wait()
        back.start()
    for back in backs:
        back.wait()


def finish(parts):
    shapes = [((BLOCK, WIDTH), BF), ((BLOCK, WIDTH), F32), ((1, WIDTH), F32), ((1, WIDTH), F32), ((1, HEAD), F32)]
    shapes += [((1, HEAD), F32), ((BLOCK, 256), F32), ((BLOCK, 128), F32), ((BLOCK, 128), F32), ((BLOCK, 256), F32)]
    shapes += [((BLOCK, 768), F32)] * 3
    return pl.pallas_call(
        finish_kernel,
        out_shape=[jax.ShapeDtypeStruct(s, d) for s, d in shapes],
        in_specs=[pl.BlockSpec(memory_space=pl.ANY)] * len(parts),
        out_specs=[pl.BlockSpec(memory_space=pl.ANY)] * len(shapes),
        scratch_shapes=[pltpu.VMEM(s, d) for s, d in shapes] + [pltpu.SemaphoreType.DMA((13,))] * 2,
        compiler_params=pltpu.CompilerParams(vmem_limit_bytes=VMEM_BYTES),
        name="finish_part",
    )(*parts)


def local(tokens, cotangent, attn_gain, mlp_gain, query_gain, key_gain, *weights):
    cos, sin = rope_tables()
    gains = (attn_gain[None], mlp_gain[None], query_gain[None], key_gain[None])
    outs = finish(layer(tokens, cotangent, gains, weights, cos, sin))
    return tuple(outs[:2]) + tuple(g[0] for g in outs[2:6]) + tuple(outs[6:])


def solution(mesh):
    rows, plane = P(("dp", "tensor"), None), P("dp", "tensor")
    return jax.shard_map(
        local,
        mesh=mesh,
        in_specs=(rows, rows, P(), P(), P(), P()) + (plane,) * 7,
        out_specs=(rows, rows, P(), P(), P(), P()) + (plane,) * 7,
        check_vma=False,
    )
```

```python
import functools

import numpy as np
import jax
import jax.numpy as jnp
from jax import lax
from jax.experimental import pallas as pl
from jax.experimental.pallas import tpu as pltpu
from jax.sharding import PartitionSpec as P

EPS = 1e-06
ROPE_BASE = 1000000.0
MESH = pl.DeviceIdType.MESH
BF = jnp.bfloat16
F32 = jnp.float32
HEAD = 128
WIDTH = 2048
BLOCK = 128
ROWS = 1024
A_COLS = 768
B_COLS = 2304
B_CUT = 896
D_CUT = 384
SCORE = HEAD ** -0.5
KV_SHAPE = (2, 2, 4, 2, 128, 128)
SCORE2 = HEAD ** -0.5 * 1.4426950408889634
VMEM_BYTES = 63 * 2**20


class Place:
    def __init__(self):
        dp = lax.axis_index("dp")
        tensor = lax.axis_index("tensor")
        self.dp = dp
        self.xlo = lax.div(dp, 8)
        self.z = lax.rem(lax.div(dp, 2), 4)
        self.c = lax.rem(dp, 2)
        self.y = lax.div(tensor, 2)
        self.xhi = lax.rem(tensor, 2)
        self.x = self.xhi * 2 + self.xlo

    def at(self, x=None, y=None, z=None, c=None):
        x = self.x if x is None else x
        y = self.y if y is None else y
        z = self.z if z is None else z
        c = self.c if c is None else c
        return (lax.rem(x, 2) * 8 + z * 2 + c, y * 2 + lax.div(x, 2))

    def sibling(self):
        return self.at(c=1 - self.c)


def ring(v, k):
    return lax.rem(v + k, 4)


def remote(src, dst, send_sem, recv_sem, target):
    return pltpu.make_async_remote_copy(
        src_ref=src, dst_ref=dst, send_sem=send_sem, recv_sem=recv_sem,
        device_id=target, device_id_type=MESH,
    )


def settle(ref, sem):
    pltpu.make_async_copy(ref, ref, sem).wait()


def rows_at(start, size):
    return pl.ds(pl.multiple_of(start, 128), size)


def greet(me):
    barrier = pltpu.get_barrier_semaphore()
    others = [me.sibling()]
    for k in (1, 2, 3):
        others.append(me.at(y=ring(me.y, k)))
        others.append(me.at(y=ring(me.y, k), c=1 - me.c))
        for c in (0, 1):
            others.append(me.at(x=ring(me.x, k), c=c))
            others.append(me.at(z=ring(me.z, k), c=c))
    for other in others:
        pl.semaphore_signal(barrier, inc=1, device_id=other, device_id_type=MESH)
    return barrier, len(others)


class GatherRows:
    sems = 13

    def __init__(self, me, buf, send, recv):
        self.me, self.buf, self.send, self.recv = me, buf, send, recv

    def piece(self, c, y, half):
        return self.buf.at[pl.ds(pl.multiple_of((c * 4 + y) * BLOCK + half * 64, 64), 64)]

    def go(self, y, half, i, target):
        ref = self.piece(self.me.c, y, half)
        remote(ref, ref, self.send.at[i], self.recv.at[i], target).start()

    def start(self):
        me = self.me
        up, down = me.at(y=ring(me.y, 1)), me.at(y=ring(me.y, 3))
        self.go(me.y, 0, 0, up)
        self.go(me.y, 1, 2, down)
        own = self.buf.at[rows_at((me.c * 4 + me.y) * BLOCK, BLOCK)]
        remote(own, own, self.send.at[6], self.recv.at[6], me.sibling()).start()

    def heard(self, i, k, half):
        me = self.me
        y = ring(me.y, 4 - k)
        settle(self.piece(me.c, y, half), self.recv.at[i])
        self.go(y, half, 7 + i, me.sibling())
        return y

    def relay(self):
        me = self.me
        up, down = me.at(y=ring(me.y, 1)), me.at(y=ring(me.y, 3))
        half = self.piece(me.c, me.y, 0)
        settle(half, self.send.at[0])
        self.go(me.y, 1, 1, up)
        settle(half, self.send.at[2])
        self.go(me.y, 0, 3, down)
        y = self.heard(0, 1, 0)
        self.go(y, 0, 4, up)
        y = self.heard(2, 3, 1)
        self.go(y, 1, 5, down)

    def own_blocks(self):
        self.heard(1, 1, 1)
        self.heard(3, 3, 0)
        self.heard(4, 2, 0)
        self.heard(5, 2, 1)

    def finish(self):
        me = self.me
        half = self.piece(me.c, me.y, 0)
        own = self.buf.at[rows_at((me.c * 4 + me.y) * BLOCK, BLOCK)]
        for i in (1, 3, 4, 5, 6, 7, 8, 9, 10, 11, 12):
            settle(own if i == 6 else half, self.send.at[i])
        for i in range(6, 13):
            settle(own if i == 6 else half, self.recv.at[i])


class ReduceRows:
    def __init__(self, me, sib_out, held, arrive, send, recv):
        self.me = me
        self.sib_out, self.held, self.arrive = sib_out, held, arrive
        self.send, self.recv = send, recv
        first = 1 - lax.div(me.y, 2)
        self.halves = (first, 1 - first)

    def other(self, tile):
        me = self.me
        for p, half in enumerate(self.halves):
            rows = rows_at(half * 256, 256)

            def step(j, _):
                cols = rows_at(j * 512, 512)
                self.sib_out[rows, cols] = tile((1 - me.c) * 512 + half * 256, j).astype(BF)
                return 0

            lax.fori_loop(0, 4, step, 0, unroll=True)
            remote(self.sib_out.at[rows], self.held.at[rows], self.send.at[6 + p], self.recv.at[6 + p],
                   me.sibling()).start()

    def piece(self, k, half):
        return pl.ds(pl.multiple_of(ring(self.me.y, k) * BLOCK + half * 64, 64), 64)

    def go(self, i, k, half, step):
        remote(self.held.at[self.piece(k, half)], self.arrive.at[i], self.send.at[i], self.recv.at[i],
               self.me.at(y=ring(self.me.y, step))).start()

    def mine(self, tile, send=True):
        me = self.me
        for p, half in enumerate(self.halves):
            rows = rows_at(half * 256, 256)
            settle(self.held.at[rows], self.recv.at[6 + p])

            def step(j, _):
                cols = rows_at(j * 512, 512)
                total = tile(me.c * 512 + half * 256, j) + self.held[rows, cols].astype(F32)
                self.held[rows, cols] = total.astype(BF)
                return 0

            lax.fori_loop(0, 4, step, 0, unroll=True)
            if not send:
                continue
            even = lax.rem(me.y, 2) == 0
            if p == 0:
                self.go(0, 2, 0, 1)
                self.go(1, 2, 1, 3)
            pl.when(even if p == 0 else jnp.logical_not(even))(lambda: self.go(3, 3, 0, 3))
            pl.when(jnp.logical_not(even) if p == 0 else even)(lambda: self.go(2, 1, 1, 1))

    def send_all(self):
        self.go(0, 2, 0, 1)
        self.go(1, 2, 1, 3)
        self.go(2, 1, 1, 1)
        self.go(3, 3, 0, 3)

    def relay(self):
        for i, k, half, step in ((0, 1, 0, 1), (1, 3, 1, 3)):
            settle(self.arrive.at[i], self.recv.at[i])
            rows = self.piece(k, half)
            self.held[rows, :] = (self.held[rows, :].astype(F32) + self.arrive[i].astype(F32)).astype(BF)
            self.go(4 + i, k, half, step)

    def wait(self):
        for i in range(2, 6):
            settle(self.arrive.at[i], self.recv.at[i])

    def total(self, r):
        half = lax.div(r, 64)
        rows = pl.ds(pl.multiple_of(r - half * 64, 16), 16)
        total = self.held[pl.ds(pl.multiple_of(self.me.y * BLOCK + r, 16), 16), :].astype(F32)
        return total + self.arrive[3 - half, rows, :].astype(F32) + self.arrive[4 + half, rows, :].astype(F32)

    def free(self):
        for p in (0, 1):
            settle(self.sib_out.at[rows_at(0, 256)], self.send.at[6 + p])

    def finish(self):
        for i in range(6):
            settle(self.arrive.at[i], self.send.at[i])


class GatherWeights:
    sems = 23

    def __init__(self, me, shard, full, col, cut, width, send, recv):
        self.me, self.shard, self.full = me, shard, full
        self.cols = (pl.ds(col, cut), pl.ds(col + cut, width - cut))
        self.from_cols = (pl.ds(0, cut), pl.ds(cut, width - cut))
        self.send, self.recv = send, recv
        self.ways = (0, 1) if cut < width else (0,)

    def slot(self, way, dp):
        return self.full.at[rows_at(dp * BLOCK, BLOCK), self.cols[way]]

    def first(self, way):
        me = self.me
        home = me.xhi
        src = self.shard.at[:, self.from_cols[way]]
        dst = self.slot(way, me.dp)
        inbox = self.recv.at[(me.xlo * 2 + me.c) if way == 0 else (10 + me.z * 2 + me.c)]
        base = 0 if way == 0 else 10
        for k in (1, 3, 2):
            target = me.at(x=ring(me.x, k), c=home) if way == 0 else me.at(z=ring(me.z, k), c=home)
            remote(src, dst, self.send.at[base + k], inbox, target).start()

        @pl.when(me.c == home)
        def _():
            pltpu.make_async_copy(src, dst, inbox).start()

        @pl.when(me.c != home)
        def _():
            remote(src, dst, self.send.at[base], inbox, me.sibling()).start()

    def second_z(self):
        me = self.me
        for xlo in (0, 1):
            for c in (0, 1):
                settle(self.slot(0, xlo * 8 + me.z * 2 + c), self.recv.at[xlo * 2 + c])
        self.go(0, me.z, 4, 1)
        self.go(1, me.z, 6, 3)
        self.go(1, me.z, 5, 1)
        self.go(0, me.z, 7, 3)

    def go(self, xlo, z, i, step):
        ref = self.pair(xlo, z)
        remote(ref, ref, self.send.at[i], self.recv.at[i], self.me.at(z=ring(self.me.z, step))).start()

    def relay(self):
        me = self.me
        for i, xlo, step in ((4, 0, 1), (6, 1, 3)):
            z = ring(me.z, 4 - step)
            settle(self.pair(xlo, z), self.recv.at[i])
            self.go(xlo, z, 8 + xlo, step)

    def second_x(self):
        me = self.me
        if 1 not in self.ways:
            return

        @pl.when(me.c == me.xhi)
        def _():
            for z in range(4):
                for c in (0, 1):
                    settle(self.slot(1, me.xlo * 8 + z * 2 + c), self.recv.at[10 + z * 2 + c])
            for i, (part, step) in enumerate(((0, 1), (1, 3), (1, 1), (0, 3))):
                self.go_x(me.xlo, part, 18 + i, ring(me.x, step))

    def go_x(self, xlo, part, i, x):
        ref = self.quarter(xlo, part)
        remote(ref, ref, self.send.at[i], self.recv.at[18 + xlo * 2 + part], self.me.at(x=x)).start()

    def near_x(self):
        me = self.me
        below = lax.div(ring(me.x, 3), 2)
        up = 1 - (below + me.c - 2 * below * me.c)
        return up, lax.rem(ring(me.x, 1 + 2 * up), 2), 1 - up

    def relay_x(self):
        if 1 not in self.ways:
            return
        up, xlo, part = self.near_x()
        settle(self.quarter(0, 0), self.recv.at[18 + xlo * 2 + part])
        self.go_x(xlo, part, 22, ring(self.me.x, 3 - 2 * up))

    def pair(self, xlo, z):
        return self.full.at[rows_at(xlo * 1024 + z * 256, 256), self.cols[0]]

    def quarter(self, xlo, part):
        return self.full.at[rows_at(xlo * 1024 + part * 512, 512), self.cols[1]]

    def arrived(self):
        me = self.me
        for i in (5, 7, 8, 9):
            settle(self.pair(0, me.z), self.recv.at[i])
        if 1 not in self.ways:
            return
        _, near, near_part = self.near_x()
        for xlo in (0, 1):
            for part in (0, 1):
                here = jnp.logical_and(me.c == me.xhi, me.xlo == xlo)
                done = jnp.logical_and(near == xlo, near_part == part)

                @pl.when(jnp.logical_not(jnp.logical_or(here, done)))
                def _():
                    settle(self.quarter(0, 0), self.recv.at[18 + xlo * 2 + part])

    def finish(self):
        me = self.me
        for way in self.ways:
            src = self.shard.at[:, self.from_cols[way]]
            base = 0 if way == 0 else 10
            for k in (1, 2, 3):
                settle(src, self.send.at[base + k])

            @pl.when(me.c != me.xhi)
            def _():
                settle(src, self.send.at[base])
        for i in range(4, 10):
            settle(self.pair(0, me.z), self.send.at[i])

        if 1 not in self.ways:
            return

        @pl.when(me.c == me.xhi)
        def _():
            for i in range(18, 22):
                settle(self.quarter(0, 0), self.send.at[i])

        settle(self.quarter(0, 0), self.send.at[22])


def dot(left, right):
    return jnp.dot(left, right, preferred_element_type=F32)


def dot_t(left, right):
    return lax.dot_general(left, right, (((1,), (1,)), ((), ())), preferred_element_type=F32)


def inverse_of(values):
    return lax.rsqrt(jnp.mean(values * values, axis=-1, keepdims=True) + EPS)


def turn(values, cosine, sine):
    return values * cosine + pltpu.roll(values, 64, 1) * sine


def mask_last(values, keep, axis):
    size = values.shape[axis]
    last = jnp.where(keep, lax.slice_in_dim(values, size - 256, size, axis=axis), 0.0)
    if size == 256:
        return last
    return jnp.concatenate([lax.slice_in_dim(values, 0, size - 256, axis=axis), last], axis=axis)


def rope_tables():
    frequency = ROPE_BASE ** (-2.0 * np.arange(64, dtype=np.float64) / HEAD)
    angle = np.arange(1024, dtype=np.float64)[:, None] * frequency[None, :]
    cos = np.concatenate([np.cos(angle), np.cos(angle)], axis=1).astype(np.float32)
    sin = np.concatenate([-np.sin(angle), np.sin(angle)], axis=1).astype(np.float32)
    pick = lambda t: t.reshape(4, 2, 128, 128).transpose(1, 0, 2, 3).reshape(2, 512, 128)
    return pick(cos), pick(sin)


WIDE, NARROW, ONE_WAY = (384, 384), (128, 128), (256, 0)


class ReduceWeights:
    sems = 17

    def __init__(self, me, grad, first_col, widths, inbox, stage, part, left, right, send, recv, load, fold=0):
        self.me, self.grad, self.widths, self.fold = me, grad, widths, fold
        self.first_cols = (first_col, first_col + widths[0])
        self.both = widths[1] > 0
        self.inbox, self.stage, self.part, self.left, self.right = inbox, stage, part, left, right
        self.send, self.recv, self.load = send, recv, load

    def place(self, way, start, size):
        col = self.first_cols[way]
        if self.fold:
            high = lax.div(start, 1024)
            start = start - high * 1024
            col = pl.multiple_of(col + high * self.fold, 128)
        return pl.ds(pl.multiple_of(start, 32), size), pl.ds(col, self.widths[way])

    def store(self, i, value):
        xlo, z = lax.div(i, 4), lax.rem(i, 4)
        value = value.astype(BF)
        self.grad[self.place(0, z * 512 + xlo * 256, 256)] = value[:, :self.widths[0]]
        for c in (0, 1) if self.both else ():
            self.grad[self.place(1, (xlo * 2 + c) * 512 + z * 128, 128)] = value[
                c * 128:(c + 1) * 128, self.widths[0]:]

    def piece(self, k, half):
        return self.grad.at[self.place(0, ring(self.me.z, k) * 512 + half * 256, 256)]

    def go(self, i, k, half, step):
        remote(self.piece(k, half), self.inbox[0].at[i], self.send.at[i], self.recv.at[i],
               self.me.at(z=ring(self.me.z, step))).start()

    def over_x(self, sources, dst, base):
        me = self.me
        for xlo in (0, 1):
            for c in (0, 1):
                src = sources(xlo, c)
                x = me.c * 2 + xlo
                self_too = jnp.logical_and(me.x == x, me.c == c)

                @pl.when(self_too)
                def _():
                    pltpu.make_async_copy(src, dst, self.recv.at[base + me.x]).start()

                @pl.when(jnp.logical_not(self_too))
                def _():
                    remote(src, dst, self.send.at[base + xlo * 2 + c], self.recv.at[base + me.x],
                           me.at(x=x, c=c)).start()

    def over_x_sent(self, ref, base):
        me = self.me
        for xlo in (0, 1):
            for c in (0, 1):
                @pl.when(jnp.logical_or(me.x != me.c * 2 + xlo, me.c != c))
                def _():
                    settle(ref, self.send.at[base + xlo * 2 + c])

    def first(self):
        self.go(0, 2, 0, 1)
        self.go(1, 2, 1, 3)
        self.go(2, 1, 1, 1)
        self.go(3, 3, 0, 3)
        if not self.both:
            return
        me = self.me
        for xlo in (0, 1):
            x = me.c * 2 + xlo
            away = ring(me.x + 4 - x, 0)
            for c in (0, 1):
                there = me.at(x=x, c=c)

                @pl.when(jnp.logical_and(away == 0, me.c == c))
                def _():
                    pltpu.make_async_copy(self.share(xlo, c), self.inbox[1].at[0], self.recv.at[6]).start()

                @pl.when(jnp.logical_and(away == 0, me.c != c))
                def _():
                    self.go_x(xlo, c, 0, there)

                @pl.when(away == 2)
                def _():
                    self.go_x(xlo, c, 3, me.at(x=ring(me.x, 3 if c == 0 else 1)))

                @pl.when(away == (3 if c == 0 else 1))
                def _():
                    self.go_x(xlo, c, 2 if c == 0 else 1, there)

    def share(self, xlo, c):
        return self.grad.at[self.place(1, jnp.int32(0) + (xlo * 2 + c) * 512, 512)]

    def go_x(self, xlo, c, slot, target):
        remote(self.share(xlo, c), self.inbox[1].at[slot], self.send.at[6 + xlo * 2 + c], self.recv.at[6 + slot],
               target).start()

    def relay_x(self):
        me = self.me
        away = ring(me.x + 4 - me.c * 2, 0)
        xlo = 1 - lax.rem(away, 2)
        c = lax.div(ring(away + 4 - xlo, 0), 2)
        self.fetched(9)

        def add(r, _):
            here = self.place(1, (xlo * 2 + c) * 512 + r * 64, 64)
            more = self.stage[1][3][pl.ds(pl.multiple_of(r * 64, 64), 64), :]
            self.grad[here] = (self.grad[here].astype(F32) + more.astype(F32)).astype(BF)
            return 0

        lax.fori_loop(0, 8, add, 0)
        self.go_x(xlo, c, 1 + c, me.at(x=me.c * 2 + xlo, c=c))

    def fetch(self, i):
        way, slot = (0, i) if i < 6 else (1, i - 6)
        settle(self.inbox[way].at[slot], self.recv.at[i])
        pltpu.make_async_copy(self.inbox[way].at[slot], self.stage[way][slot], self.load.at[i]).start()

    def fetched(self, i):
        way, slot = (0, i) if i < 6 else (1, i - 6)
        settle(self.stage[way][slot], self.load.at[i])

    def relay(self):
        for i in (0, 1, 9) if self.both else (0, 1):
            self.fetch(i)
        for i, k, half, step in ((0, 1, 0, 1), (1, 3, 1, 3)):
            self.fetched(i)
            base = ring(self.me.z, k) * 512 + half * 256

            def add(r, _):
                here = self.place(0, base + r * 64, 64)
                more = self.stage[0][i][pl.ds(pl.multiple_of(r * 64, 64), 64), :]
                self.grad[here] = (self.grad[here].astype(F32) + more.astype(F32)).astype(BF)
                return 0

            lax.fori_loop(0, 4, add, 0)
            self.go(4 + i, k, half, step)
        if self.both:
            self.relay_x()

    def second(self):
        me = self.me
        arrivals = range(2, 9 if self.both else 6)
        for i in arrivals:
            self.fetch(i)
        for i in arrivals:
            self.fetched(i)

        def add_z(r, _):
            rows = pl.ds(pl.multiple_of(r * 32, 32), 32)
            for half in (0, 1):
                here = self.place(0, me.z * 512 + half * 256 + r * 32, 32)
                total = self.grad[here].astype(F32)
                for i in (3 - half, 4 + half):
                    total = total + self.stage[0][i][rows, :].astype(F32)
                self.grad[here] = total.astype(BF)
                if not self.both:
                    continue
                rows_x = pl.ds(pl.multiple_of(half * 256 + r * 32, 32), 32)
                total = self.stage[1][0][rows_x, :].astype(F32)
                for i in (1, 2):
                    total = total + self.stage[1][i][rows_x, :].astype(F32)
                self.part[rows_x, :] = total.astype(BF)
            return 0

        lax.fori_loop(0, 8, add_z, 0)
        self.over_x(lambda xlo, c: self.grad.at[self.place(0, me.z * 512 + xlo * 256 + c * 128, 128)],
                    self.left.at[me.x], 10)
        for k in (1, 3, 2) if self.both else ():
            z = ring(me.z, k)
            remote(self.part.at[rows_at(z * 128, 128)], self.right.at[k - 1], self.send.at[13 + k],
                   self.recv.at[13 + k], me.at(z=z)).start()

    def third(self, store):
        me = self.me
        for i in range(4):
            settle(self.left.at[i], self.recv.at[10 + i])
        for k in (1, 2, 3) if self.both else ():
            settle(self.right.at[k - 1], self.recv.at[13 + k])

        def add(i, _):
            rows = pl.ds(pl.multiple_of(i * 32, 32), 32)
            left = self.left[0, rows, :].astype(F32)
            for x in range(1, 4):
                left = left + self.left[x, rows, :].astype(F32)
            store(rows, 0, left)
            if self.both:
                right = self.part[pl.ds(pl.multiple_of(me.z * 128 + i * 32, 32), 32), :].astype(F32)
                for k in range(3):
                    right = right + self.right[k, rows, :].astype(F32)
                store(rows, self.widths[0], right)
            return 0

        lax.fori_loop(0, 4, add, 0)

    def finish(self):
        me = self.me
        for i in range(6):
            settle(self.inbox[0].at[i], self.send.at[i])
        self.over_x_sent(self.left.at[0], 10)
        if not self.both:
            return
        for k in (1, 2, 3):
            settle(self.right.at[k - 1], self.send.at[13 + k])
        for xlo in (0, 1):
            for c in (0, 1):
                @pl.when(jnp.logical_or(me.x != me.c * 2 + xlo, me.c != c))
                def _():
                    settle(self.inbox[1].at[0], self.send.at[6 + xlo * 2 + c])


def dot_rows(left, right):
    return lax.dot_general(left, right, (((0,), (0,)), ((), ())), preferred_element_type=F32)


def back_norm(values, gain, upstream):
    entries = values.shape[-1]
    inverse = inverse_of(values)
    scaled = upstream * gain
    folded = jnp.sum(scaled * values, axis=-1, keepdims=True)
    grad = inverse * scaled - values * (inverse * inverse * inverse) * folded / entries
    return grad, jnp.sum(upstream * values * inverse, axis=0, keepdims=True)


def layer_kernel(
    tokens, cot, attn_gain, mlp_gain, query_gain, key_gain, wo, wq, wk, wv, wg, wu, wd, cosine, sine,
    result, tokens_grad, attn_gain_grad, mlp_gain_grad, query_gain_grad, key_gain_grad,
    qkv_grad, out_grad, gate_grad, up_grad, down_grad, n_out,
    box_q0, box_q1, box_k0, box_k1, box_o0, box_o1, box_g0, box_g1, box_u0, box_u1, box_d0, box_d1,
    n, cota, a, b, a_shard, b_shard, d_shard, da, h, dg, du, qlin, klin, qrot, kv, o, mid, cos, sin, dqkv, d_o, acc, acc_out, acc_in,
    sib_out, held, arrive, held2, arrive2,
    part_q, left_q, right_q, part_k, left_k, right_k, part_o, left_o, right_o, part_g, left_g, right_g,
    part_u, left_u, right_u, part_d, left_d, right_d, gain8, gainx, gainz, gacc,
    load, n_send, n_recv, c_send, c_recv, n2_send, n2_recv, da_send, da_recv,
    a_send, a_recv, o_send, o_recv, b_send, b_recv, w_send, w_recv, r_send, r_recv, r1_send, r1_recv, r2_send, r2_recv, r3_send, r3_recv,
    q_send, q_recv, k_send, k_recv, g_send, g_recv, u_send, u_recv, d_send, d_recv, p_send, p_recv,
    stage_load, kv_sem, swap_sem, v_send, v_recv,
):
    me = Place()
    barrier, count = greet(me)
    loads = {}

    def fetch(name, src, dst):
        loads[name] = pltpu.make_async_copy(src, dst, load.at[len(loads)])
        loads[name].start()

    for name, src, dst, col in (("wq", wq, a_shard, 0), ("wk", wk, a_shard, 256), ("wv", wv, a_shard, 384),
                                ("wg", wg, b_shard, 0), ("wu", wu, b_shard, 768), ("wd", wd, d_shard, 0)):
        fetch(name, src, dst.at[:, pl.ds(col, src.shape[1])])
    fetch("cos", cosine.at[me.xhi], cos)
    fetch("sin", sine.at[me.xhi], sin)
    own = (me.c * 4 + me.y) * BLOCK

    def norm_one(i, _):
        rows = pl.ds(pl.multiple_of(i * 16, 16), 16)
        x = tokens[rows, :].astype(F32)
        n[pl.ds(pl.multiple_of(own + i * 16, 16), 16), :] = (x * inverse_of(x) * attn_gain[...]).astype(BF)
        return 0

    lax.fori_loop(0, 8, norm_one, 0)
    cota[rows_at(own, BLOCK), :] = cot[...]
    for name in ("wq", "wk", "wv", "wg", "wu", "wd"):
        loads[name].wait()
    pl.semaphore_wait(barrier, count)

    weights_a = GatherWeights(me, a_shard, a, 0, 384, 512, a_send, a_recv)
    weights_o = GatherWeights(me, wo, a, 512, 256, 256, o_send, o_recv)
    weights_b = GatherWeights(me, b_shard, b, 0, B_CUT, 1536, b_send, b_recv)
    weights_d = GatherWeights(me, d_shard, b, 1536, D_CUT, 768, w_send, w_recv)
    rows_n = GatherRows(me, n, n_send, n_recv)
    rows_c = GatherRows(me, cota, c_send, c_recv)
    rows_n2 = GatherRows(me, n, n2_send, n2_recv)
    rows_n.start()
    weights_a.first(0)
    weights_a.first(1)
    weights_o.first(0)
    weights_a.second_z()
    weights_a.second_x()
    rows_n.relay()
    weights_a.relay()
    weights_a.relay_x()
    weights_o.second_z()
    weights_d.first(0)
    weights_b.first(0)
    rows_n.own_blocks()
    rows_n.finish()
    rows_c.start()
    weights_a.arrived()
    weights_o.relay()
    weights_d.first(1)
    weights_b.first(1)
    n_save = pltpu.make_async_copy(n, n_out, load.at[8])
    n_save.start()
    loads["cos"].wait()
    loads["sin"].wait()

    def project(s):
        rows = rows_at(s * 512, 512)
        x = n[rows, :]
        k = dot(x, a[:, 256:512])
        klin[rows, :] = k[:, 0:128]
        u = k[:, 0:128]
        u = turn(u * inverse_of(u) * key_gain[...], cos[...], sin[...]).astype(BF)
        v = k[:, 128:256].astype(BF)
        for block in range(4):
            kv[0, s, block, 0] = u[block * 128:(block + 1) * 128]
            kv[1, s, block, 0] = v[block * 128:(block + 1) * 128]

    def project_q(s):
        rows = rows_at(s * 512, 512)
        q = dot(n[rows, :], a[:, 0:256])
        qlin[rows, :] = q
        for g in (0, 1):
            u = q[:, g * 128:(g + 1) * 128]
            u = turn(u * inverse_of(u) * query_gain[...], cos[...], sin[...]).astype(BF)
            for block in range(4):
                qrot[rows_at(s * 1024 + block * 256 + g * 128, 128), :] = u[block * 128:(block + 1) * 128]

    order = (1 - me.c, me.c)
    swaps = []
    for i, s in enumerate(order):
        project(s)
        swap = remote(kv.at[:, s, :, 0], kv.at[:, s, :, 1], kv_sem.at[i], kv_sem.at[2 + i], me.at(x=ring(me.x, 2)))
        swap.start()
        swaps.append(swap)
    for s in order:
        project_q(s)
    rows_c.relay()
    weights_d.second_z()
    weights_b.second_z()

    def attend(s):
        for block in range(4):
            size = (block + 1) * 256
            q = qrot[rows_at(s * 1024 + block * 256, 256), :]
            weights = jnp.exp2(dot_t(q, kv[0, s, 0:block + 1].reshape(size, 128)) * SCORE2)
            row = lax.rem(lax.broadcasted_iota(jnp.int32, (256, 256), 0), 128)
            col = lax.broadcasted_iota(jnp.int32, (256, 256), 1)
            weights = mask_last(weights, jnp.logical_or(col <= row, col >= 256 - 128 * me.xhi), 1)
            total = jnp.sum(weights, axis=-1, keepdims=True)
            got = dot(weights.astype(BF), kv[1, s, 0:block + 1].reshape(size, 128))
            got = (got / total).astype(BF)
            rows = rows_at(s * 512 + block * 128, 128)
            o[rows, 0:128] = got[0:128]
            o[rows, 128:256] = got[128:256]

    sums = ReduceRows(me, sib_out, held, arrive, r_send, r_recv)

    def branch(row, j):
        return dot_t(o[rows_at(row, 256), :], a[rows_at(j * 512, 512), 512:768])

    swaps[0].wait()
    attend(order[0])
    weights_o.arrived()
    n_save.wait()
    sums.other(branch)
    swaps[1].wait()
    attend(order[1])
    sums.mine(branch)
    weights_d.second_x()
    sums.relay()
    weights_b.second_x()
    rows_c.own_blocks()
    rows_c.finish()
    weights_d.relay()
    weights_d.relay_x()
    weights_b.relay()
    sums.wait()

    def norm_two(i, _):
        rows = pl.ds(pl.multiple_of(i * 16, 16), 16)
        x = tokens[rows, :].astype(F32) + sums.total(i * 16)
        mid[rows, :] = x
        n[pl.ds(pl.multiple_of(own + i * 16, 16), 16), :] = (x * inverse_of(x) * mlp_gain[...]).astype(BF)
        return 0

    lax.fori_loop(0, 8, norm_two, 0)
    rows_n2.start()
    sums.free()
    sums.finish()
    rows_n2.relay()
    weights_b.relay_x()
    weights_d.arrived()

    def hidden_back(i, _):
        rows = rows_at(i * 512, 512)
        for j in range(3):
            cols = slice(j * 256, j * 256 + 256)
            du[rows, cols] = dot(cota[rows, :], b[:, 1536 + j * 256:1792 + j * 256]).astype(BF)
        return 0

    lax.fori_loop(0, 2, hidden_back, 0)
    rows_n2.own_blocks()
    weights_b.arrived()

    def hidden(s):
        def step(j, _):
            rows = rows_at(s * 512, 512)
            cols = rows_at(j * 256, 256)
            gate = dot(n[rows, :], b[:, cols])
            up = dot(n[rows, :], b[:, rows_at(768 + j * 256, 256)])
            d_hidden = du[rows, cols].astype(F32)
            sg = jax.nn.sigmoid(gate)
            active = gate * sg
            h[rows, cols] = (active * up).astype(BF)
            dg[rows, cols] = (d_hidden * up * sg * (1.0 + gate * (1.0 - sg))).astype(BF)
            du[rows, cols] = (d_hidden * active).astype(BF)
            return 0

        lax.fori_loop(0, 3, step, 0)

    hidden(me.c)
    rows_n2.finish()
    hidden(1 - me.c)
    for weights in (weights_a, weights_o, weights_b, weights_d):
        weights.finish()
    sum_n2 = ReduceRows(me, sib_out, held, arrive, r1_send, r1_recv)
    sum_result = ReduceRows(me, sib_out, held2, arrive2, r2_send, r2_recv)
    sum_n = ReduceRows(me, sib_out, held, arrive, r3_send, r3_recv)

    def back_n2(row, j):
        rows, model = rows_at(row, 256), rows_at(j * 512, 512)
        return dot_t(dg[rows, :], b[model, 0:768]) + dot_t(du[rows, :], b[model, 768:1536])

    def down(row, j):
        return dot_t(h[rows_at(row, 256), :], b[rows_at(j * 512, 512), 1536:2304])

    sum_n2.other(back_n2)
    sum_n2.mine(back_n2)
    def stages(first, second):
        quarter = [(buf, r) for buf in (dg, du) for r in range(4)]
        return ([buf.at[pl.ds(r * 256, 256), pl.ds(0, first)] for buf, r in quarter[:6]],
                [buf.at[pl.ds(r * 512, 512), pl.ds(384, max(second, 128))] for buf in (dg, du) for r in (0, 1)])

    def reduction(grad, col, widths, boxes, sums, sems, fold=0):
        return ReduceWeights(me, grad, col, widths, boxes, stages(*widths), *sums, *sems, stage_load, fold)

    red_g = reduction(b, 0, WIDE, (box_g0, box_g1), (part_g, left_g, right_g), (g_send, g_recv))
    red_u = reduction(b, 768, WIDE, (box_u0, box_u1), (part_u, left_u, right_u), (u_send, u_recv))
    red_d = reduction(b, 1536, WIDE, (box_d0, box_d1), (part_d, left_d, right_d), (d_send, d_recv))
    red_o = reduction(a, 512, ONE_WAY, (box_o0, box_o1), (part_o, left_o, right_o), (p_send, p_recv))
    red_q = reduction(n, 0, NARROW, (box_q0, box_q1), (part_q, left_q, right_q), (q_send, q_recv), 256)
    red_k = reduction(h, 0, NARROW, (box_k0, box_k1), (part_k, left_k, right_k), (k_send, k_recv), 256)

    def weight_grad(red, left, right, unroll=False, cols=None):
        def step(i, _):
            rows = rows_at(i * 256, 256)
            value = dot_rows(left[:, rows], right[...])
            red.store(i, value)
            if cols is not None:
                terms = value * a[rows, cols].astype(F32)
                terms = terms[:, 0:128] + terms[:, 128:256]
                gacc[:, rows] += jnp.sum(terms.T, axis=0, keepdims=True)
            return 0

        lax.fori_loop(0, 8, step, 0, unroll=unroll)
        red.first()

    weight_grad(red_g, n, dg)
    sum_n2.relay()
    weight_grad(red_u, n, du)
    sum_n2.free()
    sum_result.other(down)
    sum_result.mine(down, send=False)
    sum_n2.wait()
    rows_da = GatherRows(me, da, da_send, da_recv)

    def back_two(i, total):
        rows = pl.ds(pl.multiple_of(i * 16, 16), 16)
        grad, gain = back_norm(mid[rows, :], mlp_gain[...], sum_n2.total(i * 16))
        grad = grad + cot[rows, :].astype(F32)
        tokens_grad[rows, :] = grad
        da[pl.ds(pl.multiple_of(own + i * 16, 16), 16), :] = grad.astype(BF)
        return total + gain

    mlp_part = lax.fori_loop(0, 8, back_two, jnp.zeros((1, WIDTH), F32))
    rows_da.start()
    slot = me.c * 4 + me.y

    def spread(value, col):
        for i in range(8):
            gainx[me.x, i:i + 1, col:col + 256] = value[:, i * 256:(i + 1) * 256]

    gainx[me.x] = jnp.zeros((8, 640), F32)
    spread(mlp_part, 256)
    gacc[...] = jnp.zeros_like(gacc)
    sum_n2.finish()
    red_g.relay()
    weight_grad(red_d, cota, h)
    n_load = pltpu.make_async_copy(n_out, cota, load.at[9])
    n_load.start()
    rows_da.relay()
    red_u.relay()
    red_g.second()
    key = lax.broadcasted_iota(jnp.int32, (256, 256), 0)
    query = lax.rem(lax.broadcasted_iota(jnp.int32, (256, 256), 1), 128)
    keep = jnp.logical_or(key <= query, key >= 256 - 128 * me.xhi)

    def weights_at(turn_, block):
        rows, strip = {3: (0, 0), 2: (0, 1), 0: (768, 1), 1: (512 * turn_, 4)}[block]
        strip += 0 if block == 1 else 2 * turn_
        return pl.ds(rows, (block + 1) * 256), pl.ds(512 + strip * 256, 256)

    for turn_, s in enumerate(order):
        for pair in ((3, 0), (2, 1)):
            ps = []
            for block in pair:
                q = qrot[rows_at(s * 1024 + block * 256, 256), :]
                k = kv[0, s, 0:block + 1].reshape((block + 1) * 256, 128)
                ps.append(mask_last(jnp.exp2(dot_t(k, q) * SCORE2), keep, 0))
            ps = [p * (1.0 / jnp.sum(p, axis=0, keepdims=True)) for p in ps]
            for block, p in zip(pair, ps):
                n[weights_at(turn_, block)] = p.astype(BF)

    rows_da.own_blocks()

    def back_o(s):
        rows = rows_at(s * 512, 512)
        d_o[rows, :] = dot(da[rows, :], a[:, 512:768]).astype(BF)

    back_o(me.c)
    rows_da.finish()
    back_o(1 - me.c)
    sum_result.send_all()

    swaps = []
    q_gain = jnp.zeros((1, HEAD), F32)
    for turn_ in (0, 1):
        s = 1 - me.c if turn_ == 0 else me.c
        flat = kv[0, s].reshape(1024, 128).T
        dqs = {}
        for pair in ((3, 0), (2, 1)):
            sizes = [(block + 1) * 256 for block in pair]
            qs = [qrot[rows_at(s * 1024 + block * 256, 256), :] for block in pair]
            gs = []
            for block in pair:
                rows = rows_at(s * 512 + block * 128, 128)
                gs.append(jnp.concatenate([d_o[rows, 0:128], d_o[rows, 128:256]], axis=0))
            vs = [kv[1, s, 0:block + 1].reshape(size, 128) for block, size in zip(pair, sizes)]
            ps = [n[weights_at(turn_, block)] for block in pair]
            dps = [dot_t(v, g) for v, g in zip(vs, gs)]
            dss = []
            for p, dp in zip(ps, dps):
                p = p.astype(F32)
                dss.append((p * (dp - jnp.sum(dp * p, axis=0, keepdims=True))).astype(BF))
            for block, size, ds in zip(pair, sizes, dss):
                dqs[block] = (dot(flat[:, :size], ds) * SCORE).T
            dks = [dot(ds, q) * SCORE for ds, q in zip(dss, qs)]
            dvs = [dot(p, g) for p, g in zip(ps, gs)]
            for block, dk, dv in zip(pair, dks, dvs):
                for i, value in enumerate((dk, dv)):
                    value = value.reshape(block + 1, 2, 128, 128)
                    if block == 3:
                        acc[i, s] = value
                    else:
                        acc[i, s, 0:block + 1] += value
        rows = rows_at(s * 512, 512)
        for head in (0, 1):
            dq = jnp.concatenate([dqs[block][head * 128:(head + 1) * 128] for block in range(4)], axis=0)
            up = turn(dq, cos[...], -sin[...])
            grad, gain = back_norm(qlin[rows, head * 128:(head + 1) * 128], query_gain[...], up)
            dqkv[rows, head * 128:(head + 1) * 128] = grad.astype(BF)
            q_gain = q_gain + gain
        for i in (0, 1):
            acc_out[turn_, i] = acc[i, s, :, 1].astype(BF)
        swap = remote(acc_out.at[turn_], acc_in.at[turn_], swap_sem.at[turn_], swap_sem.at[2 + turn_],
                      me.at(x=ring(me.x, 2)))
        swap.start()
        swaps.append(swap)
    red_d.relay()
    weight_grad(red_o, da, o, True)
    n_load.wait()
    weight_grad(red_q, cota, dqkv.at[:, pl.ds(0, 256)], True, slice(0, 256))
    sum_result.relay()
    red_u.second()

    k_gain = jnp.zeros((1, HEAD), F32)

    def back_n(row, j):
        rows, model = rows_at(row, 256), rows_at(j * 512, 512)
        return dot_t(dqkv[rows, 0:256], a[model, 0:256]) + dot_t(dqkv[rows, 256:512], a[model, 256:512])

    for turn_ in (0, 1):
        s = 1 - me.c if turn_ == 0 else me.c
        rows = rows_at(s * 512, 512)
        swaps[turn_].wait()
        dk = (acc[0, s, :, 0] + acc_in[turn_, 0].astype(F32)).reshape(512, 128)
        dv = (acc[1, s, :, 0] + acc_in[turn_, 1].astype(F32)).reshape(512, 128)
        grad, gain = back_norm(klin[rows, :], key_gain[...], turn(dk, cos[...], -sin[...]))
        k_gain = k_gain + gain
        dqkv[rows, 256:384] = grad.astype(BF)
        dqkv[rows, 384:512] = dv.astype(BF)
        if turn_ == 0:
            sum_result.free()
            sum_n.other(back_n)
    weight_grad(red_k, cota, dqkv.at[:, pl.ds(256, 256)], True, slice(256, 512))
    spread(gacc[...] / attn_gain[...], 0)
    gainx[me.x, 0:1, 512:640] = q_gain
    gainx[me.x, 1:2, 512:640] = k_gain
    for k in (1, 2, 3):
        remote(gainx.at[me.x], gainx.at[me.x], v_send.at[6 + k], v_recv.at[8 + me.x], me.at(x=ring(me.x, k))).start()
    sum_n.mine(back_n)
    red_o.relay()
    red_q.relay()
    red_d.second()
    sum_n.relay()
    red_k.relay()
    for i in range(4):
        @pl.when(me.x != i)
        def _():
            settle(gainx.at[i], v_recv.at[8 + i])
    gainz[me.z] = gainx[0] + gainx[1] + gainx[2] + gainx[3]
    for k in (1, 2, 3):
        remote(gainz.at[me.z], gainz.at[me.z], v_send.at[9 + k], v_recv.at[12 + me.z], me.at(z=ring(me.z, k))).start()
    red_o.second()
    red_q.second()
    red_k.second()
    for i in range(4):
        @pl.when(me.z != i)
        def _():
            settle(gainz.at[i], v_recv.at[12 + i])
    gain8[slot] = gainz[0] + gainz[1] + gainz[2] + gainz[3]
    peers = [(me.y, 1 - me.c)] + [(ring(me.y, k), c) for k in (1, 2, 3) for c in (0, 1)]
    for i, (y, c) in enumerate(peers):
        remote(gain8.at[slot], gain8.at[slot], v_send.at[i], v_recv.at[slot], me.at(y=y, c=c)).start()

    def put(ref, first=0):
        def store(rows, col, value):
            ref[rows, first + col:first + col + value.shape[1]] = value
        return store

    sum_result.wait()

    def finish_result(i, _):
        rows = pl.ds(pl.multiple_of(i * 16, 16), 16)
        result[rows, :] = (mid[rows, :] + sum_result.total(i * 16)).astype(BF)
        return 0

    lax.fori_loop(0, 8, finish_result, 0)
    red_g.third(put(gate_grad))
    sum_n.wait()

    def back_one(i, _):
        rows = pl.ds(pl.multiple_of(i * 16, 16), 16)
        grad, _ = back_norm(tokens[rows, :].astype(F32), attn_gain[...], sum_n.total(i * 16))
        tokens_grad[rows, :] += grad
        return 0

    lax.fori_loop(0, 8, back_one, 0)
    red_d.third(put(down_grad))
    red_u.third(put(up_grad))
    red_o.third(put(out_grad))
    red_q.third(put(qkv_grad))
    for i in range(8):
        @pl.when(slot != i)
        def _():
            settle(gain8.at[i], v_recv.at[i])
    total = gain8[0]
    for i in range(1, 8):
        total = total + gain8[i]
    for i in range(8):
        cols = slice(i * 256, i * 256 + 256)
        attn_gain_grad[:, cols] = total[i:i + 1, 0:256]
        mlp_gain_grad[:, cols] = total[i:i + 1, 256:512]
    query_gain_grad[...] = total[0:1, 512:640]
    key_gain_grad[...] = total[1:2, 512:640]
    red_k.third(put(qkv_grad, 256))
    for i in range(13):
        settle(gain8.at[0], v_send.at[i])
    sum_result.finish()
    sum_n.free()
    sum_n.finish()
    for red in (red_g, red_u, red_d, red_o, red_q, red_k):
        red.finish()


def layer(tokens, cot, gains, weights, cos, sin):
    wq, wk, wv, wo, wg, wu, wd = weights
    args = (tokens, cot) + gains + (wo, wq, wk, wv, wg, wu, wd, cos, sin)
    vmem = pl.BlockSpec(memory_space=pltpu.VMEM)
    hbm = pl.BlockSpec(memory_space=pl.ANY)
    outs = [((BLOCK, WIDTH), BF), ((BLOCK, WIDTH), F32), ((1, WIDTH), F32), ((1, WIDTH), F32)]
    outs += [((1, HEAD), F32), ((1, HEAD), F32), ((BLOCK, 512), F32), ((BLOCK, 256), F32)]
    outs += [((BLOCK, 768), F32)] * 3
    widths = [(w[0], max(w[1], 128)) for w in (NARROW, NARROW, ONE_WAY, WIDE, WIDE, WIDE)]
    boxes = [((ROWS, WIDTH), BF)]
    boxes += [box for w in widths for box in (((6, 256, w[0]), BF), ((4, 512, w[1]), BF))]
    scratch = [
        ((ROWS, WIDTH), BF), ((ROWS, WIDTH), BF), ((WIDTH, A_COLS), BF), ((WIDTH, B_COLS), BF),
        ((BLOCK, 512), BF), ((BLOCK, 1536), BF), ((BLOCK, 768), BF), ((ROWS, WIDTH), BF),
        ((ROWS, 768), BF), ((ROWS, 768), BF), ((ROWS, 768), BF), ((ROWS, 256), F32), ((ROWS, 128), F32),
        ((2 * ROWS, 128), BF), (KV_SHAPE, BF), ((ROWS, 256), BF), ((BLOCK, WIDTH), F32),
        ((512, 128), F32), ((512, 128), F32), ((ROWS, 512), BF), ((ROWS, 256), BF), (KV_SHAPE, F32),
        ((2, 2, 4, 128, 128), BF), ((2, 2, 4, 128, 128), BF),
        ((512, WIDTH), BF), ((512, WIDTH), BF), ((6, 64, WIDTH), BF), ((512, WIDTH), BF), ((6, 64, WIDTH), BF),
    ]
    for w in widths:
        scratch += [((512, w[1]), BF), ((4, BLOCK, w[0]), BF), ((3, BLOCK, w[1]), BF)]
    scratch += [((8, 8, 640), F32), ((4, 8, 640), F32), ((4, 8, 640), F32), ((1, WIDTH), F32)]
    scratch = [pltpu.VMEM(s, d) for s, d in scratch]
    dma = pltpu.SemaphoreType.DMA
    scratch += [dma((10,))] + [dma((GatherRows.sems,))] * 8 + [dma((GatherWeights.sems,))] * 8 + [dma((8,))] * 8
    scratch += [dma((ReduceWeights.sems,))] * 12 + [dma((10,)), dma((4,)), dma((4,)), dma((13,)), dma((16,))]
    got = pl.pallas_call(
        layer_kernel,
        out_shape=[jax.ShapeDtypeStruct(s, d) for s, d in outs + boxes],
        in_specs=[vmem] * 7 + [hbm] * 8,
        out_specs=[vmem] * len(outs) + [hbm] * len(boxes),
        scratch_shapes=scratch,
        compiler_params=pltpu.CompilerParams(
            collective_id=1, has_side_effects=True, vmem_limit_bytes=VMEM_BYTES),
        name="layer_part",
    )(*args)
    return got[:len(outs)]


def finish_kernel(*refs):
    parts, outs, held, sem, out_sem = refs[:11], refs[11:24], refs[24:37], refs[37], refs[38]
    qkv = parts[6]
    sources = parts[:6] + tuple(qkv.at[:, pl.ds(*cols)] for cols in ((0, 256), (256, 128), (384, 128))) + parts[7:]
    ins = [pltpu.make_async_copy(src, dst, sem.at[i]) for i, (src, dst) in enumerate(zip(sources, held))]
    backs = [pltpu.make_async_copy(src, dst, out_sem.at[i]) for i, (src, dst) in enumerate(zip(held, outs))]
    for copy in ins:
        copy.start()
    for copy, back in zip(ins, backs):
        copy.wait()
        back.start()
    for back in backs:
        back.wait()


def finish(parts):
    shapes = [((BLOCK, WIDTH), BF), ((BLOCK, WIDTH), F32), ((1, WIDTH), F32), ((1, WIDTH), F32), ((1, HEAD), F32)]
    shapes += [((1, HEAD), F32), ((BLOCK, 256), F32), ((BLOCK, 128), F32), ((BLOCK, 128), F32), ((BLOCK, 256), F32)]
    shapes += [((BLOCK, 768), F32)] * 3
    return pl.pallas_call(
        finish_kernel,
        out_shape=[jax.ShapeDtypeStruct(s, d) for s, d in shapes],
        in_specs=[pl.BlockSpec(memory_space=pl.ANY)] * len(parts),
        out_specs=[pl.BlockSpec(memory_space=pl.ANY)] * len(shapes),
        scratch_shapes=[pltpu.VMEM(s, d) for s, d in shapes] + [pltpu.SemaphoreType.DMA((13,))] * 2,
        compiler_params=pltpu.CompilerParams(vmem_limit_bytes=VMEM_BYTES),
        name="finish_part",
    )(*parts)


def local(tokens, cotangent, attn_gain, mlp_gain, query_gain, key_gain, *weights):
    cos, sin = rope_tables()
    gains = (attn_gain[None], mlp_gain[None], query_gain[None], key_gain[None])
    outs = finish(layer(tokens, cotangent, gains, weights, cos, sin))
    return tuple(outs[:2]) + tuple(g[0] for g in outs[2:6]) + tuple(outs[6:])


def solution(mesh):
    rows, plane = P(("dp", "tensor"), None), P("dp", "tensor")
    return jax.shard_map(
        local,
        mesh=mesh,
        in_specs=(rows, rows, P(), P(), P(), P()) + (plane,) * 7,
        out_specs=(rows, rows, P(), P(), P(), P()) + (plane,) * 7,
        check_vma=False,
    )
```
